32 devices in a mesh: clip: 8 (over z, x), tm: 4 (over y, core).
Axes of the slice: x: 2, y: 2, z: 4, core: 2. Of those that a mesh axis runs over, the one named last changes fastest.
Arguments:
- mel_frames: bfloat16 [16, 2048, 80], P('clip', 'tm'), may hold values from -6 to 6
- lengths: int32 [16], P('clip'), may hold values from 512 to 2048, as said below
- conv1_weight: bfloat16 [3, 80, 768], P(None, None, 'tm'), may hold values from -0.375 to 0.375
- conv1_bias: bfloat16 [768], P('tm'), may hold values from -1.75 to 1.75
- conv2_weight: bfloat16 [3, 768, 768], P(None, None, 'tm'), may hold values from -0.125 to 0.125
- conv2_bias: bfloat16 [768], P('tm'), may hold values from -1.75 to 1.75
- ln1_gain: bfloat16 [768], P('tm'), may hold values from 0.5 to 1.5
- ln1_bias: bfloat16 [768], P('tm'), may hold values from -1.75 to 1.75
- qkv_weight: bfloat16 [768, 2304], P(None, 'tm'), may hold values from -0.21875 to 0.21875
- q_bias: bfloat16 [768], P('tm'), may hold values from -1.75 to 1.75
- v_bias: bfloat16 [768], P('tm'), may hold values from -0.125 to 0.125
- out_weight: bfloat16 [768, 768], P(None, 'tm'), may hold values from -3.5 to 3.5
- out_bias: bfloat16 [768], P('tm'), may hold values from -1.75 to 1.75
- ln2_gain: bfloat16 [768], P('tm'), may hold values from 0.5 to 1.5
- ln2_bias: bfloat16 [768], P('tm'), may hold values from -1.75 to 1.75
- fc1_weight: bfloat16 [768, 3072], P(None, 'tm'), may hold values from -0.21875 to 0.21875
- fc1_bias: bfloat16 [3072], P('tm'), may hold values from -1.75 to 1.75
- fc2_weight: bfloat16 [3072, 768], P(None, 'tm'), may hold values from -0.109375 to 0.109375
- fc2_bias: bfloat16 [768], P('tm'), may hold values from -1.75 to 1.75
- cotangent: bfloat16 [16, 1024, 768], P('clip', 'tm'), may hold values from -6 to 6
Outputs:
- out_states: bfloat16 [16, 1024, 768], P('clip', 'tm')
- mel_grad: bfloat16 [16, 2048, 80], P('clip', 'tm')
- conv1_weight_grad: float32 [3, 80, 768], P(None, None, 'tm')
- conv1_bias_grad: float32 [768], P('tm')
- conv2_weight_grad: float32 [3, 768, 768], P(None, None, 'tm')
- conv2_bias_grad: float32 [768], P('tm')
- ln1_gain_grad: float32 [768], P('tm')
- ln1_bias_grad: float32 [768], P('tm')
- qkv_weight_grad: float32 [768, 2304], P(None, 'tm')
- q_bias_grad: float32 [768], P('tm')
- v_bias_grad: float32 [768], P('tm')
- out_weight_grad: float32 [768, 768], P(None, 'tm')
- out_bias_grad: float32 [768], P('tm')
- ln2_gain_grad: float32 [768], P('tm')
- ln2_bias_grad: float32 [768], P('tm')
- fc1_weight_grad: float32 [768, 3072], P(None, 'tm')
- fc1_bias_grad: float32 [3072], P('tm')
- fc2_weight_grad: float32 [3072, 768], P(None, 'tm')
- fc2_bias_grad: float32 [768], P('tm')
The draws below stay inside these ranges and needn't reach their ends.
Inputs may be any that keep to these rules, and one draw needn't show every extreme that they name: `lengths`: in each aligned block of 2 clips (the clips of one index of clip) one clip has all 2048 frames valid; the others vary.
All inputs are finite; a program needn't handle non-finite values.
Results may differ from the reference program's by a relative error of at most 0.018.
Values may be sent and summed in bfloat16 or wider, within the bound.
A program may use at most 192 MiB of HBM per device.

```python
import math
import jax
import jax.numpy as jnp
from jax import lax

D = 768
HEADS = 12
HEAD_DIM = 64
FF = 3072
MELS = 80
CLIP_DEV = 2
STATES = 1024
FRAMES = 2048
CLIPS = 16


def draw_lengths(key, part):
    key = jax.random.fold_in(key, 3)
    base_key, pick_key = jax.random.split(key)
    drawn = jax.random.randint(base_key, (CLIPS,), FRAMES // 4, FRAMES + 1)
    chosen = jax.random.randint(pick_key, (CLIPS // CLIP_DEV,), 0, CLIP_DEV)
    slot_index = jnp.arange(CLIPS) % CLIP_DEV
    full_clip = slot_index == jnp.repeat(chosen, CLIP_DEV, total_repeat_length=CLIPS)
    return jnp.where(full_clip, FRAMES, drawn).astype(jnp.int32)


def level_of(rng, dims, shards, smallest, high):
    level, own = 1.0, jax.random.fold_in(rng, 6)
    for position, parts in shards:
        draws = jnp.exp(jax.random.uniform(jax.random.fold_in(own, position), (parts,), jnp.float32, smallest / len(shards), high / len(shards)))
        level = level * jnp.repeat(draws, dims[position] // parts).reshape([-1 if axis == position else 1 for axis in range(len(dims))])
    return level


def noise(own_key, shape, scale, limit, cuts=(), kind=jnp.bfloat16):
    array = jax.random.normal(own_key, shape, jnp.float32) * scale
    if len(cuts) > 0:
        array = level_of(own_key, shape, cuts, -0.22, 0.18) * array
    return jnp.clip(array, min=-limit, max=limit).astype(kind)


def setup_inputs(seed: int = 0) -> dict:
    splits = jax.random.split(jax.random.key(seed), 21)
    mel_frames = noise(splits[0], (CLIPS, FRAMES, MELS), 1.0, 6.0, ((0, 8), (1, 4)))
    lengths = draw_lengths(jax.random.fold_in(splits[20], 71), 0)
    conv1_weight = noise(splits[2], (3, MELS, D), (3 * MELS) ** -0.5, 0.375, ((2, 4),))
    conv1_bias = noise(splits[3], (D,), 0.3, 1.75, ((0, 4),))
    conv2_weight = noise(splits[4], (3, D, D), (3 * D) ** -0.5, 0.125, ((2, 4),))
    conv2_bias = noise(splits[5], (D,), 0.3, 1.75, ((0, 4),))
    ln1_gain = jnp.clip(1.0 + 0.1 * jax.random.normal(splits[6], (D,), jnp.float32), 0.5, 1.5).astype(jnp.bfloat16)
    ln1_bias = noise(splits[7], (D,), 0.3, 1.75, ((0, 4),))
    qkv_weight = noise(splits[8], (D, 3 * D), D ** -0.5, 0.21875, ((1, 4),))
    q_bias = noise(splits[9], (D,), 0.3, 1.75, ((0, 4),))
    v_bias = noise(splits[10], (D,), 0.02, 0.125, ((0, 4),))
    out_weight = noise(splits[11], (D, D), (max(D // 256, 1)) ** -0.5, 3.5, ((1, 4),))
    out_bias = noise(splits[12], (D,), 0.3, 1.75, ((0, 4),))
    ln2_gain = jnp.clip(1.0 + 0.1 * jax.random.normal(splits[13], (D,), jnp.float32), 0.5, 1.5).astype(jnp.bfloat16)
    ln2_bias = noise(splits[14], (D,), 0.3, 1.75, ((0, 4),))
    fc1_weight = noise(splits[15], (D, FF), D ** -0.5, 0.21875, ((1, 4),))
    fc1_bias = noise(splits[16], (FF,), 0.3, 1.75, ((0, 4),))
    fc2_weight = noise(splits[17], (FF, D), FF ** -0.5, 0.109375, ((1, 4),))
    fc2_bias = noise(splits[18], (D,), 0.3, 1.75, ((0, 4),))
    cotangent = noise(splits[19], (CLIPS, STATES, D), 1.0, 6.0, ((0, 8), (1, 4)))
    return dict(mel_frames=mel_frames, lengths=lengths, conv1_weight=conv1_weight, conv1_bias=conv1_bias, conv2_weight=conv2_weight, conv2_bias=conv2_bias, ln1_gain=ln1_gain, ln1_bias=ln1_bias, qkv_weight=qkv_weight, q_bias=q_bias, v_bias=v_bias, out_weight=out_weight, out_bias=out_bias, ln2_gain=ln2_gain, ln2_bias=ln2_bias, fc1_weight=fc1_weight, fc1_bias=fc1_bias, fc2_weight=fc2_weight, fc2_bias=fc2_bias, cotangent=cotangent)


@jax.custom_vjp
def low(v):
    return lax.optimization_barrier(v.astype(jnp.bfloat16)).astype(jnp.float32)

@jax.custom_vjp
def low_back(v):
    return v

def low_keep(v):
    return (low(v), None)

def low_pass(kept, grad):
    return (grad,)

def back_keep(v):
    return (v, None)

def back_low(kept, grad):
    return (low(grad),)
low.defvjp(low_keep, low_pass)
low_back.defvjp(back_keep, back_low)
highest = lax.Precision.HIGHEST

def gelu_exact(values_in):
    return jax.nn.gelu(values_in, approximate=False)

def layer_norm(values_in, gain, shift):
    center = values_in - lax.optimization_barrier(jnp.mean(values_in, axis=-1, keepdims=True))
    spread = lax.optimization_barrier(jnp.mean(center * center, axis=-1, keepdims=True))
    return center * lax.rsqrt(spread + 1e-05) * gain + shift

def positions(first, count, width):
    half = width // 2
    rates = jnp.exp(-(math.log(10000.0) / (half - 1)) * jnp.arange(half, dtype=jnp.float32))
    angles = (first + jnp.arange(count)).astype(jnp.float32)[:, None] * rates[None, :]
    return jnp.concatenate([jnp.sin(angles), jnp.cos(angles)], axis=1)

def clip_forward(params, mel_clip, length):
    conv1_weight, conv1_bias, conv2_weight, conv2_bias, ln1_gain, ln1_bias, qkv_weight, q_bias, v_bias, out_weight, out_bias, ln2_gain, ln2_bias, fc1_weight, fc1_bias, fc2_weight, fc2_bias = params
    model_width = conv2_weight.shape[2]
    score_scale = 1.0 / math.sqrt(HEAD_DIM)
    frame_valid = (jnp.arange(FRAMES) < length)[:, None]
    masked_mel = jnp.where(frame_valid, mel_clip, 0.0)
    padded = jnp.pad(masked_mel, ((1, 1), (0, 0)))
    conv1_pre = conv1_bias
    for shift_tap in range(3):
        conv1_pre = conv1_pre + jnp.dot(padded[shift_tap:shift_tap + FRAMES], conv1_weight[shift_tap], precision=highest)
    conv1_pre = low_back(conv1_pre)
    frame_act = low(gelu_exact(conv1_pre))
    shifted = jnp.pad(frame_act, ((1, 0), (0, 0)))
    conv2_pre = conv2_bias
    for shift_tap in range(3):
        conv2_pre = conv2_pre + jnp.dot(shifted[shift_tap:shift_tap + 2 * STATES:2], conv2_weight[shift_tap], precision=highest)
    conv2_pre = low_back(conv2_pre)
    block_input = gelu_exact(conv2_pre) + positions(0, STATES, model_width)
    normed1 = low(layer_norm(block_input, ln1_gain, ln1_bias))
    mixed = jnp.dot(normed1, qkv_weight, precision=highest)
    queries = low_back(low(mixed[:, :model_width] + q_bias))
    keys = low_back(low(mixed[:, model_width:2 * model_width]))
    values = low_back(low(mixed[:, 2 * model_width:] + v_bias))
    query_heads = queries.reshape(STATES, HEADS, HEAD_DIM)
    key_heads = keys.reshape(STATES, HEADS, HEAD_DIM)
    value_heads = values.reshape(STATES, HEADS, HEAD_DIM)
    scores = low_back(jnp.einsum('qhd,khd->hqk', query_heads, key_heads, precision=highest) * score_scale)
    key_valid = 2 * jnp.arange(STATES) < length
    scores = jnp.where(key_valid[None, None, :], scores, -1e+30)
    largest = lax.optimization_barrier(jnp.max(scores, axis=-1, keepdims=True))
    exponent = jnp.exp(scores - largest)
    probs = exponent / lax.optimization_barrier(jnp.sum(exponent, axis=-1, keepdims=True))
    attended = jnp.einsum('hqk,khd->qhd', low(probs), value_heads, precision=highest).reshape(STATES, model_width)
    attended = low_back(low(attended))
    branch = low_back(jnp.dot(attended, out_weight, precision=highest) + out_bias)
    middle = block_input + branch
    normed2 = low(layer_norm(middle, ln2_gain, ln2_bias))
    hidden_pre = low_back(jnp.dot(normed2, fc1_weight, precision=highest) + fc1_bias)
    hidden_act = low(gelu_exact(hidden_pre))
    return middle + jnp.dot(hidden_act, fc2_weight, precision=highest) + fc2_bias

def reference(mel_frames, lengths, conv1_weight, conv1_bias, conv2_weight, conv2_bias, ln1_gain, ln1_bias, qkv_weight, q_bias, v_bias, out_weight, out_bias, ln2_gain, ln2_bias, fc1_weight, fc1_bias, fc2_weight, fc2_bias, cotangent):
    params = (conv1_weight, conv1_bias, conv2_weight, conv2_bias, ln1_gain, ln1_bias, qkv_weight, q_bias, v_bias, out_weight, out_bias, ln2_gain, ln2_bias, fc1_weight, fc1_bias, fc2_weight, fc2_bias)
    floats = tuple((member.astype(jnp.float32) for member in params))

    def forward(mel_float, *weights):

        def per_clip(clip_item):
            return clip_forward(weights, clip_item[0], clip_item[1])
        return lax.map(jax.checkpoint(per_clip), (mel_float, lengths))
    outputs, pull_back = jax.vjp(forward, mel_frames.astype(jnp.float32), *floats)
    gradients = pull_back(cotangent.astype(jnp.float32))
    return (outputs.astype(jnp.bfloat16), gradients[0].astype(jnp.bfloat16), gradients[1], gradients[2], gradients[3], gradients[4], gradients[5], gradients[6], gradients[7], gradients[8], gradients[9], gradients[10], gradients[11], gradients[12], gradients[13], gradients[14], gradients[15], gradients[16], gradients[17])
```

```python
import math

import jax
import jax.numpy as jnp
from jax import lax
from jax.sharding import PartitionSpec as P

HEADS = 12
HEAD_DIM = 64
F32 = jnp.float32
BF16 = jnp.bfloat16
SCALE = 1.0 / math.sqrt(HEAD_DIM)
ROWS = 16


def xor_swap(array, axis, mask):
    size = lax.axis_size(axis)
    return lax.ppermute(array, axis, [(i, i ^ mask) for i in range(size)])


def pick(array, index, axis=0):
    return lax.dynamic_index_in_dim(array, index, axis=axis, keepdims=False)


def bits_of(size):
    return [1 << b for b in range(size.bit_length() - 1)]


def gelu_pair(v):
    a = jnp.abs(v) * (1.0 / math.sqrt(2.0))
    t = 1.0 / (1.0 + 0.3275911 * a)
    poly = t * (
        0.254829592
        + t * (-0.284496736 + t * (1.421413741 + t * (-1.453152027 + t * 1.061405429)))
    )
    bell = jnp.exp(-0.5 * v * v)
    tail = 0.5 * poly * bell
    cdf = jnp.where(v >= 0, 1.0 - tail, tail)
    return v * cdf, cdf + v * bell * (1.0 / math.sqrt(2.0 * math.pi))


def norm_parts(v):
    center = v - jnp.mean(v, axis=-1, keepdims=True)
    spread = jnp.mean(center * center, axis=-1, keepdims=True)
    scale = lax.rsqrt(spread + 1e-05)
    return center * scale, scale


def norm_back(grad, unit, scale, gain):
    a = grad * gain
    mean_a = jnp.mean(a, axis=-1, keepdims=True)
    mean_an = jnp.mean(a * unit, axis=-1, keepdims=True)
    return (a - mean_a - unit * mean_an) * scale


def positions(starts, count, width):
    half = width // 2
    rates = jnp.exp(-(math.log(10000.0) / (half - 1)) * jnp.arange(half, dtype=F32))
    angles = (starts[:, None] + jnp.arange(count)[None, :]).astype(F32)[..., None] * rates
    return jnp.concatenate([jnp.sin(angles), jnp.cos(angles)], axis=-1)


def mat(a, b):
    return jnp.dot(a, b, preferred_element_type=F32)


def mat_t(a, b):
    return lax.dot_general(a, b, (((1,), (1,)), ((), ())), preferred_element_type=F32)


def gather_rows(shard, place, parts):
    pieces = [shard]
    masks = [0]
    for mask in [m for m in bits_of(parts) if m > 1]:
        pieces = pieces + [xor_swap(p, "tm", mask) for p in pieces]
        masks = masks + [m ^ mask for m in masks]
    stack = jnp.stack(pieces)
    other = xor_swap(stack, "tm", 1)
    whole = jnp.zeros((parts,) + shard.shape, shard.dtype)
    for i, mask in enumerate(masks):
        whole = lax.dynamic_update_slice(whole, stack[i][None], (place ^ mask, 0, 0))
        whole = lax.dynamic_update_slice(whole, other[i][None], (place ^ mask ^ 1, 0, 0))
    return whole.reshape(parts * shard.shape[0], shard.shape[1])


def halve(array, axis, index, shift, size):
    for bit in bits_of(size):
        blocks = array.reshape((array.shape[0] // 2, 2) + array.shape[1:])
        mine = (index // bit) % 2
        got = xor_swap(pick(blocks, 1 - mine, 1), axis, bit * shift)
        array = (pick(blocks, mine, 1).astype(F32) + got.astype(F32)).astype(array.dtype)
    return array


def double(array, axis, index, shift, size):
    for bit in reversed(bits_of(size)):
        mine = (index // bit) % 2
        got = xor_swap(array, axis, bit * shift)
        array = jnp.stack(
            [jnp.where(mine == 0, array, got), jnp.where(mine == 0, got, array)], axis=1
        )
        array = array.reshape((array.shape[0] * 2,) + array.shape[2:])
    return array


def per_device(
    mel_frames,
    lengths,
    conv1_weight,
    conv1_bias,
    conv2_weight,
    conv2_bias,
    ln1_gain,
    ln1_bias,
    qkv_weight,
    q_bias,
    v_bias,
    out_weight,
    out_bias,
    ln2_gain,
    ln2_bias,
    fc1_weight,
    fc1_bias,
    fc2_weight,
    fc2_bias,
    cotangent,
):
    parts = lax.axis_size("tm")
    place = lax.axis_index("tm")
    clips = lax.axis_size("clip")
    clip_place = lax.axis_index("clip")
    y_size = parts // 2
    x_size = y_size
    z_size = clips // x_size
    core, y_place = place % 2, place // 2
    x_place, z_place = clip_place % x_size, clip_place // x_size
    mine = y_place % 2
    frames, mels = mel_frames.shape[1:]
    states, width = cotangent.shape[1:]
    hidden = fc1_weight.shape[1] * parts
    rows = 2 * states

    w1_own = jnp.pad(conv1_weight.reshape(3 * mels, -1).T, ((0, 0), (0, 16)))
    w2_own = conv2_weight.reshape(3 * width, -1).T
    vec_own = jnp.concatenate(
        [
            conv1_bias,
            conv2_bias,
            ln1_gain,
            ln1_bias,
            q_bias,
            v_bias,
            out_bias,
            ln2_gain,
            ln2_bias,
            fc2_bias,
            fc1_bias,
        ]
    )
    vec_own = jnp.pad(vec_own, (0, -vec_own.shape[0] % 128)).reshape(-1, 128)
    w1 = gather_rows(w1_own, place, parts)
    vecs = gather_rows(vec_own, place, parts)
    w2 = gather_rows(w2_own, place, parts)
    wqkv = gather_rows(qkv_weight.T, place, parts)
    wout = gather_rows(out_weight.T, place, parts)
    wfc1 = gather_rows(fc1_weight.T, place, parts)
    wfc2 = gather_rows(fc2_weight.T, place, parts)
    share = conv1_bias.shape[0]
    vecs = vecs.reshape(parts, -1).astype(F32)
    b1, b2, gain_one, shift_one, bq, bv, bout, gain_two, shift_two, bfc2 = [
        vecs[:, i * share : (i + 1) * share].reshape(-1) for i in range(10)
    ]
    bfc1 = vecs[:, 10 * share : 10 * share + fc1_bias.shape[0]].reshape(-1)

    def swapped(array):
        got = xor_swap(pick(array, 1 - mine), "tm", 2)
        own = pick(array, mine)
        return jnp.where(mine == 0, jnp.stack([own, got]), jnp.stack([got, own]))

    length = pick(lengths, mine)
    segs_of = lambda device: 4 * (device // 4) + 2 * jnp.arange(2) + device % 2
    seg = segs_of(place)
    frame_ids = seg[:, None] * frames + jnp.arange(frames)[None, :]
    frame_valid = (frame_ids < length)[..., None]
    mel_clip = swapped(mel_frames)
    cot = swapped(cotangent).reshape(rows, width)
    masked = jnp.where(frame_valid, mel_clip, jnp.zeros_like(mel_clip))
    pairs = masked.reshape(2, states, 2, mels)
    even, odd = pairs[:, :, 0], pairs[:, :, 1]

    def neighbours(first, last):
        got_first, got_last = xor_swap((first, last), "tm", 1)
        far_last, far_first = jnp.zeros_like(last[0]), jnp.zeros_like(first[0])
        if y_size > 2:
            up = [(i, i + 3) for i in range(parts - 3) if i % 2 == 1]
            far_last = lax.ppermute(last[1], "tm", up)
            far_first = lax.ppermute(first[0], "tm", [(j, i) for i, j in up])
        is_zero = core == 0
        before = jnp.stack(
            [
                jnp.where(is_zero, far_last, got_last[0]),
                jnp.where(is_zero, got_last[0], got_last[1]),
            ]
        )
        after = jnp.stack(
            [
                jnp.where(is_zero, got_first[0], got_first[1]),
                jnp.where(is_zero, got_first[1], far_first),
            ]
        )
        return before, after

    before, after = neighbours(even[:, 0], jnp.stack([even[:, -1], odd[:, -1]], axis=1))
    odd_before = jnp.concatenate([before[:, 1:2], odd[:, :-1]], axis=1)
    even_after = jnp.concatenate([even[:, 1:], after[:, None]], axis=1)
    taps = jnp.concatenate(
        [
            jnp.concatenate([odd_before, even, odd], axis=2).reshape(rows, 3 * mels),
            jnp.concatenate([even, odd, even_after], axis=2).reshape(rows, 3 * mels),
            jnp.concatenate([before[:, 0], before[:, 1], even[:, 0]], axis=1),
            jnp.zeros((ROWS - 2, 3 * mels), BF16),
        ],
        axis=0,
    )
    taps = jnp.pad(taps, ((0, 0), (0, 16)))
    frame_pre = mat_t(taps, w1) + b1
    frame_act, frame_slope = gelu_pair(frame_pre)
    frame_act = frame_act.astype(BF16)
    frame_slope = frame_slope.astype(BF16)
    even_act = frame_act[:rows]
    odd_act = frame_act[rows : 2 * rows]
    inside = (seg > 0)[:, None]
    edge_act = jnp.where(inside, frame_act[2 * rows : 2 * rows + 2], 0)
    edge_slope = jnp.where(inside, frame_slope[2 * rows : 2 * rows + 2], 0)
    prev_act = jnp.concatenate(
        [edge_act[:, None], odd_act.reshape(2, states, width)[:, :-1]], axis=1
    ).reshape(rows, width)
    state_taps = jnp.concatenate([prev_act, even_act, odd_act], axis=1)
    state_pre = mat_t(state_taps, w2) + b2
    state_act, state_slope = gelu_pair(state_pre)
    block_input = state_act + positions(seg * states, states, width).reshape(rows, width)
    unit1, scale1 = norm_parts(block_input)
    normed1 = (unit1 * gain_one + shift_one).astype(BF16)
    bias_qkv = jnp.concatenate([bq, jnp.zeros_like(bq), bv])
    mixed = (mat_t(normed1, wqkv) + bias_qkv).astype(BF16)
    queries = mixed[:, :width]
    keys = mixed[:, width : 2 * width]
    values = mixed[:, 2 * width :]

    group = [m for m in bits_of(parts) if m != 2]
    pair = jnp.stack([keys, values])
    masks = [0]
    for mask in group:
        pair = jnp.concatenate([pair, xor_swap(pair, "tm", mask)], axis=1)
        masks = masks + [m ^ mask for m in masks]
    segs = jnp.concatenate([segs_of(place ^ m) for m in masks])
    key_ids = (segs[:, None] * states + jnp.arange(states)[None, :]).reshape(-1)
    key_valid = 2 * key_ids < length
    all_states = key_ids.shape[0]

    def heads(array):
        return array.reshape(-1, HEADS, HEAD_DIM)

    q_h, k_h, v_h = heads(queries), heads(pair[0]), heads(pair[1])
    scores = jnp.einsum("qhd,khd->hqk", q_h, k_h, preferred_element_type=F32) * SCALE
    scores = jnp.where(key_valid, scores, -1e30)
    largest = jnp.max(scores, axis=-1, keepdims=True)
    exponent = jnp.exp(scores - largest)
    probs = (exponent / jnp.sum(exponent, axis=-1, keepdims=True)).astype(BF16)
    attended = jnp.einsum("hqk,khd->qhd", probs, v_h, preferred_element_type=F32)
    attended = attended.reshape(rows, width).astype(BF16)
    middle = block_input + mat_t(attended, wout) + bout
    unit2, scale2 = norm_parts(middle)
    normed2 = (unit2 * gain_two + shift_two).astype(BF16)
    hidden_act, hidden_slope = gelu_pair(mat_t(normed2, wfc1) + bfc1)
    hidden_act = hidden_act.astype(BF16)
    hidden_slope = hidden_slope.astype(BF16)
    out_rows = (middle + mat_t(hidden_act, wfc2) + bfc2).astype(BF16)

    def unswapped(array):
        got = xor_swap(pick(array, 1 - mine), "tm", 2)
        own = pick(array, mine)
        return jnp.where(mine == 0, jnp.stack([own, got]), jnp.stack([got, own]))

    out_states = unswapped(out_rows.reshape(2, states, width))

    def chip_grad(grad, acts):
        blocks = grad.reshape(rows, y_size, 2, -1)
        sent, kept = pick(blocks, 1 - core, 2), pick(blocks, core, 2)
        product = lambda g: jnp.einsum("ryn,rk->ynk", g, acts, preferred_element_type=F32)
        got = xor_swap(product(sent).astype(BF16), "tm", 1)
        total = (product(kept) + got.astype(F32)).astype(BF16)
        return total.reshape(y_size, -1, width)

    def all_sum(pieces):
        packed = jnp.concatenate(pieces, axis=1)
        sizes = [p.shape[1] for p in pieces]
        count = sum(sizes)
        step = ROWS * x_size * z_size
        packed = jnp.pad(packed, ((0, 0), (0, -count % step), (0, 0)))
        packed = halve(packed, "tm", y_place, 2, y_size)[0]
        packed = packed.reshape(z_size, x_size, -1, width).swapaxes(0, 1)
        packed = halve(packed, "clip", x_place, 1, x_size)[0]
        packed = halve(packed, "clip", z_place, x_size, z_size)
        packed = double(packed, "clip", z_place, x_size, z_size)
        packed = double(packed[None], "clip", x_place, 1, x_size)
        packed = packed.swapaxes(0, 1).reshape(-1, width)
        ends = [sum(sizes[: i + 1]) for i in range(len(sizes))]
        return [packed[e - s : e].astype(F32) for e, s in zip(ends, sizes)]

    cot_float = cot.astype(F32)
    fc2_part = chip_grad(cot, hidden_act)
    bfc2_grad = jnp.sum(cot_float, axis=0)
    hidden_grad = (mat(cot, wfc2) * hidden_slope.astype(F32)).astype(BF16)
    fc1_part = chip_grad(hidden_grad, normed2)
    bfc1_grad = jnp.sum(hidden_grad.astype(F32), axis=0)
    normed2_grad = mat(hidden_grad, wfc1)
    gain_two_grad = jnp.sum(normed2_grad * unit2, axis=0)
    shift_two_grad = jnp.sum(normed2_grad, axis=0)
    middle_grad = cot_float + norm_back(normed2_grad, unit2, scale2, gain_two)
    branch_grad = middle_grad.astype(BF16)
    out_part = chip_grad(branch_grad, attended)
    bout_grad = jnp.sum(branch_grad.astype(F32), axis=0)
    fc2_sum, fc1_sum, out_sum = all_sum([fc2_part, fc1_part, out_part])

    attended_grad = mat(branch_grad, wout).astype(BF16)
    a_h = heads(attended_grad)
    row_dot = jnp.sum(a_h.astype(F32) * heads(attended).astype(F32), axis=-1)
    probs_grad = jnp.einsum("qhd,khd->hqk", a_h, v_h, preferred_element_type=F32)
    score_grad = (probs.astype(F32) * (probs_grad - row_dot.T[..., None])).astype(BF16)
    queries_grad = jnp.einsum("hqk,khd->qhd", score_grad, k_h, preferred_element_type=F32)
    queries_grad = (queries_grad * SCALE).reshape(rows, width).astype(BF16)
    keys_term = jnp.einsum("hqk,qhd->khd", score_grad, q_h, preferred_element_type=F32) * SCALE
    values_term = jnp.einsum("hqk,qhd->khd", probs, a_h, preferred_element_type=F32)
    terms = jnp.stack(
        [keys_term.reshape(all_states, width), values_term.reshape(all_states, width)]
    ).astype(BF16)
    for mask in reversed(group):
        half = terms.shape[1] // 2
        got = xor_swap(terms[:, half:], "tm", mask)
        terms = (terms[:, :half].astype(F32) + got.astype(F32)).astype(BF16)
    projected_grad = jnp.concatenate([queries_grad, terms[0], terms[1]], axis=1)
    qkv_part = chip_grad(projected_grad, normed1)
    projected_sum = jnp.sum(projected_grad.astype(F32), axis=0)
    normed1_grad = mat(projected_grad, wqkv)
    gain_one_grad = jnp.sum(normed1_grad * unit1, axis=0)
    shift_one_grad = jnp.sum(normed1_grad, axis=0)
    input_grad = middle_grad + norm_back(normed1_grad, unit1, scale1, gain_one)
    state_grad = (input_grad * state_slope).astype(BF16)
    conv2_part = chip_grad(state_grad, state_taps)
    b2_grad = jnp.sum(state_grad.astype(F32), axis=0)
    taps_grad = mat(state_grad, w2)
    prev_grad = taps_grad[:, :width].reshape(2, states, width)
    odd_grad = taps_grad[:, 2 * width :].reshape(2, states, width)
    odd_grad = odd_grad + jnp.pad(prev_grad[:, 1:], ((0, 0), (0, 1), (0, 0)))
    main_grad = jnp.concatenate(
        [taps_grad[:, width : 2 * width], odd_grad.reshape(rows, width)], axis=0
    )
    main_grad = (main_grad * frame_slope[: 2 * rows]).astype(BF16)
    edge_grad = (prev_grad[:, 0] * edge_slope).astype(BF16)
    edge_grad = jnp.pad(edge_grad, ((0, ROWS - 2), (0, 0)))
    frame_grad = jnp.concatenate([main_grad, edge_grad], axis=0)
    b1_grad = jnp.sum(frame_grad.astype(F32), axis=0)

    blocks = frame_grad.reshape(-1, y_size, 2, share)
    sent, kept = pick(blocks, 1 - core, 2), pick(blocks, core, 2)
    product = lambda g: jnp.einsum("ryn,rk->ynk", g, taps, preferred_element_type=F32)
    got = xor_swap(product(sent).astype(BF16), "tm", 1)
    conv1_part = (product(kept) + got.astype(F32)).astype(BF16).reshape(y_size, -1, width)

    vec_grads = [
        b1_grad,
        b2_grad,
        gain_one_grad,
        shift_one_grad,
        projected_sum[:width],
        projected_sum[2 * width :],
        bout_grad,
        gain_two_grad,
        shift_two_grad,
        bfc2_grad,
        bfc1_grad,
    ]
    vec_part = jnp.concatenate([v.reshape(y_size, 2, -1) for v in vec_grads], axis=2)
    got = xor_swap(pick(vec_part, 1 - core, 1), "tm", 1)
    vec_part = (pick(vec_part, core, 1) + got).astype(BF16)
    vec_part = jnp.pad(vec_part, ((0, 0), (0, -vec_part.shape[1] % width)))
    vec_part = vec_part.reshape(y_size, -1, width)
    qkv_sum, conv2_sum, conv1_sum, vec_sum = all_sum([qkv_part, conv2_part, conv1_part, vec_part])

    taps_back = mat(frame_grad, w1)
    tap = lambda a, i: a[..., i * mels : (i + 1) * mels]
    even_back = taps_back[:rows].reshape(2, states, -1)
    odd_back = taps_back[rows : 2 * rows].reshape(2, states, -1)
    edge_back = taps_back[2 * rows : 2 * rows + 2]
    even_mel = tap(even_back, 1) + tap(odd_back, 0)
    even_mel = even_mel + jnp.concatenate(
        [tap(edge_back, 2)[:, None], tap(odd_back, 2)[:, :-1]], axis=1
    )
    odd_mel = tap(even_back, 2) + tap(odd_back, 1)
    odd_mel = odd_mel + jnp.pad(tap(even_back, 0)[:, 1:], ((0, 0), (0, 1), (0, 0)))
    to_before = jnp.stack([tap(edge_back, 0), tap(even_back, 0)[:, 0] + tap(edge_back, 1)], axis=1)
    to_after = tap(odd_back, 2)[:, -1]
    from_before, from_after = neighbours(to_before, to_after)
    even_mel = even_mel.at[:, 0].add(from_before).at[:, -1].add(from_after[:, 0])
    odd_mel = odd_mel.at[:, -1].add(from_after[:, 1])
    mel_back = jnp.stack([even_mel, odd_mel], axis=2).reshape(2, frames, mels)
    mel_back = jnp.where(frame_valid, mel_back, 0.0).astype(BF16)
    mel_grad = unswapped(mel_back)

    vec_flat = vec_sum.reshape(-1)
    vec_out = [vec_flat[i * share : (i + 1) * share] for i in range(10)]
    vec_out.append(vec_flat[10 * share : 10 * share + fc1_bias.shape[0]])
    conv1_out = conv1_sum.reshape(share, -1)[:, : 3 * mels].T.reshape(3, mels, share)
    conv2_out = conv2_sum.reshape(share, 3 * width).T.reshape(3, width, share)
    return (
        out_states,
        mel_grad,
        conv1_out,
        vec_out[0],
        conv2_out,
        vec_out[1],
        vec_out[2],
        vec_out[3],
        qkv_sum.T,
        vec_out[4],
        vec_out[5],
        out_sum.T,
        vec_out[6],
        vec_out[7],
        vec_out[8],
        fc1_sum.T,
        vec_out[10],
        fc2_sum.reshape(share, hidden).T,
        vec_out[9],
    )


def solution(mesh):
    return jax.shard_map(
        per_device,
        mesh=mesh,
        in_specs=(
            P("clip", "tm", None),
            P("clip"),
            P(None, None, "tm"),
            P("tm"),
            P(None, None, "tm"),
            P("tm"),
            P("tm"),
            P("tm"),
            P(None, "tm"),
            P("tm"),
            P("tm"),
            P(None, "tm"),
            P("tm"),
            P("tm"),
            P("tm"),
            P(None, "tm"),
            P("tm"),
            P(None, "tm"),
            P("tm"),
            P("clip", "tm", None),
        ),
        out_specs=(
            P("clip", "tm", None),
            P("clip", "tm", None),
            P(None, None, "tm"),
            P("tm"),
            P(None, None, "tm"),
            P("tm"),
            P("tm"),
            P("tm"),
            P(None, "tm"),
            P("tm"),
            P("tm"),
            P(None, "tm"),
            P("tm"),
            P("tm"),
            P("tm"),
            P(None, "tm"),
            P("tm"),
            P(None, "tm"),
            P("tm"),
        ),
        check_vma=False,
    )
```

```python
import functools
import math

import jax
import jax.numpy as jnp
import numpy as np
from jax import lax
from jax.experimental import pallas as pl
from jax.experimental.pallas import tpu as pltpu
from jax.sharding import PartitionSpec as P

HEADS = 12
HEAD_DIM = 64
F32 = jnp.float32
BF16 = jnp.bfloat16
SCALE = 1.0 / math.sqrt(HEAD_DIM)
TILE = 16
LANES = 128
MESH = pl.DeviceIdType.MESH
ANY = pl.BlockSpec(memory_space=pl.ANY)
VMEM = pl.BlockSpec(memory_space=pltpu.VMEM)


def xor_swap(array, axis, mask):
    size = lax.axis_size(axis)
    return lax.ppermute(array, axis, [(i, i ^ mask) for i in range(size)])


def pick(array, index, axis=0):
    return lax.dynamic_index_in_dim(array, index, axis=axis, keepdims=False)


def bits_of(size):
    return [1 << b for b in range(size.bit_length() - 1)]


def combos(masks):
    found = [0]
    for mask in masks:
        found = found + [m ^ mask for m in found]
    return found


def flip(index, mask):
    return index + mask * (1 - 2 * ((index // mask) % 2))


def flip_all(index, mask):
    for bit in bits_of(2 * mask) if mask else []:
        if mask & bit:
            index = flip(index, bit)
    return index


def gelu_pair(v):
    a = jnp.abs(v) * (1.0 / math.sqrt(2.0))
    t = 1.0 / (1.0 + 0.3275911 * a)
    poly = t * (
        0.254829592
        + t * (-0.284496736 + t * (1.421413741 + t * (-1.453152027 + t * 1.061405429)))
    )
    bell = jnp.exp(-0.5 * v * v)
    tail = 0.5 * poly * bell
    cdf = jnp.where(v >= 0, 1.0 - tail, tail)
    return v * cdf, cdf + v * bell * (1.0 / math.sqrt(2.0 * math.pi))


def norm_parts(v):
    center = v - jnp.mean(v, axis=-1, keepdims=True)
    spread = jnp.mean(center * center, axis=-1, keepdims=True)
    scale = lax.rsqrt(spread + 1e-05)
    return center * scale, scale


def norm_back(grad, unit, scale, gain):
    a = grad * gain
    mean_a = jnp.mean(a, axis=-1, keepdims=True)
    mean_an = jnp.mean(a * unit, axis=-1, keepdims=True)
    return (a - mean_a - unit * mean_an) * scale


def positions(count, width):
    half = width // 2
    rates = np.exp(-(math.log(10000.0) / (half - 1)) * np.arange(half))
    angles = np.arange(count)[:, None] * rates[None, :]
    return np.concatenate([np.sin(angles), np.cos(angles)], axis=1).astype(np.float32)


def mat(a, b):
    return jnp.dot(a, b, preferred_element_type=F32)


def mat_t(a, b):
    return lax.dot_general(a, b, (((1,), (1,)), ((), ())), preferred_element_type=F32)


def mat_l(a, b):
    return lax.dot_general(a, b, (((0,), (0,)), ((), ())), preferred_element_type=F32)


def aligned(index, step):
    return pl.multiple_of(index * step, step)


class Place:
    def __init__(self):
        self.parts = lax.axis_size("tm")
        self.clips = lax.axis_size("clip")
        self.tm = lax.axis_index("tm")
        self.cl = lax.axis_index("clip")
        self.y_size = self.parts // 2
        self.x_size = self.y_size
        self.z_size = self.clips // self.x_size
        self.core = self.tm % 2
        self.y = self.tm // 2
        self.x = self.cl % self.x_size
        self.z = self.cl // self.x_size

    def tm_partner(self, mask):
        return {"tm": flip(self.tm, mask)}

    def clip_partner(self, mask):
        return {"clip": flip(self.cl, mask)}


def greet(partners):
    barrier = pltpu.get_barrier_semaphore()
    for partner in partners:
        pl.semaphore_signal(barrier, inc=1, device_id=partner, device_id_type=MESH)
    pl.semaphore_wait(barrier, len(partners))


class Gather:
    def __init__(self, at, own, full, first, count, sends, receives, base):
        self.at, self.own, self.full = at, own, full
        self.first, self.count = first, count
        self.shard = own.shape[0]
        self.split = at.x_size if count % (TILE * at.x_size) == 0 else 1
        self.sends, self.receives, self.base = sends, receives, base
        self.used = 0
        self.y_masks = [2 * b for b in bits_of(at.y_size)]
        self.x_masks = bits_of(at.x_size) if self.split > 1 else []
        self.y_copies, self.x_copies, self.core_copies = [], [], []
        self.started = []

    @staticmethod
    def slots(parts, split):
        y_size = parts // 2
        ys = y_size - 1
        xs = ys * (split - 1)
        return ys + xs + 1 + ys * split

    def region(self, mask, part):
        rows = self.count // self.split
        index = flip_all(self.at.tm, mask) * self.shard + self.first
        if part is not None:
            index = index + part * rows
        else:
            rows = self.count
        return pl.ds(pl.multiple_of(index, TILE), rows)

    def send(self, source, region, partner):
        slot = self.base + self.used
        self.used += 1
        copy = pltpu.make_async_remote_copy(
            src_ref=source,
            dst_ref=self.full.at[region],
            send_sem=self.sends.at[slot],
            recv_sem=self.receives.at[slot],
            device_id=partner,
            device_id_type=MESH,
        )
        copy.start()
        self.started.append(copy)
        return copy

    def part(self, mask):
        return flip_all(self.at.x, mask) if self.split > 1 else 0

    def start(self):
        at = self.at
        rows = self.count // self.split
        first = pl.multiple_of(self.first + self.part(0) * rows, TILE)
        self.pending = []
        mask = self.y_masks[0]
        copy = self.send(
            self.own.at[pl.ds(first, rows)], self.region(0, self.part(0)), at.tm_partner(mask)
        )
        self.pending.append((copy, mask))
        whole = self.own.at[pl.ds(self.first, self.count)]
        self.core_copies.append(self.send(whole, self.region(0, None), at.tm_partner(1)))

    def relay(self, mask, part):
        region = self.region(mask, part)
        self.core_copies.append(self.send(self.full.at[region], region, self.at.tm_partner(1)))

    def after_y(self):
        at = self.at
        have = []
        for i, mask in enumerate(self.y_masks):
            for copy, m in self.pending:
                copy.wait_recv()
                have.append(m)
            self.pending = []
            if i + 1 < len(self.y_masks):
                after = self.y_masks[i + 1]
                for m in [0] + have:
                    region = self.region(m, self.part(0))
                    if m == 0:
                        rows = self.count // self.split
                        first = pl.multiple_of(self.first + self.part(0) * rows, TILE)
                        source = self.own.at[pl.ds(first, rows)]
                    else:
                        source = self.full.at[region]
                    copy = self.send(source, region, at.tm_partner(after))
                    self.pending.append((copy, m ^ after))
        self.have = have
        for x_mask in self.x_masks[:1]:
            for m in have:
                region = self.region(m, self.part(0))
                copy = self.send(self.full.at[region], region, at.clip_partner(x_mask))
                self.x_copies.append((copy, m, x_mask))
        for m in have:
            self.relay(m, self.part(0))

    def after_x(self):
        at = self.at
        got = [0]
        for i, x_mask in enumerate(self.x_masks):
            fresh = []
            for copy, m, q in self.x_copies:
                copy.wait_recv()
                self.relay(m, self.part(q))
                if q not in fresh:
                    fresh.append(q)
            got = got + fresh
            self.x_copies = []
            if i + 1 < len(self.x_masks):
                after = self.x_masks[i + 1]
                for m in self.have:
                    for q in got:
                        region = self.region(m, self.part(q))
                        copy = self.send(self.full.at[region], region, at.clip_partner(after))
                        self.x_copies.append((copy, m, q ^ after))

    def finish(self):
        for copy in self.core_copies:
            copy.wait_recv()

    def close(self):
        for copy in self.started:
            copy.wait_send()


def front_kernel(states, mel_in, w1_own, vec_own, w2_own, wqkv_own, pos_in, *refs):
    (
        w1, vec_raw, vecs, w2, wqkv, taps, x_even, x_odd, slope_even, slope_odd,
        slope_state, block_input, normed, queries, keys, values,
        mel, odd_act, tmp, pos, sends, receives, kv_send, kv_recv, local,
    ) = refs
    at = Place()
    width = block_input.shape[1]
    rows = 2 * states
    block = 256
    mine = at.y % 2
    partners = [at.tm_partner(m) for m in bits_of(at.parts)]
    partners += [at.clip_partner(m) for m in bits_of(at.x_size)]
    seg = [4 * (at.tm // 4) + 2 * s + at.core for s in range(2)]

    locals_ = [
        pltpu.make_async_copy(mel_in.at[mine], mel.at[mine], local.at[0]),
        pltpu.make_async_copy(w1_own, w1.at[pl.ds(aligned(at.tm, w1_own.shape[0]), w1_own.shape[0])], local.at[1]),
        pltpu.make_async_copy(vec_own, vec_raw.at[pl.ds(aligned(at.tm, TILE), TILE)], local.at[2]),
        pltpu.make_async_copy(w2_own, w2.at[pl.ds(aligned(at.tm, w2_own.shape[0]), w2_own.shape[0])], local.at[3]),
        pltpu.make_async_copy(wqkv_own, wqkv.at[pl.ds(aligned(at.tm, wqkv_own.shape[0]), wqkv_own.shape[0])], local.at[4]),
    ]
    for s in range(2):
        locals_.append(
            pltpu.make_async_copy(
                pos_in.at[pl.ds(aligned(seg[s], states), states)],
                pos.at[pl.ds(s * states, states)],
                local.at[5 + s],
            )
        )
    for copy in locals_:
        copy.start()
    greet(partners)
    swap = pltpu.make_async_remote_copy(
        src_ref=mel_in.at[1 - mine],
        dst_ref=mel.at[mine],
        send_sem=kv_send.at[0],
        recv_sem=kv_recv.at[0],
        device_id=at.tm_partner(2),
        device_id_type=MESH,
    )
    swap.start()
    base = 0
    groups = []
    for own, full, pieces in ((w1_own, w1, 1), (vec_own, vec_raw, 1), (w2_own, w2, 2), (wqkv_own, wqkv, 2)):
        count = own.shape[0] // pieces if own.shape[0] % (pieces * TILE * at.x_size) == 0 else own.shape[0]
        for first in range(0, own.shape[0], count):
            g = Gather(at, own, full, first, count, sends, receives, base)
            base += Gather.slots(at.parts, g.split)
            groups.append(g)
    small, large = groups[:2], groups[2:]
    second = [g for g in large if g.own is w2_own]
    third = [g for g in large if g.own is wqkv_own]
    for g in small + second:
        g.start()
    swap.wait_recv()
    locals_[0].wait()
    for s in range(2):
        m = mel[s].astype(F32)
        size = m.shape[0]
        before = pltpu.roll(m, 1, 0)
        after = pltpu.roll(m, size - 1, 0)
        low, high = pl.ds(0, LANES), pl.ds(LANES, LANES)
        even_rows = pl.ds(s * states, states)
        odd_rows = pl.ds(s * size, size)
        x_even[even_rows, low] = before[:states, LANES:].astype(BF16)
        x_even[even_rows, pl.ds(LANES, 2 * LANES)] = m[:states].astype(BF16)
        x_odd[odd_rows, pl.ds(0, 2 * LANES)] = m.astype(BF16)
        x_odd[odd_rows, pl.ds(2 * LANES, LANES)] = after[:, :LANES].astype(BF16)
    for g in small:
        g.after_y()
    for g in second:
        g.after_y()
    for g in third:
        g.start()
    for g in small:
        g.after_x()
        g.finish()
    locals_[1].wait()
    locals_[2].wait()
    total = jnp.zeros(vecs.shape, F32)
    share = width // at.parts
    for j in range(at.parts):
        piece = vec_raw[pl.ds(j * TILE, TILE)].astype(F32)
        low = (j * share) // LANES * LANES
        cells = [piece]
        if low > 0:
            cells = [jnp.zeros((TILE, low), F32)] + cells
        if width - low - piece.shape[1] > 0:
            cells = cells + [jnp.zeros((TILE, width - low - piece.shape[1]), F32)]
        placed = jnp.concatenate(cells, axis=1)
        shift = j * share - low
        total = total + (pltpu.roll(placed, shift, 1) if shift else placed)
    vecs[...] = total

    def vec(i, cols):
        return vecs[pl.ds(i, 1), cols]

    size = states + TILE
    for s in range(2):

        def odd_columns(j, carry, s=s):
            cols = pl.ds(aligned(j, block), block)
            tmp[pl.ds(0, size)] = mat_t(x_odd[pl.ds(s * size, size)], w1[cols])

            def odd_rows(i, carry):
                r = pl.ds(aligned(i, 64), 64)
                act, slope = gelu_pair(tmp[r] + vec(0, cols))
                odd_act[r, cols] = act
                taps[pl.ds(aligned(i, 64) + s * states, 64), pl.ds(2 * width + aligned(j, block), block)] = act.astype(BF16)
                slope_odd[pl.ds(aligned(i, 64) + s * size, 64), cols] = slope.astype(BF16)
                return carry

            lax.fori_loop(0, states // 64, odd_rows, 0)
            r = pl.ds(states, TILE)
            act, slope = gelu_pair(tmp[r] + vec(0, cols))
            last = lax.broadcasted_iota(jnp.int32, act.shape, 0) == TILE - 1
            first = jnp.minimum(seg[s], 1).astype(F32)
            act = jnp.where(last, act * first, 0.0)
            slope = jnp.where(last, slope * first, 0.0)
            odd_act[r, cols] = act
            slope_odd[pl.ds(s * size + states, TILE), cols] = slope.astype(BF16)
            moved = pltpu.roll(odd_act[:, cols], 1, 0)
            taps[pl.ds(s * states, states), cols] = moved[:states].astype(BF16)
            return carry

        lax.fori_loop(0, width // block, odd_columns, 0)

        def even_columns(j, carry, s=s):
            cols = pl.ds(aligned(j, block), block)
            tmp[pl.ds(0, states)] = mat_t(x_even[pl.ds(s * states, states)], w1[cols])

            def even_rows(i, carry):
                r = pl.ds(aligned(i, 64), 64)
                act, slope = gelu_pair(tmp[r] + vec(0, cols))
                out = pl.ds(aligned(i, 64) + s * states, 64)
                taps[out, pl.ds(width + aligned(j, block), block)] = act.astype(BF16)
                slope_even[out, cols] = slope.astype(BF16)
                return carry

            lax.fori_loop(0, states // 64, even_rows, 0)
            return carry

        lax.fori_loop(0, width // block, even_columns, 0)

    for g in second:
        g.after_x()
    for g in third:
        g.after_y()
    for g in second:
        g.finish()
    locals_[3].wait()
    locals_[5].wait()
    locals_[6].wait()

    def state_columns(j, carry):
        cols = pl.ds(aligned(j, block), block)
        tmp[pl.ds(0, rows)] = mat_t(taps[...], w2[cols])

        def state_rows(i, carry):
            r = pl.ds(aligned(i, 64), 64)
            act, slope = gelu_pair(tmp[r] + vec(1, cols))
            block_input[r, cols] = act + pos[r, cols]
            slope_state[r, cols] = slope.astype(BF16)
            return carry

        lax.fori_loop(0, rows // 64, state_rows, 0)
        return carry

    lax.fori_loop(0, width // block, state_columns, 0)
    for g in third:
        g.after_x()
    full = pl.ds(0, width)

    def norm_rows(i, carry):
        r = pl.ds(aligned(i, 32), 32)
        unit, _ = norm_parts(block_input[r])
        normed[r] = (unit * vec(2, full) + vec(3, full)).astype(BF16)
        return carry

    lax.fori_loop(0, rows // 32, norm_rows, 0)
    for g in third:
        g.finish()
    locals_[4].wait()
    group = [m for m in bits_of(at.parts) if m != 2]

    def exchange(array, base):
        held = rows
        for n, mask in enumerate(group):
            copy = pltpu.make_async_remote_copy(
                src_ref=array.at[pl.ds(0, held)],
                dst_ref=array.at[pl.ds(held, held)],
                send_sem=kv_send.at[base + n],
                recv_sem=kv_recv.at[base + n],
                device_id=at.tm_partner(mask),
                device_id_type=MESH,
            )
            copy.start()
            if n + 1 < len(group):
                copy.wait()
                held = 2 * held
            else:
                return copy

    def project(target, first, bias):
        def columns(j, carry):
            cols = pl.ds(aligned(j, block), block)
            part = mat_t(normed[...], wqkv[pl.ds(first + aligned(j, block), block)])
            if bias is not None:
                part = part + vec(bias, cols)
            target[pl.ds(0, rows), cols] = part.astype(BF16)
            return carry

        lax.fori_loop(0, width // block, columns, 0)

    project(keys, width, None)
    key_copy = exchange(keys, 1)
    project(values, 2 * width, 5)
    value_copy = exchange(values, 1 + len(group))
    project(queries, 0, 4)
    key_copy.wait()
    value_copy.wait()
    swap.wait_send()
    for g in groups:
        g.close()


def front(mel, w1_own, vec_own, w2_own, wqkv_own, pos, parts, x_size):
    states = mel.shape[1] - TILE
    rows, width = 2 * states, pos.shape[1]
    every = pos.shape[0]
    shapes = [
        ((parts * w1_own.shape[0], w1_own.shape[1]), BF16),
        ((parts * TILE, vec_own.shape[1]), BF16),
        ((TILE, width), F32),
        ((parts * w2_own.shape[0], w2_own.shape[1]), BF16),
        ((parts * wqkv_own.shape[0], wqkv_own.shape[1]), BF16),
        ((rows, 3 * width), BF16),
        ((rows, 3 * LANES), BF16),
        ((rows + 2 * TILE, 3 * LANES), BF16),
        ((rows, width), BF16),
        ((rows + 2 * TILE, width), BF16),
        ((rows, width), BF16),
        ((rows, width), F32),
        ((rows, width), BF16),
        ((rows, width), BF16),
        ((every, width), BF16),
        ((every, width), BF16),
    ]
    slots = 6 * Gather.slots(parts, x_size)
    return pl.pallas_call(
        functools.partial(front_kernel, states),
        out_shape=[jax.ShapeDtypeStruct(s, d) for s, d in shapes],
        in_specs=[VMEM] * 5 + [ANY],
        out_specs=[VMEM] * len(shapes),
        scratch_shapes=[
            pltpu.VMEM(mel.shape, BF16),
            pltpu.VMEM((states + TILE, width), F32),
            pltpu.VMEM((max(rows, states + TILE), 256), F32),
            pltpu.VMEM((rows, width), F32),
            pltpu.SemaphoreType.DMA((slots,)),
            pltpu.SemaphoreType.DMA((slots,)),
            pltpu.SemaphoreType.DMA((8,)),
            pltpu.SemaphoreType.DMA((8,)),
            pltpu.SemaphoreType.DMA((7,)),
        ],
        compiler_params=pltpu.CompilerParams(
            collective_id=1, has_side_effects=True, vmem_limit_bytes=60 << 20
        ),
        name="front",
    )(mel, w1_own, vec_own, w2_own, wqkv_own, pos)


def reduce_kernel(rows, ahead, source, result, own, landing_y, *refs):
    at = Place()
    chunks = result.shape[0] // rows
    y_bits = list(reversed(bits_of(at.y_size)))
    plane = [("x", b, b) for b in bits_of(at.x_size)]
    plane += [("z", b, b * at.x_size) for b in bits_of(at.z_size)]
    depth = len(plane)
    refs = list(refs)
    sums, landing = [], []
    for k in range(depth):
        sums.append(refs.pop(0))
        landing.append(refs.pop(0))
    sends, receives, local = refs
    coord = {"x": at.x, "z": at.z}
    mine = [(coord[c] // b) % 2 for c, b, _ in plane]
    partner = [at.clip_partner(mask) for _, _, mask in plane]
    y_partner = [at.tm_partner(2 * b) for b in y_bits]
    greet(y_partner + partner)
    tops = len(y_bits)
    held = [0]
    for b in y_bits:
        held.append(held[-1] + b * ((at.y // b) % 2))

    def remote(src, dst, c, slot, device):
        return pltpu.make_async_remote_copy(
            src_ref=src,
            dst_ref=dst,
            send_sem=sends.at[c, slot],
            recv_sem=receives.at[c, slot],
            device_id=device,
            device_id_type=MESH,
        )

    def load(c):
        return pltpu.make_async_copy(
            source.at[pl.ds(held[1], y_bits[0]), pl.ds(c * rows, rows)], own.at[c], local.at[c]
        )

    def y_copy(c, k):
        b = y_bits[k]
        if k == 0:
            away = b * (1 - (at.y // b) % 2)
            src = source.at[pl.ds(away, b), pl.ds(c * rows, rows)]
        else:
            away = b * (1 - (at.y // b) % 2)
            src = own.at[c, pl.ds(away, b)]
        first = sum(y_bits[:k])
        return remote(src, landing_y.at[c, pl.ds(first, b)], c, k, y_partner[k])

    def half(k, bit):
        count = rows >> (k + 1)
        return pl.ds(aligned(bit, count), count)

    def spread(c, k):
        src = sums[k].at[c, half(k, 1 - mine[k])]
        return remote(src, landing[k].at[c], c, tops + k, partner[k])

    def kept(c, k):
        first = c * rows
        for i in range(k + 1):
            first = first + mine[i] * (rows >> (i + 1))
        return pl.ds(pl.multiple_of(first, rows >> (k + 1)), rows >> (k + 1))

    def collect(c, k):
        region = result.at[kept(c, k)]
        return remote(region, region, c, tops + depth + k, partner[k])

    def add(a, b):
        return (a.astype(F32) + b.astype(F32)).astype(BF16)

    def step(stage, c):
        if stage == 0:
            y_copy(c, 0).start()
            load(c).start()
        elif stage <= tops:
            k = stage - 1
            if k == 0:
                load(c).wait()
            y_copy(c, k).wait_recv()
            b = y_bits[k]
            first = sum(y_bits[:k])
            if k == 0:
                total = add(own[c], landing_y[c, pl.ds(first, b)])
            else:
                total = add(own[c, pl.ds(b * ((at.y // b) % 2), b)], landing_y[c, pl.ds(first, b)])
            if k + 1 < tops:
                own[c, pl.ds(0, b)] = total
                y_copy(c, k + 1).start()
            else:
                sums[0][c] = total[0]
                spread(c, 0).start()
        elif stage <= tops + depth:
            k = stage - tops - 1
            spread(c, k).wait_recv()
            total = add(sums[k][c, half(k, mine[k])], landing[k][c])
            if k + 1 < depth:
                sums[k + 1][c] = total
                spread(c, k + 1).start()
            else:
                result[kept(c, k)] = total
                collect(c, k).start()
        else:
            k = depth - 1 - (stage - tops - depth - 1)
            collect(c, k).wait_recv()
            if k > 0:
                collect(c, k - 1).start()

    stages = 1 + tops + 2 * depth
    delays = [0] + [ahead + s for s in range(stages - 1)]
    for time in range(chunks + delays[-1]):
        for stage in range(stages):
            c = time - delays[stage]
            if 0 <= c < chunks:
                step(stage, c)
    for c in range(chunks):
        for k in range(tops):
            y_copy(c, k).wait_send()
        for k in range(depth):
            spread(c, k).wait_send()
            collect(c, k).wait_send()


def reduce_all(source, clips):
    y_size, count, width = source.shape
    x_size = y_size
    plane = len(bits_of(x_size)) + len(bits_of(clips // x_size))
    rows = TILE << plane
    chunks = count // rows
    scratch = [
        pltpu.VMEM((chunks, y_size // 2, rows, width), BF16),
        pltpu.VMEM((chunks, y_size - 1, rows, width), BF16),
    ]
    for k in range(plane):
        scratch.append(pltpu.VMEM((chunks, rows >> k, width), BF16))
        scratch.append(pltpu.VMEM((chunks, rows >> (k + 1), width), BF16))
    slots = len(bits_of(y_size)) + 2 * plane
    scratch += [pltpu.SemaphoreType.DMA((chunks, slots))] * 2
    scratch += [pltpu.SemaphoreType.DMA((chunks,))]
    return pl.pallas_call(
        functools.partial(reduce_kernel, rows, 3),
        out_shape=jax.ShapeDtypeStruct((count, width), BF16),
        in_specs=[ANY],
        out_specs=VMEM,
        scratch_shapes=scratch,
        compiler_params=pltpu.CompilerParams(
            collective_id=2, has_side_effects=True, vmem_limit_bytes=60 << 20
        ),
        name="reduce",
    )(source)


def gather_rows(shard, place, parts):
    pieces = [shard]
    masks = [0]
    for mask in [m for m in bits_of(parts) if m > 1]:
        pieces = pieces + [xor_swap(p, "tm", mask) for p in pieces]
        masks = masks + [m ^ mask for m in masks]
    stack = jnp.stack(pieces)
    other = xor_swap(stack, "tm", 1)
    whole = jnp.zeros((parts,) + shard.shape, shard.dtype)
    for i, mask in enumerate(masks):
        whole = lax.dynamic_update_slice(whole, stack[i][None], (place ^ mask, 0, 0))
        whole = lax.dynamic_update_slice(whole, other[i][None], (place ^ mask ^ 1, 0, 0))
    return whole.reshape(parts * shard.shape[0], shard.shape[1])


def per_device(
    mel_frames,
    lengths,
    conv1_weight,
    conv1_bias,
    conv2_weight,
    conv2_bias,
    ln1_gain,
    ln1_bias,
    qkv_weight,
    q_bias,
    v_bias,
    out_weight,
    out_bias,
    ln2_gain,
    ln2_bias,
    fc1_weight,
    fc1_bias,
    fc2_weight,
    fc2_bias,
    cotangent,
):
    parts = lax.axis_size("tm")
    place = lax.axis_index("tm")
    clips = lax.axis_size("clip")
    y_size = parts // 2
    core, y_place = place % 2, place // 2
    mine = y_place % 2
    frames, mels = mel_frames.shape[1:]
    states, width = cotangent.shape[1:]
    hidden = fc1_weight.shape[1] * parts
    rows = 2 * states
    share = conv1_bias.shape[0]
    size = states + TILE

    w1_own = jnp.pad(conv1_weight, ((0, 0), (0, LANES - mels), (0, 0))).reshape(3 * LANES, share).T
    w2_own = conv2_weight.reshape(3 * width, share).T
    vec_list = [
        conv1_bias, conv2_bias, ln1_gain, ln1_bias, q_bias, v_bias, out_bias, ln2_gain, ln2_bias,
        fc2_bias,
    ]
    vec_own = jnp.concatenate([jnp.stack(vec_list), fc1_bias.reshape(-1, share)], axis=0)
    vec_count = vec_own.shape[0]
    vec_own = jnp.pad(vec_own, ((0, TILE - vec_count), (0, -share % LANES)))

    frame_ids = place * frames + jnp.arange(frames)
    frame_valid = (frame_ids[None, :] < lengths[:, None])[..., None]
    masked = jnp.where(frame_valid, mel_frames, jnp.zeros_like(mel_frames))
    masked = jnp.pad(masked.reshape(2, states, 2, mels), ((0, 0), (0, 0), (0, 0), (0, LANES - mels)))
    masked = masked.reshape(2, states, 2 * LANES)
    up = [(i, i + 1) for i in range(parts - 1)]
    down = [(j, i) for i, j in up]
    before = lax.ppermute(masked[:, states - 1 :], "tm", up)
    after = lax.ppermute(masked[:, :1], "tm", down)
    gap = jnp.zeros((2, TILE - 2, 2 * LANES), BF16)
    mel_ext = jnp.concatenate([masked, after, gap, before], axis=1)
    (
        w1, vec_raw, vecs, w2, wqkv, state_taps, x_even, x_odd, slope_even, slope_odd,
        state_slope, block_input, normed1, queries, keys, values,
    ) = front(
        mel_ext, w1_own, vec_own, w2_own, qkv_weight.T,
        jnp.asarray(positions(states * parts, width)), parts, y_size,
    )
    gain_one, bout, gain_two, shift_two, bfc2 = [vecs[i] for i in (2, 6, 7, 8, 9)]
    bfc1 = vec_raw.reshape(parts, TILE, -1)[:, 10:vec_count, :share].astype(F32).reshape(-1)
    wout = gather_rows(out_weight.T, place, parts)
    wfc1 = gather_rows(fc1_weight.T, place, parts)
    wfc2 = gather_rows(fc2_weight.T, place, parts)

    def swapped(array):
        got = xor_swap(pick(array, 1 - mine), "tm", 2)
        own = pick(array, mine)
        return jnp.where(mine == 0, jnp.stack([own, got]), jnp.stack([got, own]))

    length = pick(lengths, mine)
    cot = swapped(cotangent).reshape(rows, width)
    unit1, scale1 = norm_parts(block_input)
    group = [m for m in bits_of(parts) if m != 2]
    segs = [4 * ((place ^ m) // 4) + 2 * jnp.arange(2) + (place ^ m) % 2 for m in combos(group)]
    segs = jnp.concatenate(segs)
    key_ids = (segs[:, None] * states + jnp.arange(states)[None, :]).reshape(-1)
    key_valid = 2 * key_ids < length
    all_states = key_ids.shape[0]

    def heads(array):
        return array.reshape(-1, HEADS, HEAD_DIM)

    q_h, k_h, v_h = heads(queries), heads(keys), heads(values)
    scores = jnp.einsum("qhd,khd->hqk", q_h, k_h, preferred_element_type=F32) * SCALE
    scores = jnp.where(key_valid, scores, -1e30)
    largest = jnp.max(scores, axis=-1, keepdims=True)
    exponent = jnp.exp(scores - largest)
    probs = (exponent / jnp.sum(exponent, axis=-1, keepdims=True)).astype(BF16)
    attended = jnp.einsum("hqk,khd->qhd", probs, v_h, preferred_element_type=F32)
    attended = attended.reshape(rows, width).astype(BF16)
    middle = block_input + mat_t(attended, wout) + bout
    unit2, scale2 = norm_parts(middle)
    normed2 = (unit2 * gain_two + shift_two).astype(BF16)
    hidden_act, hidden_slope = gelu_pair(mat_t(normed2, wfc1) + bfc1)
    hidden_act = hidden_act.astype(BF16)
    hidden_slope = hidden_slope.astype(BF16)
    out_rows = (middle + mat_t(hidden_act, wfc2) + bfc2).astype(BF16)

    def unswapped(array):
        got = xor_swap(pick(array, 1 - mine), "tm", 2)
        own = pick(array, mine)
        return jnp.where(mine == 0, jnp.stack([own, got]), jnp.stack([got, own]))

    out_states = unswapped(out_rows.reshape(2, states, width))

    def chip_sum(full):
        blocks = full.astype(BF16).reshape(y_size, 2, -1, full.shape[1])
        got = xor_swap(pick(blocks, 1 - core, 1), "tm", 1)
        return (pick(blocks, core, 1).astype(F32) + got.astype(F32)).astype(BF16)

    def chip_grad(grad, acts):
        return chip_sum(mat_l(grad, acts))

    cot_float = cot.astype(F32)
    fc2_parts = [chip_grad(cot, hidden_act[:, i : i + width]) for i in range(0, hidden, width)]
    bfc2_grad = jnp.sum(cot_float, axis=0)
    hidden_grad = (mat(cot, wfc2) * hidden_slope.astype(F32)).astype(BF16)
    fc1_part = chip_grad(hidden_grad, normed2)
    bfc1_grad = jnp.sum(hidden_grad.astype(F32), axis=0)
    normed2_grad = mat(hidden_grad, wfc1)
    gain_two_grad = jnp.sum(normed2_grad * unit2, axis=0)
    shift_two_grad = jnp.sum(normed2_grad, axis=0)
    middle_grad = cot_float + norm_back(normed2_grad, unit2, scale2, gain_two)
    branch_grad = middle_grad.astype(BF16)
    out_part = chip_grad(branch_grad, attended)
    bout_grad = jnp.sum(branch_grad.astype(F32), axis=0)

    attended_grad = mat(branch_grad, wout).astype(BF16)
    a_h = heads(attended_grad)
    row_dot = jnp.sum(a_h.astype(F32) * heads(attended).astype(F32), axis=-1)
    probs_grad = jnp.einsum("qhd,khd->hqk", a_h, v_h, preferred_element_type=F32)
    score_grad = (probs.astype(F32) * (probs_grad - row_dot.T[..., None])).astype(BF16)
    queries_grad = jnp.einsum("hqk,khd->qhd", score_grad, k_h, preferred_element_type=F32)
    queries_grad = (queries_grad * SCALE).reshape(rows, width).astype(BF16)
    keys_term = jnp.einsum("hqk,qhd->khd", score_grad, q_h, preferred_element_type=F32) * SCALE
    values_term = jnp.einsum("hqk,qhd->khd", probs, a_h, preferred_element_type=F32)
    terms = jnp.stack(
        [keys_term.reshape(all_states, width), values_term.reshape(all_states, width)]
    ).astype(BF16)
    for mask in reversed(group):
        half = terms.shape[1] // 2
        got = xor_swap(terms[:, half:], "tm", mask)
        terms = (terms[:, :half].astype(F32) + got.astype(F32)).astype(BF16)
    projected_grad = jnp.concatenate([queries_grad, terms[0], terms[1]], axis=1)
    qkv_part = chip_grad(projected_grad, normed1)
    projected_sum = jnp.sum(projected_grad.astype(F32), axis=0)
    normed1_grad = mat(projected_grad, wqkv)
    gain_one_grad = jnp.sum(normed1_grad * unit1, axis=0)
    shift_one_grad = jnp.sum(normed1_grad, axis=0)
    input_grad = middle_grad + norm_back(normed1_grad, unit1, scale1, gain_one)
    state_grad = (input_grad * state_slope).astype(BF16)
    conv2_parts = [
        chip_grad(state_grad, state_taps[:, i : i + width]) for i in range(0, 3 * width, width)
    ]
    b2_grad = jnp.sum(state_grad.astype(F32), axis=0)
    taps_grad = mat(state_grad, w2)
    prev_grad = taps_grad[:, :width].reshape(2, states, width)
    odd_grad = taps_grad[:, 2 * width :].reshape(2, states, width)
    odd_grad = odd_grad + jnp.pad(prev_grad[:, 1:], ((0, 0), (0, 1), (0, 0)))
    edge_grad = jnp.pad(prev_grad[:, :1], ((0, 0), (TILE - 1, 0), (0, 0)))
    odd_grad = jnp.concatenate([odd_grad, edge_grad], axis=1).reshape(2 * size, width)
    odd_grad = (odd_grad * slope_odd).astype(BF16)
    even_grad = (taps_grad[:, width : 2 * width] * slope_even).astype(BF16)
    b1_grad = jnp.sum(even_grad.astype(F32), axis=0) + jnp.sum(odd_grad.astype(F32), axis=0)
    conv1_part = chip_sum(mat_l(even_grad, x_even) + mat_l(odd_grad, x_odd))
    half = conv1_part.shape[1] // 2
    conv1_part = jnp.concatenate([conv1_part[:, :half], conv1_part[:, half:]], axis=2)

    vec_grads = [
        b1_grad, b2_grad, gain_one_grad, shift_one_grad, projected_sum[:width],
        projected_sum[2 * width :], bout_grad, gain_two_grad, shift_two_grad, bfc2_grad,
    ]
    vec_part = jnp.stack([v.reshape(parts, share) for v in vec_grads], axis=1)
    vec_part = jnp.concatenate([vec_part, bfc1_grad.reshape(parts, -1, share)], axis=1)
    vec_part = vec_part.reshape(y_size, 2, vec_count, share)
    got = xor_swap(pick(vec_part, 1 - core, 1), "tm", 1)
    vec_part = (pick(vec_part, core, 1) + got).astype(BF16)
    vec_part = jnp.pad(vec_part, ((0, 0), (0, TILE - vec_count), (0, width - share)))
    pieces = fc2_parts + [fc1_part, out_part, qkv_part] + conv2_parts + [conv1_part, vec_part]
    sizes = [p.shape[1] for p in pieces]
    packed = jnp.concatenate(pieces, axis=1)
    step = TILE * clips
    packed = jnp.pad(packed, ((0, 0), (0, -packed.shape[1] % step), (0, 0)))
    summed = reduce_all(packed, clips)
    ends = [sum(sizes[: i + 1]) for i in range(len(sizes))]
    sums = [summed[e - s : e].astype(F32) for e, s in zip(ends, sizes)]
    fc2_sum = jnp.concatenate([s.T for s in sums[: len(fc2_parts)]], axis=0)
    fc1_sum, out_sum, qkv_sum = sums[len(fc2_parts) : len(fc2_parts) + 3]
    conv2_sum = jnp.stack([s.T for s in sums[-5:-2]])
    conv1_sum = sums[-2]
    conv1_sum = jnp.concatenate([conv1_sum[:, : 3 * LANES], conv1_sum[:, 3 * LANES :]], axis=0)
    conv1_sum = conv1_sum.T.reshape(3, LANES, share)[:, :mels]
    vec_sum = sums[-1][:vec_count, :share]

    even_back = mat(even_grad, w1).reshape(2, states, 3 * LANES)
    even_back = jnp.pad(even_back, ((0, 0), (0, TILE), (0, 0)))
    odd_back = mat(odd_grad, w1).reshape(2, size, 3 * LANES)
    even_mel = even_back[..., LANES : 2 * LANES] + odd_back[..., :LANES]
    even_mel = even_mel + jnp.roll(odd_back[..., 2 * LANES :], 1, axis=1)
    odd_mel = jnp.roll(even_back[..., :LANES], -1, axis=1)
    odd_mel = odd_mel + even_back[..., 2 * LANES :] + odd_back[..., LANES : 2 * LANES]
    mel_back = unswapped(jnp.stack([even_mel[..., :mels], odd_mel[..., :mels]], axis=2))
    from_before = lax.ppermute(mel_back[:, states], "tm", up)
    from_after = lax.ppermute(mel_back[:, size - 1], "tm", down)
    mel_back = mel_back[:, :states].at[:, 0].add(from_before).at[:, -1].add(from_after)
    mel_back = mel_back.reshape(2, frames, mels)
    mel_grad = jnp.where(frame_valid, mel_back, 0.0).astype(BF16)

    return (
        out_states,
        mel_grad,
        conv1_sum,
        vec_sum[0],
        conv2_sum,
        vec_sum[1],
        vec_sum[2],
        vec_sum[3],
        qkv_sum.T,
        vec_sum[4],
        vec_sum[5],
        out_sum.T,
        vec_sum[6],
        vec_sum[7],
        vec_sum[8],
        fc1_sum.T,
        vec_sum[10:].reshape(-1),
        fc2_sum,
        vec_sum[9],
    )


def solution(mesh):
    return jax.shard_map(
        per_device,
        mesh=mesh,
        in_specs=(
            P("clip", "tm", None),
            P("clip"),
            P(None, None, "tm"),
            P("tm"),
            P(None, None, "tm"),
            P("tm"),
            P("tm"),
            P("tm"),
            P(None, "tm"),
            P("tm"),
            P("tm"),
            P(None, "tm"),
            P("tm"),
            P("tm"),
            P("tm"),
            P(None, "tm"),
            P("tm"),
            P(None, "tm"),
            P("tm"),
            P("clip", "tm", None),
        ),
        out_specs=(
            P("clip", "tm", None),
            P("clip", "tm", None),
            P(None, None, "tm"),
            P("tm"),
            P(None, None, "tm"),
            P("tm"),
            P("tm"),
            P("tm"),
            P(None, "tm"),
            P("tm"),
            P("tm"),
            P(None, "tm"),
            P("tm"),
            P("tm"),
            P("tm"),
            P(None, "tm"),
            P("tm"),
            P(None, "tm"),
            P("tm"),
        ),
        check_vma=False,
    )
```

```python
import functools
import math

import jax
import jax.numpy as jnp
import numpy as np
from jax import lax
from jax.experimental import pallas as pl
from jax.experimental.pallas import tpu as pltpu
from jax.sharding import PartitionSpec as P

HEADS = 12
HEAD_DIM = 64
F32 = jnp.float32
BF16 = jnp.bfloat16
SCALE = 1.0 / math.sqrt(HEAD_DIM)
TILE = 16
LANES = 128
MESH = pl.DeviceIdType.MESH
ANY = pl.BlockSpec(memory_space=pl.ANY)
VMEM = pl.BlockSpec(memory_space=pltpu.VMEM)


def xor_swap(array, axis, mask):
    size = lax.axis_size(axis)
    return lax.ppermute(array, axis, [(i, i ^ mask) for i in range(size)])


def pick(array, index, axis=0):
    return lax.dynamic_index_in_dim(array, index, axis=axis, keepdims=False)


def bits_of(size):
    return [1 << b for b in range(size.bit_length() - 1)]


def combos(masks):
    found = [0]
    for mask in masks:
        found = found + [m ^ mask for m in found]
    return found


def flip(index, mask):
    return index + mask * (1 - 2 * ((index // mask) % 2))


def flip_all(index, mask):
    for bit in bits_of(2 * mask) if mask else []:
        if mask & bit:
            index = flip(index, bit)
    return index


def gelu_pair(v):
    a = jnp.abs(v) * (1.0 / math.sqrt(2.0))
    t = 1.0 / (1.0 + 0.3275911 * a)
    poly = t * (
        0.254829592
        + t * (-0.284496736 + t * (1.421413741 + t * (-1.453152027 + t * 1.061405429)))
    )
    bell = jnp.exp(-0.5 * v * v)
    tail = 0.5 * poly * bell
    cdf = jnp.where(v >= 0, 1.0 - tail, tail)
    return v * cdf, cdf + v * bell * (1.0 / math.sqrt(2.0 * math.pi))


def norm_parts(v):
    center = v - jnp.mean(v, axis=-1, keepdims=True)
    spread = jnp.mean(center * center, axis=-1, keepdims=True)
    scale = lax.rsqrt(spread + 1e-05)
    return center * scale, scale


def norm_back(grad, unit, scale, gain):
    a = grad * gain
    mean_a = jnp.mean(a, axis=-1, keepdims=True)
    mean_an = jnp.mean(a * unit, axis=-1, keepdims=True)
    return (a - mean_a - unit * mean_an) * scale


def positions(count, width):
    half = width // 2
    rates = np.exp(-(math.log(10000.0) / (half - 1)) * np.arange(half))
    angles = np.arange(count)[:, None] * rates[None, :]
    return np.concatenate([np.sin(angles), np.cos(angles)], axis=1).astype(np.float32)


def mat(a, b):
    return jnp.dot(a, b, preferred_element_type=F32)


def mat_t(a, b):
    return lax.dot_general(a, b, (((1,), (1,)), ((), ())), preferred_element_type=F32)


def mat_l(a, b):
    return lax.dot_general(a, b, (((0,), (0,)), ((), ())), preferred_element_type=F32)


def aligned(index, step):
    return pl.multiple_of(index * step, step)


class Place:
    def __init__(self):
        self.parts = lax.axis_size("tm")
        self.clips = lax.axis_size("clip")
        self.tm = lax.axis_index("tm")
        self.cl = lax.axis_index("clip")
        self.y_size = self.parts // 2
        self.x_size = self.y_size
        self.z_size = self.clips // self.x_size
        self.core = self.tm % 2
        self.y = self.tm // 2
        self.x = self.cl % self.x_size
        self.z = self.cl // self.x_size

    def tm_partner(self, mask):
        return {"tm": flip(self.tm, mask)}

    def clip_partner(self, mask):
        return {"clip": flip(self.cl, mask)}


def greet(partners):
    barrier = pltpu.get_barrier_semaphore()
    for partner in partners:
        pl.semaphore_signal(barrier, inc=1, device_id=partner, device_id_type=MESH)
    pl.semaphore_wait(barrier, len(partners))


class Gather:
    def __init__(self, at, own, full, first, count, sends, receives, base):
        self.at, self.own, self.full = at, own, full
        self.first, self.count = first, count
        self.shard = own.shape[0]
        self.split = at.x_size if count % (TILE * at.x_size) == 0 else 1
        self.sends, self.receives, self.base = sends, receives, base
        self.used = 0
        self.y_masks = [2 * b for b in bits_of(at.y_size)]
        self.x_masks = bits_of(at.x_size) if self.split > 1 else []
        self.y_copies, self.x_copies, self.core_copies = [], [], []
        self.started = []

    @staticmethod
    def slots(parts, split):
        y_size = parts // 2
        ys = y_size - 1
        xs = ys * (split - 1)
        return ys + xs + 1 + ys * split

    def region(self, mask, part):
        rows = self.count // self.split
        index = flip_all(self.at.tm, mask) * self.shard + self.first
        if part is not None:
            index = index + part * rows
        else:
            rows = self.count
        return pl.ds(pl.multiple_of(index, TILE), rows)

    def send(self, source, region, partner):
        slot = self.base + self.used
        self.used += 1
        copy = pltpu.make_async_remote_copy(
            src_ref=source,
            dst_ref=self.full.at[region],
            send_sem=self.sends.at[slot],
            recv_sem=self.receives.at[slot],
            device_id=partner,
            device_id_type=MESH,
        )
        copy.start()
        self.started.append(copy)
        return copy

    def part(self, mask):
        return flip_all(self.at.x, mask) if self.split > 1 else 0

    def start(self):
        at = self.at
        rows = self.count // self.split
        first = pl.multiple_of(self.first + self.part(0) * rows, TILE)
        self.pending = []
        mask = self.y_masks[0]
        copy = self.send(
            self.own.at[pl.ds(first, rows)], self.region(0, self.part(0)), at.tm_partner(mask)
        )
        self.pending.append((copy, mask))
        whole = self.own.at[pl.ds(self.first, self.count)]
        self.core_copies.append(self.send(whole, self.region(0, None), at.tm_partner(1)))

    def relay(self, mask, part):
        region = self.region(mask, part)
        self.core_copies.append(self.send(self.full.at[region], region, self.at.tm_partner(1)))

    def after_y(self):
        at = self.at
        have = []
        for i, mask in enumerate(self.y_masks):
            for copy, m in self.pending:
                copy.wait_recv()
                have.append(m)
            self.pending = []
            if i + 1 < len(self.y_masks):
                after = self.y_masks[i + 1]
                for m in [0] + have:
                    region = self.region(m, self.part(0))
                    if m == 0:
                        rows = self.count // self.split
                        first = pl.multiple_of(self.first + self.part(0) * rows, TILE)
                        source = self.own.at[pl.ds(first, rows)]
                    else:
                        source = self.full.at[region]
                    copy = self.send(source, region, at.tm_partner(after))
                    self.pending.append((copy, m ^ after))
        self.have = have
        for x_mask in self.x_masks[:1]:
            for m in have:
                region = self.region(m, self.part(0))
                copy = self.send(self.full.at[region], region, at.clip_partner(x_mask))
                self.x_copies.append((copy, m, x_mask))
        for m in have:
            self.relay(m, self.part(0))

    def after_x(self):
        at = self.at
        got = [0]
        for i, x_mask in enumerate(self.x_masks):
            fresh = []
            for copy, m, q in self.x_copies:
                copy.wait_recv()
                self.relay(m, self.part(q))
                if q not in fresh:
                    fresh.append(q)
            got = got + fresh
            self.x_copies = []
            if i + 1 < len(self.x_masks):
                after = self.x_masks[i + 1]
                for m in self.have:
                    for q in got:
                        region = self.region(m, self.part(q))
                        copy = self.send(self.full.at[region], region, at.clip_partner(after))
                        self.x_copies.append((copy, m, q ^ after))

    def finish(self):
        for copy in self.core_copies:
            copy.wait_recv()

    def close(self):
        for copy in self.started:
            copy.wait_send()


def front_kernel(states, mel_in, w1_own, vec_own, w2_own, wqkv_own, wout_own, wfc1_own, pos_in, *refs):
    (
        w1, vec_raw, vecs, w2, wqkv, taps, x_even, x_odd, slope_even, slope_odd,
        slope_state, block_input, normed, queries, keys, values, wout, wfc1,
        mel, odd_act, tmp, pos, sends, receives, kv_send, kv_recv, local,
    ) = refs
    at = Place()
    width = block_input.shape[1]
    rows = 2 * states
    block = 256
    mine = at.y % 2
    partners = [at.tm_partner(m) for m in bits_of(at.parts)]
    partners += [at.clip_partner(m) for m in bits_of(at.x_size)]
    seg = [4 * (at.tm // 4) + 2 * s + at.core for s in range(2)]

    locals_ = [
        pltpu.make_async_copy(mel_in.at[mine], mel.at[mine], local.at[0]),
        pltpu.make_async_copy(w1_own, w1.at[pl.ds(aligned(at.tm, w1_own.shape[0]), w1_own.shape[0])], local.at[1]),
        pltpu.make_async_copy(vec_own, vec_raw.at[pl.ds(aligned(at.tm, TILE), TILE)], local.at[2]),
        pltpu.make_async_copy(w2_own, w2.at[pl.ds(aligned(at.tm, w2_own.shape[0]), w2_own.shape[0])], local.at[3]),
        pltpu.make_async_copy(wqkv_own, wqkv.at[pl.ds(aligned(at.tm, wqkv_own.shape[0]), wqkv_own.shape[0])], local.at[4]),
    ]
    for own, full, sem in ((wout_own, wout, 7), (wfc1_own, wfc1, 8)):
        n = own.shape[0]
        locals_.append(pltpu.make_async_copy(own, full.at[pl.ds(aligned(at.tm, n), n)], local.at[sem]))
    for s in range(2):
        locals_.append(
            pltpu.make_async_copy(
                pos_in.at[pl.ds(aligned(seg[s], states), states)],
                pos.at[pl.ds(s * states, states)],
                local.at[5 + s],
            )
        )
    for copy in locals_:
        copy.start()
    greet(partners)
    swap = pltpu.make_async_remote_copy(
        src_ref=mel_in.at[1 - mine],
        dst_ref=mel.at[mine],
        send_sem=kv_send.at[0],
        recv_sem=kv_recv.at[0],
        device_id=at.tm_partner(2),
        device_id_type=MESH,
    )
    swap.start()
    base = 0
    groups = []
    for own, full, pieces in ((w1_own, w1, 1), (vec_own, vec_raw, 1), (w2_own, w2, 2), (wqkv_own, wqkv, 2), (wout_own, wout, 1), (wfc1_own, wfc1, 2)):
        count = own.shape[0] // pieces if own.shape[0] % (pieces * TILE * at.x_size) == 0 else own.shape[0]
        for first in range(0, own.shape[0], count):
            g = Gather(at, own, full, first, count, sends, receives, base)
            base += Gather.slots(at.parts, g.split)
            groups.append(g)
    small, large = groups[:2], groups[2:]
    second = [g for g in large if g.own is w2_own]
    third = [g for g in large if g.own is wqkv_own]
    fourth = [g for g in large if g.own is wout_own or g.own is wfc1_own]
    for g in small + second:
        g.start()
    swap.wait_recv()
    locals_[0].wait()
    for s in range(2):
        m = mel[s].astype(F32)
        size = m.shape[0]
        before = pltpu.roll(m, 1, 0)
        after = pltpu.roll(m, size - 1, 0)
        low, high = pl.ds(0, LANES), pl.ds(LANES, LANES)
        even_rows = pl.ds(s * states, states)
        odd_rows = pl.ds(s * size, size)
        x_even[even_rows, low] = before[:states, LANES:].astype(BF16)
        x_even[even_rows, pl.ds(LANES, 2 * LANES)] = m[:states].astype(BF16)
        x_odd[odd_rows, pl.ds(0, 2 * LANES)] = m.astype(BF16)
        x_odd[odd_rows, pl.ds(2 * LANES, LANES)] = after[:, :LANES].astype(BF16)
    for g in small:
        g.after_y()
    for g in second:
        g.after_y()
    for g in third:
        g.start()
    for g in small:
        g.after_x()
        g.finish()
    locals_[1].wait()
    locals_[2].wait()
    total = jnp.zeros(vecs.shape, F32)
    share = width // at.parts
    for j in range(at.parts):
        piece = vec_raw[pl.ds(j * TILE, TILE)].astype(F32)
        low = (j * share) // LANES * LANES
        cells = [piece]
        if low > 0:
            cells = [jnp.zeros((TILE, low), F32)] + cells
        if width - low - piece.shape[1] > 0:
            cells = cells + [jnp.zeros((TILE, width - low - piece.shape[1]), F32)]
        placed = jnp.concatenate(cells, axis=1)
        shift = j * share - low
        total = total + (pltpu.roll(placed, shift, 1) if shift else placed)
    vecs[...] = total

    def vec(i, cols):
        return vecs[pl.ds(i, 1), cols]

    size = states + TILE
    for s in range(2):

        def odd_columns(j, carry, s=s):
            cols = pl.ds(aligned(j, block), block)
            tmp[pl.ds(0, size)] = mat_t(x_odd[pl.ds(s * size, size)], w1[cols])

            def odd_rows(i, carry):
                r = pl.ds(aligned(i, 64), 64)
                act, slope = gelu_pair(tmp[r] + vec(0, cols))
                odd_act[r, cols] = act
                taps[pl.ds(aligned(i, 64) + s * states, 64), pl.ds(2 * width + aligned(j, block), block)] = act.astype(BF16)
                slope_odd[pl.ds(aligned(i, 64) + s * size, 64), cols] = slope.astype(BF16)
                return carry

            lax.fori_loop(0, states // 64, odd_rows, 0)
            r = pl.ds(states, TILE)
            act, slope = gelu_pair(tmp[r] + vec(0, cols))
            last = lax.broadcasted_iota(jnp.int32, act.shape, 0) == TILE - 1
            first = jnp.minimum(seg[s], 1).astype(F32)
            act = jnp.where(last, act * first, 0.0)
            slope = jnp.where(last, slope * first, 0.0)
            odd_act[r, cols] = act
            slope_odd[pl.ds(s * size + states, TILE), cols] = slope.astype(BF16)
            moved = pltpu.roll(odd_act[:, cols], 1, 0)
            taps[pl.ds(s * states, states), cols] = moved[:states].astype(BF16)
            return carry

        lax.fori_loop(0, width // block, odd_columns, 0)

        def even_columns(j, carry, s=s):
            cols = pl.ds(aligned(j, block), block)
            tmp[pl.ds(0, states)] = mat_t(x_even[pl.ds(s * states, states)], w1[cols])

            def even_rows(i, carry):
                r = pl.ds(aligned(i, 64), 64)
                act, slope = gelu_pair(tmp[r] + vec(0, cols))
                out = pl.ds(aligned(i, 64) + s * states, 64)
                taps[out, pl.ds(width + aligned(j, block), block)] = act.astype(BF16)
                slope_even[out, cols] = slope.astype(BF16)
                return carry

            lax.fori_loop(0, states // 64, even_rows, 0)
            return carry

        lax.fori_loop(0, width // block, even_columns, 0)

    for g in second:
        g.after_x()
    for g in third:
        g.after_y()
    for g in fourth:
        g.start()
    for g in second:
        g.finish()
    locals_[3].wait()
    locals_[7].wait()
    locals_[8].wait()

    def state_columns(j, carry):
        cols = pl.ds(aligned(j, block), block)
        tmp[pl.ds(0, rows)] = mat_t(taps[...], w2[cols])

        def state_rows(i, carry):
            r = pl.ds(aligned(i, 64), 64)
            act, slope = gelu_pair(tmp[r] + vec(1, cols))
            block_input[r, cols] = act + pos[r, cols]
            slope_state[r, cols] = slope.astype(BF16)
            return carry

        lax.fori_loop(0, rows // 64, state_rows, 0)
        return carry

    lax.fori_loop(0, width // block, state_columns, 0)
    for g in third:
        g.after_x()
    full = pl.ds(0, width)

    def norm_rows(i, carry):
        r = pl.ds(aligned(i, 32), 32)
        unit, _ = norm_parts(block_input[r])
        normed[r] = (unit * vec(2, full) + vec(3, full)).astype(BF16)
        return carry

    lax.fori_loop(0, rows // 32, norm_rows, 0)
    for g in third:
        g.finish()
    locals_[4].wait()
    group = [m for m in bits_of(at.parts) if m != 2]

    def exchange(array, base):
        held = rows
        for n, mask in enumerate(group):
            copy = pltpu.make_async_remote_copy(
                src_ref=array.at[pl.ds(0, held)],
                dst_ref=array.at[pl.ds(held, held)],
                send_sem=kv_send.at[base + n],
                recv_sem=kv_recv.at[base + n],
                device_id=at.tm_partner(mask),
                device_id_type=MESH,
            )
            copy.start()
            if n + 1 < len(group):
                copy.wait()
                held = 2 * held
            else:
                return copy

    def project(target, first, bias):
        def columns(j, carry):
            cols = pl.ds(aligned(j, block), block)
            part = mat_t(normed[...], wqkv[pl.ds(first + aligned(j, block), block)])
            if bias is not None:
                part = part + vec(bias, cols)
            target[pl.ds(0, rows), cols] = part.astype(BF16)
            return carry

        lax.fori_loop(0, width // block, columns, 0)

    project(keys, width, None)
    key_copy = exchange(keys, 1)
    for g in fourth:
        g.after_y()
    project(values, 2 * width, 5)
    value_copy = exchange(values, 1 + len(group))
    project(queries, 0, 4)
    for g in fourth:
        g.after_x()
    key_copy.wait()
    value_copy.wait()
    for g in fourth:
        g.finish()
    locals_[5].wait()
    locals_[6].wait()
    swap.wait_send()
    for g in groups:
        g.close()


def front(mel, w1_own, vec_own, w2_own, wqkv_own, wout_own, wfc1_own, pos, parts, x_size):
    states = mel.shape[1] - TILE
    rows, width = 2 * states, pos.shape[1]
    every = 2 * pos.shape[0] // 2
    shapes = [
        ((parts * w1_own.shape[0], w1_own.shape[1]), BF16),
        ((parts * TILE, vec_own.shape[1]), BF16),
        ((TILE, width), F32),
        ((parts * w2_own.shape[0], w2_own.shape[1]), BF16),
        ((parts * wqkv_own.shape[0], wqkv_own.shape[1]), BF16),
        ((rows, 3 * width), BF16),
        ((rows, 3 * LANES), BF16),
        ((rows + 2 * TILE, 3 * LANES), BF16),
        ((rows, width), BF16),
        ((rows + 2 * TILE, width), BF16),
        ((rows, width), BF16),
        ((rows, width), F32),
        ((rows, width), BF16),
        ((rows, width), BF16),
        ((every, width), BF16),
        ((every, width), BF16),
        ((parts * wout_own.shape[0], width), BF16),
        ((parts * wfc1_own.shape[0], width), BF16),
    ]
    slots = 9 * Gather.slots(parts, x_size)
    return pl.pallas_call(
        functools.partial(front_kernel, states),
        out_shape=[jax.ShapeDtypeStruct(s, d) for s, d in shapes],
        in_specs=[VMEM] * 7 + [ANY],
        out_specs=[VMEM] * len(shapes),
        scratch_shapes=[
            pltpu.VMEM(mel.shape, BF16),
            pltpu.VMEM((states + TILE, width), F32),
            pltpu.VMEM((max(rows, states + TILE), 256), F32),
            pltpu.VMEM((rows, width), F32),
            pltpu.SemaphoreType.DMA((slots,)),
            pltpu.SemaphoreType.DMA((slots,)),
            pltpu.SemaphoreType.DMA((8,)),
            pltpu.SemaphoreType.DMA((8,)),
            pltpu.SemaphoreType.DMA((9,)),
        ],
        compiler_params=pltpu.CompilerParams(
            collective_id=1, has_side_effects=True, vmem_limit_bytes=60 << 20
        ),
        name="front",
    )(mel, w1_own, vec_own, w2_own, wqkv_own, wout_own, wfc1_own, pos)


def attention_kernel(q, k, v, bias, w_own, *refs):
    attended, inverse, w_full, expo, buffer, expo_sem, sends, receives, local = refs
    at = Place()
    rows = q.shape[0]
    pairs = q.shape[1] // LANES
    n = w_own.shape[0]
    keep = pltpu.make_async_copy(w_own, w_full.at[pl.ds(aligned(at.tm, n), n)], local.at[0])
    keep.start()
    greet(
        [at.tm_partner(m) for m in bits_of(at.parts)]
        + [at.clip_partner(m) for m in bits_of(at.x_size)]
    )
    groups, base = [], 0
    count = n // 2 if n % (2 * TILE * at.x_size) == 0 else n
    for first in range(0, n, count):
        groups.append(Gather(at, w_own, w_full, first, count, sends, receives, base))
        base += Gather.slots(at.parts, groups[-1].split)
    for g in groups:
        g.start()
    inverse[...] = jnp.zeros(inverse.shape, F32)
    lane = lax.broadcasted_iota(jnp.int32, (rows, LANES), 1)

    def out_copy(p, h):
        return pltpu.make_async_copy(buffer.at[h], expo.at[2 * p + h], expo_sem.at[h])

    def pair_body(p, carry):
        cols = pl.ds(aligned(p, LANES), LANES)
        for h in range(2):

            @pl.when(p > 0)
            def _(h=h):
                out_copy(p - 1, h).wait()

        scaled = q[:, cols].astype(F32) * SCALE
        inv = inverse[...]
        outs = []
        scores = []
        for h in range(2):
            own = (lane < HEAD_DIM) if h == 0 else (lane >= HEAD_DIM)
            head = jnp.where(own, scaled, 0.0).astype(BF16)
            scores.append(mat_t(head, k[:, cols]) + bias[pl.ds(0, 1)])
        for h in range(2):
            largest = jnp.max(scores[h], axis=-1, keepdims=True)
            exponent = jnp.exp(scores[h] - largest)
            one = 1.0 / jnp.sum(exponent, axis=-1, keepdims=True)
            low = exponent.astype(BF16)
            buffer[h] = low
            outs.append(mat(low, v[:, cols]) * one)
            inv = jnp.where(lane == 2 * p + h, one, inv)
        attended[:, cols] = jnp.where(lane < HEAD_DIM, outs[0], outs[1]).astype(BF16)
        inverse[...] = inv
        for h in range(2):
            out_copy(p, h).start()
        return carry

    third = pairs // 3
    lax.fori_loop(0, third, pair_body, 0)
    groups[0].after_y()
    lax.fori_loop(third, 2 * third, pair_body, 0)
    for g in groups[1:]:
        g.after_y()
    groups[0].after_x()
    lax.fori_loop(2 * third, pairs, pair_body, 0)
    for g in groups[1:]:
        g.after_x()
    for h in range(2):
        out_copy(pairs - 1, h).wait()
    keep.wait()
    for g in groups:
        g.finish()
        g.close()


def attention(q, k, v, bias, w_own, parts, x_size):
    rows, width = q.shape
    every = k.shape[0]
    slots = 2 * Gather.slots(parts, x_size)
    return pl.pallas_call(
        attention_kernel,
        out_shape=[
            jax.ShapeDtypeStruct((rows, width), BF16),
            jax.ShapeDtypeStruct((rows, LANES), F32),
            jax.ShapeDtypeStruct((parts * w_own.shape[0], w_own.shape[1]), BF16),
            jax.ShapeDtypeStruct((width // HEAD_DIM, rows, every), BF16),
        ],
        in_specs=[VMEM] * 5,
        out_specs=[VMEM] * 3 + [ANY],
        scratch_shapes=[
            pltpu.VMEM((2, rows, every), BF16),
            pltpu.SemaphoreType.DMA((2,)),
            pltpu.SemaphoreType.DMA((slots,)),
            pltpu.SemaphoreType.DMA((slots,)),
            pltpu.SemaphoreType.DMA((1,)),
        ],
        compiler_params=pltpu.CompilerParams(
            collective_id=2, has_side_effects=True, vmem_limit_bytes=60 << 20
        ),
        name="attention",
    )(q, k, v, bias, w_own)


class Reducer:
    def __init__(self, at, rows, ahead, held, result, landings, sends, receives):
        self.at, self.rows, self.ahead = at, rows, ahead
        self.source, self.result, self.landings = held, result, landings
        self.sends, self.receives = sends, receives
        self.chunks = result.shape[0] // rows
        self.y_bits = list(reversed(bits_of(at.y_size)))
        plane = [(at.x, b, b) for b in bits_of(at.x_size)]
        plane += [(at.z, b, b * at.x_size) for b in bits_of(at.z_size)]
        self.mine = [(place // b) % 2 for place, b, _ in plane]
        self.partner = [at.clip_partner(mask) for _, _, mask in plane]
        self.y_partner = [at.tm_partner(2 * b) for b in self.y_bits]
        self.tops, self.depth = len(self.y_bits), len(plane)
        self.stages = 1 + self.tops + 2 * self.depth
        self.delays = [0] + [ahead + s for s in range(self.stages - 1)]
        self.times = self.chunks + self.delays[-1]

    @staticmethod
    def scratch(y_size, plane, chunks, rows, width):
        shapes = [pltpu.VMEM((chunks, b, rows, width), BF16) for b in reversed(bits_of(y_size))]
        shapes += [pltpu.VMEM((chunks, rows >> (k + 1), width), BF16) for k in range(plane)]
        slots = len(bits_of(y_size)) + 2 * plane
        return shapes + [pltpu.SemaphoreType.DMA((chunks, slots))] * 2

    def remote(self, src, dst, c, slot, device):
        return pltpu.make_async_remote_copy(
            src_ref=src,
            dst_ref=dst,
            send_sem=self.sends.at[c, slot],
            recv_sem=self.receives.at[c, slot],
            device_id=device,
            device_id_type=MESH,
        )

    def chunk(self, c):
        return pl.ds(pl.multiple_of(c * self.rows, self.rows), self.rows)

    def y_copy(self, c, k):
        b = self.y_bits[k]
        away = b * (1 - (self.at.y // b) % 2)
        if k == 0:
            src = self.source.at[pl.ds(away, b), self.chunk(c)]
        else:
            src = self.landings[k - 1].at[c, pl.ds(away, b)]
        return self.remote(src, self.landings[k].at[c], c, k, self.y_partner[k])

    def half(self, k, bit):
        count = self.rows >> (k + 1)
        return pl.ds(aligned(bit, count), count)

    def current(self, k, c, region):
        if k == 0:
            return self.landings[self.tops - 1].at[c, 0, region]
        return self.landings[self.tops + k - 1].at[c, region]

    def spread(self, c, k):
        src = self.current(k, c, self.half(k, 1 - self.mine[k]))
        dst = self.landings[self.tops + k].at[c]
        return self.remote(src, dst, c, self.tops + k, self.partner[k])

    def kept(self, c, k):
        first = c * self.rows
        for i in range(k + 1):
            first = first + self.mine[i] * (self.rows >> (i + 1))
        count = self.rows >> (k + 1)
        return pl.ds(pl.multiple_of(first, count), count)

    def collect(self, c, k):
        region = self.result.at[self.kept(c, k)]
        src = self.landings[self.tops + k].at[c] if k == self.depth - 1 else region
        return self.remote(src, region, c, self.tops + self.depth + k, self.partner[k])

    def keep(self, c):
        k = self.depth - 1
        return pltpu.make_async_copy(
            self.landings[self.tops + k].at[c], self.result.at[self.kept(c, k)], self.local.at[c]
        )

    def run(self, stage, c):
        if stage == 0:
            self.y_copy(c, 0).start()
        elif stage <= self.tops:
            k = stage - 1
            b = self.y_bits[k]
            own = pl.ds(b * ((self.at.y // b) % 2), b)
            self.y_copy(c, k).wait_recv()
            mine = self.source[own, self.chunk(c)] if k == 0 else self.landings[k - 1][c, own]
            total = mine.astype(F32) + self.landings[k][c].astype(F32)
            self.landings[k][c] = total.astype(BF16)
            if k + 1 < self.tops:
                self.y_copy(c, k + 1).start()
            else:
                self.spread(c, 0).start()
        elif stage <= self.tops + self.depth:
            k = stage - self.tops - 1
            self.spread(c, k).wait_recv()
            mine = self.current(k, c, self.half(k, self.mine[k]))[...]
            total = mine.astype(F32) + self.landings[self.tops + k][c].astype(F32)
            self.landings[self.tops + k][c] = total.astype(BF16)
            if k + 1 < self.depth:
                self.spread(c, k + 1).start()
            else:
                self.collect(c, k).start()
                self.keep(c).start()
        else:
            k = self.depth - 1 - (stage - self.tops - self.depth - 1)
            self.collect(c, k).wait_recv()
            if k == self.depth - 1:
                self.keep(c).wait()
            if k > 0:
                self.collect(c, k - 1).start()

    def step(self, time):
        for stage in range(self.stages):
            c = time - self.delays[stage]

            @pl.when((c >= 0) & (c < self.chunks))
            def _(stage=stage, c=c):
                self.run(stage, c)

    def steps(self, first, last):
        def body(time, carry):
            self.step(time)
            return carry

        lax.fori_loop(first, last, body, 0)

    def close(self):
        def body(c, carry):
            for k in range(self.tops):
                self.y_copy(c, k).wait_send()
            for k in range(self.depth):
                self.spread(c, k).wait_send()
                self.collect(c, k).wait_send()
            return carry

        lax.fori_loop(0, self.chunks, body, 0)


def tile_of(count):
    return max(t for t in range(TILE, 257, TILE) if count % t == 0)


def back_plan(parts, clips, width, hidden):
    share = width // parts
    plane = len(bits_of(parts // 2)) + len(bits_of(clips // (parts // 2)))
    rows = TILE << plane
    plan, first = {}, 0
    early = [("fc2", hidden // parts), ("fc1", hidden // parts), ("out", share)]
    late = [("qkv", 3 * share), ("conv2", 3 * share), ("conv1", share // 2), ("vec", TILE)]
    for group in (early, late):
        for name, count in group:
            plan[name] = (first, count)
            first += count
        plan["gap%d" % len(plan)] = (first, -first % rows)
        first += -first % rows
    plan["last"] = plan["end"] = (first, 0)
    return plan, plane, rows, first


def back_kernel(plan, rows, *refs):
    (
        hid_in, hid_gt_in, cot_t_in, normed2_in, branch_t_in, attended_in, att_grad_in, q_in, k_in,
        v_in, inv_in, expo, wqkv_in, w2_in, w1_in, normed1_in, block_input_in, middle_in,
        slope_state_in, slope_even_in, slope_odd_in, taps_in, x_even_in, x_odd_in, vec_in, vecs_in,
        result, mel_out,
        held, stage, arena, w2, w1, g_t, cot_t, branch_t, normed2, attended, att_grad, q, kv, inv,
        normed1, block_input, middle, slope_odd, x_even, x_odd, vec, vec_got, vecs,
        ebuf, score_grad, q_t, k_t, v_t, kv_land, q_grad, state_grad, prev, even_grad, odd_grad,
        conv1_t, mel_v,
        core_send, core_recv, kv_send, kv_recv, load_sem, expo_sem, local,
    ) = refs[: 28 + 43]
    *landings, sends, receives = refs[28 + 43 :]
    at = Place()
    width = q.shape[1]
    count = q.shape[0]
    states = count // 2
    size = states + TILE
    every = k_in.shape[0]
    hidden = hid_in.shape[1]
    share = width // at.parts
    core, mine = at.core, at.y % 2
    core_partner = at.tm_partner(1)

    loads = {}

    def load(name, src, dst):
        copy = pltpu.make_async_copy(src, dst, load_sem.at[len(loads)])
        copy.start()
        loads[name] = copy

    def need(*names):
        for name in names:
            loads[name].wait()

    blocks = hidden // width
    for i in range(blocks):
        load("hid%d" % i, hid_in.at[:, pl.ds(i * width, width)], arena.at[pl.ds(i * count, count)])
    load("cot", cot_t_in, cot_t)
    load("hid_gt", hid_gt_in, g_t)
    load("normed2", normed2_in, normed2)
    load("branch", branch_t_in, branch_t)
    load("attended", attended_in, attended)
    load("q", q_in, q)
    load("att_grad", att_grad_in, att_grad)
    load("inv", inv_in, inv)
    load("k", k_in, kv.at[pl.ds(0, every)])
    load("v", v_in, kv.at[pl.ds(every, every)])
    load("normed1", normed1_in, normed1)
    load("block_input", block_input_in, block_input)
    load("middle", middle_in, middle)
    load("w2", w2_in, w2)
    load("w1", w1_in, w1)
    load("slope_odd", slope_odd_in, slope_odd)
    load("x_even", x_even_in, x_even)
    load("x_odd", x_odd_in, x_odd)
    load("vec", vec_in, vec)
    load("vecs", vecs_in, vecs)

    def fetch(n, slot):
        return pltpu.make_async_copy(expo.at[n], ebuf.at[slot], expo_sem.at[slot])

    fetch(0, 0).start()
    reducer = Reducer(at, rows, 3, held, result, landings, sends, receives)
    reducer.local = local
    greet([core_partner] + reducer.y_partner + reducer.partner)
    done = [0]

    def advance(steps, ready):
        last = max(done[0], min(done[0] + steps, plan[ready][0] // rows))
        if ready == "end":
            last = reducer.times
        reducer.steps(done[0], last)
        done[0] = last
    for name, (first, n) in plan.items():
        if name.startswith("gap") and n:
            for y in range(at.y_size):
                held[y, pl.ds(first, n)] = jnp.zeros((n, width), BF16)

    copies = {}
    slots = {}
    ring = [None] * stage.shape[0]
    turn = [0]

    def give(name, first, parts):
        for y in range(at.y_size):
            slot = turn[0] % len(ring)
            turn[0] += 1
            if ring[slot] is not None:
                ring[slot].wait_send()
            offset = 0
            for n, rows_of, acts in parts:
                tile = tile_of(n)
                for i in range(n // tile):
                    g = rows_of(2 * y + 1 - core, i * tile, tile)
                    stage[slot, pl.ds(offset + i * tile, tile)] = mat(g, acts()).astype(BF16)
                offset += n
            number = len(copies)
            copy = pltpu.make_async_remote_copy(
                src_ref=stage.at[slot, pl.ds(0, offset)],
                dst_ref=held.at[y, pl.ds(first, offset)],
                send_sem=core_send.at[number],
                recv_sem=core_recv.at[number],
                device_id=core_partner,
                device_id_type=MESH,
            )
            copy.start()
            ring[slot] = copy
            copies[name, y] = copy

    def take(name, first, parts):
        for y in range(at.y_size):
            copies[name, y].wait_recv()
            offset = first
            for n, rows_of, acts in parts:
                tile = tile_of(n)
                for i in range(n // tile):
                    g = rows_of(2 * y + core, i * tile, tile)
                    place = pl.ds(offset + i * tile, tile)
                    total = mat(g, acts()) + held[y, place].astype(F32)
                    held[y, place] = total.astype(BF16)
                offset += n

    def rows_from(ref, base, n):
        def rows_of(part, offset, tile):
            return ref[pl.ds(pl.multiple_of(base + part * n + offset, TILE), tile)]

        return rows_of

    def whole(ref):
        return lambda: ref[...]

    def block_of(ref, i, n):
        return lambda: ref[pl.ds(i * n, n)]

    fc2 = [(share, rows_from(cot_t, 0, share), block_of(arena, i, count)) for i in range(blocks)]
    fc1 = [(hidden // at.parts, rows_from(g_t, 0, hidden // at.parts), whole(normed2))]
    out = [(share, rows_from(branch_t, 0, share), whole(attended))]
    need("cot", *["hid%d" % i for i in range(blocks)])
    give("fc2", plan["fc2"][0], fc2)
    need("hid_gt", "normed2")
    give("fc1", plan["fc1"][0], fc1)
    need("branch", "attended")
    give("out", plan["out"][0], out)
    take("fc2", plan["fc2"][0], fc2)
    advance(3, "fc1")
    take("fc1", plan["fc1"][0], fc1)
    take("out", plan["out"][0], out)
    load("slope_even", slope_even_in, normed2)
    load("wqkv", wqkv_in, arena.at[pl.ds(0, wqkv_in.shape[0])])
    need("q", "att_grad", "inv", "k", "v")

    pairs = width // LANES
    lane = lax.broadcasted_iota(jnp.int32, (count, LANES), 1)

    def pair_body(p, carry):
        cols = pl.ds(aligned(p, LANES), LANES)
        q_t[...] = jnp.transpose(q[:, cols].astype(F32)).astype(BF16)
        grads = []
        for h in range(2):
            n = 2 * p + h
            if h == 0:
                fetch(n + 1, 1).start()
            else:

                @pl.when(p < pairs - 1)
                def _(n=n):
                    fetch(n + 1, 0).start()

            fetch(n, h).wait()
            scale = jnp.sum(jnp.where(lane == n, inv[...], 0.0), axis=-1, keepdims=True)
            keep = (lane < HEAD_DIM) if h == 0 else (lane >= HEAD_DIM)
            grad = jnp.where(keep, att_grad[:, cols].astype(F32) * scale, 0.0).astype(BF16)
            wide = grad.astype(F32)
            dot = jnp.sum(wide * attended[:, cols].astype(F32), axis=-1, keepdims=True)
            grad_t = jnp.transpose(wide).astype(BF16)[HEAD_DIM * h : HEAD_DIM * (h + 1)]
            head = pl.ds(pl.multiple_of(p * LANES + h * HEAD_DIM, HEAD_DIM), HEAD_DIM)
            v_t[head, :] = mat(grad_t, ebuf[h]).astype(BF16)
            diff = mat_t(grad, kv[pl.ds(every, every), cols]) - dot
            score_grad[...] = (ebuf[h].astype(F32) * diff).astype(BF16)
            grads.append(mat(score_grad[...], kv[pl.ds(0, every), cols]) * SCALE)
            part = q_t[pl.ds(HEAD_DIM * h, HEAD_DIM)]
            k_t[head, :] = (mat(part, score_grad[...]) * SCALE).astype(BF16)
        q_grad[:, cols] = jnp.where(lane < HEAD_DIM, grads[0], grads[1]).astype(BF16)

        @pl.when(p < most)
        def _():
            reducer.step(done[0] + p)

        return carry

    most = min(pairs, plan["qkv"][0] // rows - done[0])
    lax.fori_loop(0, pairs, pair_body, 0)
    done[0] += most

    for i in range(3):
        load("taps%d" % i, taps_in.at[:, pl.ds(i * width, width)], kv.at[pl.ds(i * count, count)])
    load("slope_state", slope_state_in, kv.at[pl.ds(3 * count, count)])
    group = [m for m in bits_of(at.parts) if m != 2]
    held_cols = every
    first = 0
    for number, mask in enumerate(reversed(group)):
        held_cols = held_cols // 2
        sent = []
        for i, ref in enumerate((k_t, v_t)):
            copy = pltpu.make_async_remote_copy(
                src_ref=ref.at[:, pl.ds(held_cols, held_cols)],
                dst_ref=kv_land.at[i, :, pl.ds(first, held_cols)],
                send_sem=kv_send.at[number, i],
                recv_sem=kv_recv.at[number, i],
                device_id=at.tm_partner(mask),
                device_id_type=MESH,
            )
            copy.start()
            sent.append(copy)
        if number == 0:
            g_t[pl.ds(0, width)] = jnp.transpose(q_grad[...].astype(F32)).astype(BF16)
            advance(1, "qkv")
        for i, (ref, copy) in enumerate(zip((k_t, v_t), sent)):
            copy.wait()
            low = pl.ds(0, held_cols)
            total = ref[:, low].astype(F32) + kv_land[i, :, pl.ds(first, held_cols)].astype(F32)
            ref[:, low] = total.astype(BF16)
        first += held_cols
    own = pl.ds(0, count)
    for i, (ref, target) in enumerate(((k_t, q), (v_t, att_grad))):
        part = ref[:, own]
        g_t[pl.ds((i + 1) * width, width)] = part
        target[...] = jnp.transpose(part.astype(F32)).astype(BF16)
    need("normed1", "vec")
    vec[pl.ds(4, 1)] = jnp.sum(q_grad[...].astype(F32), axis=0, keepdims=True)
    vec[pl.ds(5, 1)] = jnp.sum(att_grad[...].astype(F32), axis=0, keepdims=True)
    qkv = [(3 * share, rows_from(g_t, 0, 3 * share), whole(normed1))]
    give("qkv", plan["qkv"][0], qkv)
    advance(1, "qkv")
    need("wqkv", "block_input", "middle", "slope_state", "vecs")

    tile = 128
    vec[pl.ds(2, 2)] = jnp.zeros((2, width), F32)

    def norm_rows(i, carry):
        r = pl.ds(aligned(i, tile), tile)
        grad = mat(q_grad[r], arena[pl.ds(0, width)])
        grad = grad + mat(q[r], arena[pl.ds(width, width)])
        grad = grad + mat(att_grad[r], arena[pl.ds(2 * width, width)])
        unit, scale = norm_parts(block_input[r])
        vec[pl.ds(2, 1)] += jnp.sum(grad * unit, axis=0, keepdims=True)
        vec[pl.ds(3, 1)] += jnp.sum(grad, axis=0, keepdims=True)
        total = middle[r] + norm_back(grad, unit, scale, vecs[pl.ds(2, 1)])
        slope = kv[pl.ds(aligned(i, tile) + 3 * count, tile)].astype(F32)
        state_grad[r] = (total * slope).astype(BF16)
        return carry

    lax.fori_loop(0, count // tile, norm_rows, 0)
    vec[pl.ds(1, 1)] = jnp.sum(state_grad[...].astype(F32), axis=0, keepdims=True)
    take("qkv", plan["qkv"][0], qkv)
    advance(1, "conv2")
    cot_t[...] = jnp.transpose(state_grad[...].astype(F32)).astype(BF16)
    need("taps0", "taps1", "taps2")
    conv2 = [(share, rows_from(cot_t, 0, share), block_of(kv, i, count)) for i in range(3)]
    give("conv2", plan["conv2"][0], conv2)
    advance(1, "conv2")
    need("w2", "w1", "slope_even", "slope_odd")
    prev[...] = mat(state_grad[...], w2[:, pl.ds(0, width)])
    for s in range(2):
        r = pl.ds(s * states, states)
        even = mat(state_grad[r], w2[:, pl.ds(width, width)])
        even_grad[r] = (even * normed2[r].astype(F32)).astype(BF16)
        odd = mat(state_grad[r], w2[:, pl.ds(2 * width, width)])
        place = lax.broadcasted_iota(jnp.int32, (states, width), 0)
        moved = pltpu.roll(prev[r], states - 1, 0)
        odd = odd + jnp.where(place < states - 1, moved, 0.0)
        r_odd = pl.ds(s * size, states)
        odd_grad[r_odd] = (odd * slope_odd[r_odd].astype(F32)).astype(BF16)
        r_edge = pl.ds(s * size + states, TILE)
        edge = jnp.broadcast_to(prev[pl.ds(s * states, 1)], (TILE, width))
        odd_grad[r_edge] = (edge * slope_odd[r_edge].astype(F32)).astype(BF16)
    take("conv2", plan["conv2"][0], conv2)
    advance(1, "conv1")
    need("x_even", "x_odd")
    vec[pl.ds(0, 1)] = jnp.sum(even_grad[...].astype(F32), axis=0, keepdims=True) + jnp.sum(
        odd_grad[...].astype(F32), axis=0, keepdims=True
    )
    vec_copy = pltpu.make_async_remote_copy(
        src_ref=vec,
        dst_ref=vec_got,
        send_sem=core_send.at[len(copies)],
        recv_sem=core_recv.at[len(copies)],
        device_id=core_partner,
        device_id_type=MESH,
    )
    vec_copy.start()
    conv1 = mat_l(even_grad[...], x_even[...]) + mat_l(odd_grad[...], x_odd[...])
    conv1_t[...] = conv1.astype(BF16)
    cols = conv1.shape[1]
    half = share // 2
    ring_slot = turn[0] % len(ring)
    if ring[ring_slot] is not None:
        ring[ring_slot].wait_send()
    conv1_copies = []
    first = plan["conv1"][0]

    def conv1_rows(part):
        low = conv1_t[pl.ds(pl.multiple_of(part * share, TILE), half)]
        high = conv1_t[pl.ds(pl.multiple_of(part * share + half, TILE), half)]
        return jnp.concatenate([low, high], axis=1)

    for y in range(at.y_size):
        stage[ring_slot, pl.ds(y * half, half)] = conv1_rows(2 * y + 1 - core)
        number = len(copies) + 1 + y
        copy = pltpu.make_async_remote_copy(
            src_ref=stage.at[ring_slot, pl.ds(y * half, half)],
            dst_ref=held.at[y, pl.ds(first, half)],
            send_sem=core_send.at[number],
            recv_sem=core_recv.at[number],
            device_id=core_partner,
            device_id_type=MESH,
        )
        copy.start()
        conv1_copies.append(copy)
    for y, copy in enumerate(conv1_copies):
        copy.wait_recv()
        place = pl.ds(first, half)
        total = conv1_rows(2 * y + core).astype(F32) + held[y, place].astype(F32)
        held[y, place] = total.astype(BF16)
    vec_copy.wait()
    total = (vec[...] + vec_got[...]).astype(BF16)
    for y in range(at.y_size):
        held[y, pl.ds(plan["vec"][0], TILE)] = total
    advance(1, "last")
    for s in range(2):
        even = mat(even_grad[pl.ds(s * states, states)], w1[...])
        even = jnp.concatenate([even, jnp.zeros((TILE, cols), F32)], axis=0)
        odd = mat(odd_grad[pl.ds(s * size, size)], w1[...])
        one, two, three = [slice(i * LANES, (i + 1) * LANES) for i in range(3)]
        mel_v[s, :, one] = even[:, two] + odd[:, one] + pltpu.roll(odd[:, three], 1, 0)
        mel_v[s, :, two] = pltpu.roll(even[:, one], size - 1, 0) + even[:, three] + odd[:, two]
    swap = pltpu.make_async_remote_copy(
        src_ref=mel_v.at[1 - mine],
        dst_ref=mel_out.at[mine],
        send_sem=kv_send.at[len(group), 0],
        recv_sem=kv_recv.at[len(group), 0],
        device_id=at.tm_partner(2),
        device_id_type=MESH,
    )
    swap.start()
    keep_mel = pltpu.make_async_copy(mel_v.at[mine], mel_out.at[mine], load_sem.at[len(loads)])
    keep_mel.start()
    advance(0, "end")
    for copy in ring:
        if copy is not None and copy is not ring[ring_slot]:
            copy.wait_send()
    for copy in conv1_copies:
        copy.wait_send()
    swap.wait()
    keep_mel.wait()
    reducer.close()


def back(operands, parts, clips):
    (
        hid, hid_gt, cot_t, normed2, branch_t, attended, att_grad, q, k, v, inv, expo, wqkv, w2, w1,
        normed1, block_input, middle, slope_state, slope_even, slope_odd, taps, x_even, x_odd, vec,
        vecs,
    ) = operands
    count, width = q.shape
    every = k.shape[0]
    hidden = hid.shape[1]
    states = count // 2
    size = states + TILE
    y_size = parts // 2
    plan, plane, rows, total = back_plan(parts, clips, width, hidden)
    big = max(hidden // parts, 3 * (width // parts))
    scratch = [
        ((y_size, total, width), BF16),
        ((3, big, width), BF16),
        ((max(hidden // width * count, 3 * width), width), BF16),
        (w2.shape, BF16),
        (w1.shape, BF16),
        ((max(hidden, 3 * width), count), BF16),
        ((width, count), BF16),
        ((width, count), BF16),
        ((count, width), BF16),
        ((count, width), BF16),
        ((count, width), BF16),
        ((count, width), BF16),
        ((max(2 * every, 4 * count), width), BF16),
        (inv.shape, F32),
        ((count, width), BF16),
        ((count, width), F32),
        ((count, width), F32),
        (slope_odd.shape, BF16),
        (x_even.shape, BF16),
        (x_odd.shape, BF16),
        ((TILE, width), F32),
        ((TILE, width), F32),
        ((TILE, width), F32),
        ((2, count, every), BF16),
        ((count, every), BF16),
        ((LANES, count), BF16),
        ((width, every), BF16),
        ((width, every), BF16),
        ((2, width, every - count), BF16),
        ((count, width), BF16),
        ((count, width), BF16),
        ((count, width), F32),
        ((count, width), BF16),
        ((2 * size, width), BF16),
        ((width, x_even.shape[1]), BF16),
        ((2, size, 2 * LANES), F32),
    ]
    scratch = [pltpu.VMEM(s, d) for s, d in scratch]
    groups = len(bits_of(parts)) - 1
    scratch += [
        pltpu.SemaphoreType.DMA((7 * y_size + 1,)),
        pltpu.SemaphoreType.DMA((7 * y_size + 1,)),
        pltpu.SemaphoreType.DMA((groups + 1, 2)),
        pltpu.SemaphoreType.DMA((groups + 1, 2)),
        pltpu.SemaphoreType.DMA((32 + hidden // width,)),
        pltpu.SemaphoreType.DMA((2,)),
        pltpu.SemaphoreType.DMA((total // rows,)),
    ]
    scratch += Reducer.scratch(y_size, plane, total // rows, rows, width)
    return pl.pallas_call(
        functools.partial(back_kernel, plan, rows),
        out_shape=[
            jax.ShapeDtypeStruct((total, width), BF16),
            jax.ShapeDtypeStruct((2, size, 2 * LANES), F32),
        ],
        in_specs=[ANY] * len(operands),
        out_specs=[ANY] * 2,
        scratch_shapes=scratch,
        compiler_params=pltpu.CompilerParams(
            collective_id=3, has_side_effects=True, vmem_limit_bytes=64 << 20
        ),
        name="back",
    )(*operands)


def per_device(
    mel_frames,
    lengths,
    conv1_weight,
    conv1_bias,
    conv2_weight,
    conv2_bias,
    ln1_gain,
    ln1_bias,
    qkv_weight,
    q_bias,
    v_bias,
    out_weight,
    out_bias,
    ln2_gain,
    ln2_bias,
    fc1_weight,
    fc1_bias,
    fc2_weight,
    fc2_bias,
    cotangent,
):
    parts = lax.axis_size("tm")
    place = lax.axis_index("tm")
    clips = lax.axis_size("clip")
    y_size = parts // 2
    core, y_place = place % 2, place // 2
    mine = y_place % 2
    frames, mels = mel_frames.shape[1:]
    states, width = cotangent.shape[1:]
    hidden = fc1_weight.shape[1] * parts
    rows = 2 * states
    share = conv1_bias.shape[0]
    size = states + TILE

    w1_own = jnp.pad(conv1_weight, ((0, 0), (0, LANES - mels), (0, 0))).reshape(3 * LANES, share).T
    w2_own = conv2_weight.reshape(3 * width, share).T
    vec_list = [
        conv1_bias, conv2_bias, ln1_gain, ln1_bias, q_bias, v_bias, out_bias, ln2_gain, ln2_bias,
        fc2_bias,
    ]
    vec_own = jnp.concatenate([jnp.stack(vec_list), fc1_bias.reshape(-1, share)], axis=0)
    vec_count = vec_own.shape[0]
    vec_own = jnp.pad(vec_own, ((0, TILE - vec_count), (0, -share % LANES)))

    frame_ids = place * frames + jnp.arange(frames)
    frame_valid = (frame_ids[None, :] < lengths[:, None])[..., None]
    masked = jnp.where(frame_valid, mel_frames, jnp.zeros_like(mel_frames))
    masked = jnp.pad(masked.reshape(2, states, 2, mels), ((0, 0), (0, 0), (0, 0), (0, LANES - mels)))
    masked = masked.reshape(2, states, 2 * LANES)
    up = [(i, i + 1) for i in range(parts - 1)]
    down = [(j, i) for i, j in up]
    before = lax.ppermute(masked[:, states - 1 :], "tm", up)
    after = lax.ppermute(masked[:, :1], "tm", down)
    gap = jnp.zeros((2, TILE - 2, 2 * LANES), BF16)
    mel_ext = jnp.concatenate([masked, after, gap, before], axis=1)
    (
        w1, vec_raw, vecs, w2, wqkv, state_taps, x_even, x_odd, slope_even, slope_odd,
        state_slope, block_input, normed1, queries, keys, values, wout, wfc1,
    ) = front(
        mel_ext, w1_own, vec_own, w2_own, qkv_weight.T, out_weight.T, fc1_weight.T,
        jnp.asarray(positions(states * parts, width)), parts, y_size,
    )
    gain_one, bout, gain_two, shift_two, bfc2 = [vecs[i] for i in (2, 6, 7, 8, 9)]
    bfc1 = vec_raw.reshape(parts, TILE, -1)[:, 10:vec_count, :share].astype(F32).reshape(-1)

    def swapped(array):
        got = xor_swap(pick(array, 1 - mine), "tm", 2)
        own = pick(array, mine)
        return jnp.where(mine == 0, jnp.stack([own, got]), jnp.stack([got, own]))

    length = pick(lengths, mine)
    cot = swapped(cotangent).reshape(rows, width)
    group = [m for m in bits_of(parts) if m != 2]
    segs = [4 * ((place ^ m) // 4) + 2 * jnp.arange(2) + (place ^ m) % 2 for m in combos(group)]
    segs = jnp.concatenate(segs)
    key_ids = (segs[:, None] * states + jnp.arange(states)[None, :]).reshape(-1)
    key_valid = 2 * key_ids < length
    all_states = key_ids.shape[0]

    bias = jnp.broadcast_to(jnp.where(key_valid, 0.0, -1e30).astype(F32), (8, all_states))
    attended, inverse, wfc2, exponents = attention(
        queries, keys, values, bias, fc2_weight.T, parts, y_size
    )
    middle = block_input + mat_t(attended, wout) + bout
    unit2, scale2 = norm_parts(middle)
    normed2 = (unit2 * gain_two + shift_two).astype(BF16)
    hidden_act, hidden_slope = gelu_pair(mat_t(normed2, wfc1) + bfc1)
    hidden_act = hidden_act.astype(BF16)
    hidden_slope = hidden_slope.astype(BF16)
    out_rows = (middle + mat_t(hidden_act, wfc2) + bfc2).astype(BF16)

    def unswapped(array):
        got = xor_swap(pick(array, 1 - mine), "tm", 2)
        own = pick(array, mine)
        return jnp.where(mine == 0, jnp.stack([own, got]), jnp.stack([got, own]))

    out_states = unswapped(out_rows.reshape(2, states, width))

    cot_float = cot.astype(F32)
    bfc2_grad = jnp.sum(cot_float, axis=0)
    hidden_grad = (mat(cot, wfc2) * hidden_slope.astype(F32)).astype(BF16)
    bfc1_grad = jnp.sum(hidden_grad.astype(F32), axis=0)
    normed2_grad = mat(hidden_grad, wfc1)
    gain_two_grad = jnp.sum(normed2_grad * unit2, axis=0)
    shift_two_grad = jnp.sum(normed2_grad, axis=0)
    middle_grad = cot_float + norm_back(normed2_grad, unit2, scale2, gain_two)
    branch_grad = middle_grad.astype(BF16)
    bout_grad = jnp.sum(branch_grad.astype(F32), axis=0)

    attended_grad = mat(branch_grad, wout).astype(BF16)
    zeros = jnp.zeros((width,), F32)
    vec_grads = [zeros] * 6 + [bout_grad, gain_two_grad, shift_two_grad, bfc2_grad]
    vec_part = jnp.concatenate([jnp.stack(vec_grads), bfc1_grad.reshape(-1, width)], axis=0)
    vec_part = jnp.pad(vec_part, ((0, TILE - vec_count), (0, 0)))
    summed, mel_back = back(
        (
            hidden_act, hidden_grad.T, cot.T, normed2, branch_grad.T, attended, attended_grad, queries,
            keys, values, inverse, exponents, wqkv, w2, w1, normed1, block_input, middle_grad,
            state_slope, slope_even, slope_odd, state_taps, x_even, x_odd, vec_part, vecs,
        ),
        parts,
        clips,
    )
    plan = back_plan(parts, clips, width, hidden)[0]

    def rows_of(name):
        first, count = plan[name]
        return summed[first : first + count].astype(F32)

    fc2_sum = rows_of("fc2").reshape(hidden // width, share, width)
    fc2_sum = jnp.swapaxes(fc2_sum, 1, 2).reshape(hidden, share)
    conv2_sum = jnp.swapaxes(rows_of("conv2").reshape(3, share, width), 1, 2)
    conv1_sum = rows_of("conv1")
    conv1_sum = jnp.concatenate([conv1_sum[:, : 3 * LANES], conv1_sum[:, 3 * LANES :]], axis=0)
    conv1_sum = conv1_sum.T.reshape(3, LANES, share)[:, :mels]
    all_vec = rows_of("vec")
    vec_sum = lax.dynamic_slice_in_dim(all_vec, place * share, share, axis=1)
    bfc1_sum = lax.dynamic_slice_in_dim(
        all_vec[10:vec_count].reshape(-1), place * (hidden // parts), hidden // parts
    )

    from_before = lax.ppermute(mel_back[:, states], "tm", up)
    from_after = lax.ppermute(mel_back[:, size - 1], "tm", down)
    mel_back = mel_back[:, :states].at[:, 0].add(from_before).at[:, -1].add(from_after)
    mel_back = mel_back.reshape(2, states, 2, LANES)[..., :mels].reshape(2, frames, mels)
    mel_grad = jnp.where(frame_valid, mel_back, 0.0).astype(BF16)

    return (
        out_states,
        mel_grad,
        conv1_sum,
        vec_sum[0],
        conv2_sum,
        vec_sum[1],
        vec_sum[2],
        vec_sum[3],
        rows_of("qkv").T,
        vec_sum[4],
        vec_sum[5],
        rows_of("out").T,
        vec_sum[6],
        vec_sum[7],
        vec_sum[8],
        rows_of("fc1").T,
        bfc1_sum,
        fc2_sum,
        vec_sum[9],
    )


def solution(mesh):
    return jax.shard_map(
        per_device,
        mesh=mesh,
        in_specs=(
            P("clip", "tm", None),
            P("clip"),
            P(None, None, "tm"),
            P("tm"),
            P(None, None, "tm"),
            P("tm"),
            P("tm"),
            P("tm"),
            P(None, "tm"),
            P("tm"),
            P("tm"),
            P(None, "tm"),
            P("tm"),
            P("tm"),
            P("tm"),
            P(None, "tm"),
            P("tm"),
            P(None, "tm"),
            P("tm"),
            P("clip", "tm", None),
        ),
        out_specs=(
            P("clip", "tm", None),
            P("clip", "tm", None),
            P(None, None, "tm"),
            P("tm"),
            P(None, None, "tm"),
            P("tm"),
            P("tm"),
            P("tm"),
            P(None, "tm"),
            P("tm"),
            P("tm"),
            P(None, "tm"),
            P("tm"),
            P("tm"),
            P("tm"),
            P(None, "tm"),
            P("tm"),
            P(None, "tm"),
            P("tm"),
        ),
        check_vma=False,
    )
```

```python
import functools
import math

import jax
import jax.numpy as jnp
import numpy as np
from jax import lax
from jax.experimental import pallas as pl
from jax.experimental.pallas import tpu as pltpu
from jax.sharding import PartitionSpec as P

HEADS = 12
HEAD_DIM = 64
F32 = jnp.float32
BF16 = jnp.bfloat16
SCALE = 1.0 / math.sqrt(HEAD_DIM)
TILE = 16
LANES = 128
MESH = pl.DeviceIdType.MESH
ANY = pl.BlockSpec(memory_space=pl.ANY)
VMEM = pl.BlockSpec(memory_space=pltpu.VMEM)


def xor_swap(array, axis, mask):
    size = lax.axis_size(axis)
    return lax.ppermute(array, axis, [(i, i ^ mask) for i in range(size)])


def pick(array, index, axis=0):
    return lax.dynamic_index_in_dim(array, index, axis=axis, keepdims=False)


def bits_of(size):
    return [1 << b for b in range(size.bit_length() - 1)]


def combos(masks):
    found = [0]
    for mask in masks:
        found = found + [m ^ mask for m in found]
    return found


def flip(index, mask):
    return index + mask * (1 - 2 * ((index // mask) % 2))


def flip_all(index, mask):
    for bit in bits_of(2 * mask) if mask else []:
        if mask & bit:
            index = flip(index, bit)
    return index


def gelu_pair(v):
    a = jnp.abs(v) * (1.0 / math.sqrt(2.0))
    t = 1.0 / (1.0 + 0.3275911 * a)
    poly = t * (
        0.254829592
        + t * (-0.284496736 + t * (1.421413741 + t * (-1.453152027 + t * 1.061405429)))
    )
    bell = jnp.exp(-0.5 * v * v)
    tail = 0.5 * poly * bell
    cdf = jnp.where(v >= 0, 1.0 - tail, tail)
    return v * cdf, cdf + v * bell * (1.0 / math.sqrt(2.0 * math.pi))


def norm_parts(v):
    center = v - jnp.mean(v, axis=-1, keepdims=True)
    spread = jnp.mean(center * center, axis=-1, keepdims=True)
    scale = lax.rsqrt(spread + 1e-05)
    return center * scale, scale


def norm_back(grad, unit, scale, gain):
    a = grad * gain
    mean_a = jnp.mean(a, axis=-1, keepdims=True)
    mean_an = jnp.mean(a * unit, axis=-1, keepdims=True)
    return (a - mean_a - unit * mean_an) * scale


def positions(count, width):
    half = width // 2
    rates = np.exp(-(math.log(10000.0) / (half - 1)) * np.arange(half))
    angles = np.arange(count)[:, None] * rates[None, :]
    return np.concatenate([np.sin(angles), np.cos(angles)], axis=1).astype(np.float32)


def mat(a, b):
    return jnp.dot(a, b, preferred_element_type=F32)


def mat_t(a, b):
    return lax.dot_general(a, b, (((1,), (1,)), ((), ())), preferred_element_type=F32)


def mat_l(a, b):
    return lax.dot_general(a, b, (((0,), (0,)), ((), ())), preferred_element_type=F32)


def aligned(index, step):
    return pl.multiple_of(index * step, step)


class Place:
    def __init__(self):
        self.parts = lax.axis_size("tm")
        self.clips = lax.axis_size("clip")
        self.tm = lax.axis_index("tm")
        self.cl = lax.axis_index("clip")
        self.y_size = self.parts // 2
        self.x_size = self.y_size
        self.z_size = self.clips // self.x_size
        self.core = self.tm % 2
        self.y = self.tm // 2
        self.x = self.cl % self.x_size
        self.z = self.cl // self.x_size

    def tm_partner(self, mask):
        return {"tm": flip(self.tm, mask)}

    def clip_partner(self, mask):
        return {"clip": flip(self.cl, mask)}


def greet(partners):
    barrier = pltpu.get_barrier_semaphore()
    for partner in partners:
        pl.semaphore_signal(barrier, inc=1, device_id=partner, device_id_type=MESH)
    pl.semaphore_wait(barrier, len(partners))


class Gather:
    def __init__(self, at, own, full, first, count, split, sends, receives, base):
        self.at, self.own, self.full = at, own, full
        self.first, self.count = first, count
        self.shard = own.shape[0]
        while split > 1 and count % (TILE * split):
            split //= 2
        self.split = split if split >= at.x_size else 1
        self.sends, self.receives, self.base = sends, receives, base
        self.used = 0
        self.y_masks = [2 * b for b in bits_of(at.y_size)]
        self.x_masks = bits_of(self.split)
        self.pending, self.have, self.got = [], [], [0]
        self.phase = 0
        self.core_copies, self.started = [], []

    @staticmethod
    def slots(parts, split):
        ys = parts // 2 - 1
        return ys + ys * (split - 1) + 1 + ys * split

    def region(self, mask, part):
        rows = self.count // self.split
        index = flip_all(self.at.tm, mask) * self.shard + self.first
        if part is not None:
            index = index + part * rows
        else:
            rows = self.count
        return pl.ds(pl.multiple_of(index, TILE), rows)

    def send(self, source, region, partner):
        slot = self.base + self.used
        self.used += 1
        copy = pltpu.make_async_remote_copy(
            src_ref=source,
            dst_ref=self.full.at[region],
            send_sem=self.sends.at[slot],
            recv_sem=self.receives.at[slot],
            device_id=partner,
            device_id_type=MESH,
        )
        copy.start()
        self.started.append(copy)
        return copy

    def part(self, mask):
        return flip_all(self.at.cl % self.split, mask) if self.split > 1 else 0

    def own_part(self):
        rows = self.count // self.split
        return self.own.at[pl.ds(pl.multiple_of(self.first + self.part(0) * rows, TILE), rows)]

    def start(self):
        at = self.at
        mask = self.y_masks[0]
        copy = self.send(self.own_part(), self.region(0, self.part(0)), at.tm_partner(mask))
        self.pending.append((copy, mask, 0))
        whole = self.own.at[pl.ds(self.first, self.count)]
        self.core_copies.append(self.send(whole, self.region(0, None), at.tm_partner(1)))

    def relay(self, mask, part):
        region = self.region(mask, part)
        self.core_copies.append(self.send(self.full.at[region], region, self.at.tm_partner(1)))

    def pass_on(self):
        if self.phase < len(self.x_masks):
            mask = self.x_masks[self.phase]
            for m in self.have:
                for q in self.got:
                    region = self.region(m, self.part(q))
                    copy = self.send(self.full.at[region], region, self.at.clip_partner(mask))
                    self.pending.append((copy, m, q ^ mask))

    def after_y(self):
        at = self.at
        for i, mask in enumerate(self.y_masks):
            for copy, m, _ in self.pending:
                copy.wait_recv()
                self.have.append(m)
            self.pending = []
            if i + 1 < len(self.y_masks):
                after = self.y_masks[i + 1]
                for m in [0] + self.have:
                    region = self.region(m, self.part(0))
                    source = self.full.at[region] if m else self.own_part()
                    copy = self.send(source, region, at.tm_partner(after))
                    self.pending.append((copy, m ^ after, 0))
        self.pass_on()
        for m in self.have:
            self.relay(m, self.part(0))

    def after_x(self):
        if self.phase == len(self.x_masks):
            return
        arrived, self.pending = self.pending, []
        for copy, _, _ in arrived:
            copy.wait_recv()
        self.got = self.got + [q ^ self.x_masks[self.phase] for q in self.got]
        self.phase += 1
        self.pass_on()
        for _, m, q in arrived:
            self.relay(m, self.part(q))

    def finish(self):
        for copy in self.core_copies:
            copy.wait_recv()

    def close(self):
        for copy in self.started:
            copy.wait_send()


def fore_kernel(states, *refs):
    (
        mel_in, w1_own, vec_own, w2_own, wqkv_own, wout_own, wfc1_own, wfc2_own, pos_in,
        bias,
        w1_out, w2_out, wqkv_out, vecs_out, taps_out, x_even_out, x_odd_out, slope_even_out,
        slope_odd_out, slope_state_out, block_input_out, normed_out, queries_out, keys_out,
        values_out, attended_out, inverse_out, wout, wfc1, wfc2, expo,
        w1, vec_raw, vecs, w2, wqkv, taps, x_even, x_odd, slope_even, slope_odd, slope_state,
        block_input, normed, queries, keys, values, attended, inverse,
        mel, beside, edges, odd_act, tmp, pos, buffer, own_out, own_fc1, own_fc2,
        sends, receives, kv_send, kv_recv, mel_send, mel_recv, local, out_sem, expo_sem,
    ) = refs
    at = Place()
    width = block_input.shape[1]
    rows = 2 * states
    size = states + TILE
    block = 256
    mine = at.y % 2
    seg = [4 * (at.tm // 4) + 2 * s + at.core for s in range(2)]
    right = {"tm": (at.tm + 1) % at.parts}
    left = {"tm": (at.tm + at.parts - 1) % at.parts}
    partners = [at.tm_partner(m) for m in bits_of(at.parts)] + [right, left]
    partners += [at.clip_partner(m) for m in bits_of(at.x_size)]

    loads = {}

    def load(name, src, dst):
        loads[name] = pltpu.make_async_copy(src, dst, local.at[len(loads)])
        loads[name].start()

    def place_of(own):
        return pl.ds(aligned(at.tm, own.shape[0]), own.shape[0])

    kept = []

    def keep(src, dst):
        kept.append(pltpu.make_async_copy(src, dst, out_sem.at[len(kept)]))
        kept[-1].start()

    load("mel", mel_in.at[mine], mel.at[mine])
    for name, own, full in (
        ("w1", w1_own, w1), ("vec", vec_own, vec_raw), ("w2", w2_own, w2), ("wqkv", wqkv_own, wqkv),
    ):
        load(name, own, full.at[place_of(own)])
    through = (("wout", wout_own, own_out), ("wfc1", wfc1_own, own_fc1), ("wfc2", wfc2_own, own_fc2))
    for name, own, stop in through:
        load(name, own, stop)
    for s in range(2):
        from_table = pos_in.at[pl.ds(aligned(seg[s], states), states)]
        load("pos%d" % s, from_table, pos.at[pl.ds(s * states, states)])
    greet(partners)

    def send(src, dst, slot, partner):
        copy = pltpu.make_async_remote_copy(
            src_ref=src,
            dst_ref=dst,
            send_sem=mel_send.at[slot],
            recv_sem=mel_recv.at[slot],
            device_id=partner,
            device_id_type=MESH,
        )
        copy.start()
        return copy

    to_right = send(mel_in.at[:, pl.ds(states - TILE, TILE)], beside.at[0], 0, right)
    to_left = send(mel_in.at[:, pl.ds(0, TILE)], beside.at[1], 1, left)
    swap = send(mel_in.at[1 - mine], mel.at[mine], 2, at.tm_partner(2))
    base = 0
    groups = {}
    split = at.x_size
    for name, own, full, pieces in (
        ("w1", w1_own, w1, 1), ("vec", vec_own, vec_raw, 1), ("w2", w2_own, w2, 2),
        ("qkv", wqkv_own, wqkv, 2), ("out", wout_own, wout, 1), ("fc1", wfc1_own, wfc1, 2),
        ("fc2", wfc2_own, wfc2, 2),
    ):
        whole = own.shape[0]
        count = whole // pieces if whole % (pieces * TILE * split) == 0 else whole
        groups[name] = []
        for first in range(0, whole, count):
            g = Gather(at, own, full, first, count, split, sends, receives, base)
            base += Gather.slots(at.parts, g.split)
            groups[name].append(g)

    def part(name, i):
        return groups[name][i : i + 1]

    def run(what, *pieces):
        for piece in pieces:
            for g in piece:
                getattr(g, what)()

    def finish(*names):
        for name in names:
            run("finish", groups[name])

    run("start", part("w1", 0), part("vec", 0), part("w2", 0), part("w2", 1))
    to_right.wait_recv()
    to_left.wait_recv()
    forward = [
        send(beside.at[i, 1 - mine], edges.at[mine, i], 3 + i, at.tm_partner(2)) for i in range(2)
    ]
    for i in range(2):
        edges[mine, i] = beside[i, mine]
    swap.wait_recv()
    loads["mel"].wait()
    for copy in forward:
        copy.wait_recv()
    for s in range(2):
        row = lax.broadcasted_iota(jnp.int32, (TILE, 2 * LANES), 0)
        has_before = jnp.minimum(seg[s], 1).astype(F32)
        has_after = jnp.minimum(at.parts - 1 - seg[s], 1).astype(F32)
        tail = jnp.where(row == 0, edges[s, 1].astype(F32) * has_after, 0.0)
        tail = jnp.where(row == TILE - 1, edges[s, 0].astype(F32) * has_before, tail)
        m = jnp.concatenate([mel[s].astype(F32), tail], axis=0)
        before = pltpu.roll(m, 1, 0)
        after = pltpu.roll(m, size - 1, 0)
        low = pl.ds(0, LANES)
        even_rows = pl.ds(s * states, states)
        odd_rows = pl.ds(s * size, size)
        x_even[even_rows, low] = before[:states, LANES:].astype(BF16)
        x_even[even_rows, pl.ds(LANES, 2 * LANES)] = m[:states].astype(BF16)
        x_odd[odd_rows, pl.ds(0, 2 * LANES)] = m.astype(BF16)
        x_odd[odd_rows, pl.ds(2 * LANES, LANES)] = after[:, :LANES].astype(BF16)
    keep(x_even, x_even_out)
    keep(x_odd, x_odd_out)
    for (name, own, stop), full in zip(through, (wout, wfc1, wfc2)):
        loads[name].wait()
        keep(stop, full.at[place_of(own)])
    run("after_y", groups["w1"], groups["vec"], part("w2", 0))
    run("start", part("qkv", 0))
    run("after_x", groups["w1"], groups["vec"])
    finish("w1", "vec")
    loads["w1"].wait()
    loads["vec"].wait()
    keep(w1, w1_out)
    total = jnp.zeros(vecs.shape, F32)
    share = width // at.parts
    for j in range(at.parts):
        piece = vec_raw[pl.ds(j * TILE, TILE)].astype(F32)
        low = (j * share) // LANES * LANES
        cells = [piece]
        if low > 0:
            cells = [jnp.zeros((TILE, low), F32)] + cells
        if width - low - piece.shape[1] > 0:
            cells = cells + [jnp.zeros((TILE, width - low - piece.shape[1]), F32)]
        placed = jnp.concatenate(cells, axis=1)
        shift = j * share - low
        total = total + (pltpu.roll(placed, shift, 1) if shift else placed)
    row = lax.broadcasted_iota(jnp.int32, vecs.shape, 0)
    total = jnp.where(row < 10, total, 0.0)
    pieces = wfc1_own.shape[0] // share
    for j in range(at.parts):
        for i in range(pieces):
            first = (j * pieces + i) * share
            piece = vec_raw[pl.ds(j * TILE, TILE)].astype(F32)[10 + i : 11 + i]
            column = first % width
            low = column // LANES * LANES
            cells = [piece]
            if low > 0:
                cells = [jnp.zeros((1, low), F32)] + cells
            if width - low - piece.shape[1] > 0:
                cells = cells + [jnp.zeros((1, width - low - piece.shape[1]), F32)]
            placed = jnp.broadcast_to(jnp.concatenate(cells, axis=1), vecs.shape)
            if column - low:
                placed = pltpu.roll(placed, column - low, 1)
            total = total + jnp.where(row == 10 + first // width, placed, 0.0)
    vecs[...] = total

    def vec(i, cols):
        return vecs[pl.ds(i, 1), cols]

    keep(vecs, vecs_out)
    between = [
        lambda: (run("after_y", part("w2", 1)), run("start", part("qkv", 1))),
        lambda: None,
        lambda: (run("after_x", part("w2", 0)), run("after_y", part("qkv", 0)), run("start", part("out", 0), part("fc1", 0))),
        lambda: (run("after_x", part("w2", 1)), run("after_y", part("qkv", 1)), run("start", part("fc1", 1))),
    ]
    for s in range(2):

        def odd_columns(j, carry, s=s):
            cols = pl.ds(aligned(j, block), block)
            tmp[pl.ds(0, size)] = mat_t(x_odd[pl.ds(s * size, size)], w1[cols])

            def odd_rows(i, carry):
                r = pl.ds(aligned(i, 64), 64)
                act, slope = gelu_pair(tmp[r] + vec(0, cols))
                odd_act[r, cols] = act
                taps[pl.ds(aligned(i, 64) + s * states, 64), pl.ds(2 * width + aligned(j, block), block)] = act.astype(BF16)
                slope_odd[pl.ds(aligned(i, 64) + s * size, 64), cols] = slope.astype(BF16)
                return carry

            lax.fori_loop(0, states // 64, odd_rows, 0)
            r = pl.ds(states, TILE)
            act, slope = gelu_pair(tmp[r] + vec(0, cols))
            last = lax.broadcasted_iota(jnp.int32, act.shape, 0) == TILE - 1
            first = jnp.minimum(seg[s], 1).astype(F32)
            act = jnp.where(last, act * first, 0.0)
            slope = jnp.where(last, slope * first, 0.0)
            odd_act[r, cols] = act
            slope_odd[pl.ds(s * size + states, TILE), cols] = slope.astype(BF16)
            moved = pltpu.roll(odd_act[:, cols], 1, 0)
            taps[pl.ds(s * states, states), cols] = moved[:states].astype(BF16)
            return carry

        lax.fori_loop(0, width // block, odd_columns, 0)
        between[2 * s]()

        def even_columns(j, carry, s=s):
            cols = pl.ds(aligned(j, block), block)
            tmp[pl.ds(0, states)] = mat_t(x_even[pl.ds(s * states, states)], w1[cols])

            def even_rows(i, carry):
                r = pl.ds(aligned(i, 64), 64)
                act, slope = gelu_pair(tmp[r] + vec(0, cols))
                out = pl.ds(aligned(i, 64) + s * states, 64)
                taps[out, pl.ds(width + aligned(j, block), block)] = act.astype(BF16)
                slope_even[out, cols] = slope.astype(BF16)
                return carry

            lax.fori_loop(0, states // 64, even_rows, 0)
            return carry

        lax.fori_loop(0, width // block, even_columns, 0)
        between[2 * s + 1]()

    finish("w2")
    loads["w2"].wait()
    loads["pos0"].wait()
    loads["pos1"].wait()
    keep(w2, w2_out)
    keep(taps, taps_out)
    keep(slope_even, slope_even_out)
    keep(slope_odd, slope_odd_out)

    def state_columns(j, carry):
        cols = pl.ds(aligned(j, block), block)
        tmp[pl.ds(0, rows)] = mat_t(taps[...], w2[cols])

        def state_rows(i, carry):
            r = pl.ds(aligned(i, 64), 64)
            act, slope = gelu_pair(tmp[r] + vec(1, cols))
            block_input[r, cols] = act + pos[r, cols]
            slope_state[r, cols] = slope.astype(BF16)
            return carry

        lax.fori_loop(0, rows // 64, state_rows, 0)
        return carry

    third = width // block // 3
    lax.fori_loop(0, third, state_columns, 0)
    run("after_y", groups["out"])
    lax.fori_loop(third, 2 * third, state_columns, 0)
    run("after_x", part("qkv", 0))
    lax.fori_loop(2 * third, width // block, state_columns, 0)
    keep(block_input, block_input_out)
    keep(slope_state, slope_state_out)
    full = pl.ds(0, width)

    def norm_rows(i, carry):
        r = pl.ds(aligned(i, 32), 32)
        unit, _ = norm_parts(block_input[r])
        normed[r] = (unit * vec(2, full) + vec(3, full)).astype(BF16)
        return carry

    lax.fori_loop(0, rows // 32, norm_rows, 0)
    run("after_x", part("qkv", 1))
    keep(normed, normed_out)
    finish("qkv")
    loads["wqkv"].wait()
    keep(wqkv, wqkv_out)
    group = [m for m in bits_of(at.parts) if m != 2]

    def exchange(array, base):
        held = rows
        for n, mask in enumerate(group):
            copy = pltpu.make_async_remote_copy(
                src_ref=array.at[pl.ds(0, held)],
                dst_ref=array.at[pl.ds(held, held)],
                send_sem=kv_send.at[base + n],
                recv_sem=kv_recv.at[base + n],
                device_id=at.tm_partner(mask),
                device_id_type=MESH,
            )
            copy.start()
            if n + 1 < len(group):
                copy.wait()
                held = 2 * held
            else:
                return copy

    def project(target, first, bias):
        def columns(j, carry):
            cols = pl.ds(aligned(j, block), block)
            part = mat_t(normed[...], wqkv[pl.ds(first + aligned(j, block), block)])
            if bias is not None:
                part = part + vec(bias, cols)
            target[pl.ds(0, rows), cols] = part.astype(BF16)
            return carry

        lax.fori_loop(0, width // block, columns, 0)

    project(keys, width, None)
    key_copy = exchange(keys, 1)
    run("after_y", part("fc1", 0))
    run("start", part("fc2", 0))
    run("after_x", groups["out"])
    project(values, 2 * width, 5)
    value_copy = exchange(values, 1 + len(group))
    project(queries, 0, 4)
    keep(queries, queries_out)
    run("after_y", part("fc1", 1))
    run("start", part("fc2", 1))
    key_copy.wait()
    value_copy.wait()
    keep(keys, keys_out)
    keep(values, values_out)
    q, k, v = queries, keys, values
    pairs = width // LANES
    inverse[...] = jnp.zeros(inverse.shape, F32)
    lane = lax.broadcasted_iota(jnp.int32, (rows, LANES), 1)

    def out_copy(p, h):
        return pltpu.make_async_copy(buffer.at[h], expo.at[2 * p + h], expo_sem.at[h])

    def pair_body(p, carry):
        cols = pl.ds(aligned(p, LANES), LANES)
        for h in range(2):

            @pl.when(p > 0)
            def _(h=h):
                out_copy(p - 1, h).wait()

        scaled = q[:, cols].astype(F32) * SCALE
        inv = inverse[...]
        outs = []
        scores = []
        for h in range(2):
            own = (lane < HEAD_DIM) if h == 0 else (lane >= HEAD_DIM)
            head = jnp.where(own, scaled, 0.0).astype(BF16)
            scores.append(mat_t(head, k[:, cols]) + bias[pl.ds(0, 1)])
        for h in range(2):
            largest = jnp.max(scores[h], axis=-1, keepdims=True)
            exponent = jnp.exp(scores[h] - largest)
            one = 1.0 / jnp.sum(exponent, axis=-1, keepdims=True)
            low = exponent.astype(BF16)
            buffer[h] = low
            outs.append(mat(low, v[:, cols]) * one)
            inv = jnp.where(lane == 2 * p + h, one, inv)
        attended[:, cols] = jnp.where(lane < HEAD_DIM, outs[0], outs[1]).astype(BF16)
        inverse[...] = inv
        for h in range(2):
            out_copy(p, h).start()
        return carry

    events = [
        ("after_x", part("fc1", 0)),
        ("after_y", part("fc2", 0)),
        ("after_x", part("fc1", 1)),
        ("after_y", part("fc2", 1)),
        ("after_x", part("fc2", 0)),
        ("after_x", part("fc2", 1)),
    ]
    for i, event in enumerate(events):
        lax.fori_loop(i * pairs // len(events), (i + 1) * pairs // len(events), pair_body, 0)
        run(*event)
    keep(attended, attended_out)
    keep(inverse, inverse_out)
    for h in range(2):
        out_copy(pairs - 1, h).wait()
    finish("out", "fc1", "fc2")
    for copy in [to_right, to_left, swap] + forward:
        copy.wait_send()
    for pieces in groups.values():
        run("close", pieces)
    for copy in kept:
        copy.wait()


def fore(mel, owns, pos, bias, parts, x_size):
    w1_own, vec_own, w2_own, wqkv_own, wout_own, wfc1_own, wfc2_own = owns
    states = mel.shape[1]
    rows, width = 2 * states, pos.shape[1]
    every = bias.shape[1]
    full = lambda own: ((parts * own.shape[0], own.shape[1]), BF16)
    both = [
        full(w1_own),
        full(w2_own),
        full(wqkv_own),
        ((TILE, width), F32),
        ((rows, 3 * width), BF16),
        ((rows, 3 * LANES), BF16),
        ((rows + 2 * TILE, 3 * LANES), BF16),
        ((rows, width), BF16),
        ((rows + 2 * TILE, width), BF16),
        ((rows, width), BF16),
        ((rows, width), F32),
        ((rows, width), BF16),
        ((rows, width), BF16),
        ((every, width), BF16),
        ((every, width), BF16),
        ((rows, width), BF16),
        ((rows, LANES), F32),
    ]
    shapes = both + [
        full(wout_own),
        full(wfc1_own),
        full(wfc2_own),
        ((width // HEAD_DIM, rows, every), BF16),
    ]
    here = [pltpu.VMEM(s, d) for s, d in both]
    vec_raw = pltpu.VMEM((parts * TILE, vec_own.shape[1]), BF16)
    here = [here[0], vec_raw, here[3], here[1], here[2]] + here[4:]
    slots = 12 * Gather.slots(parts, x_size)
    return pl.pallas_call(
        functools.partial(fore_kernel, states),
        out_shape=[jax.ShapeDtypeStruct(s, d) for s, d in shapes],
        in_specs=[ANY] * 9 + [VMEM],
        out_specs=[ANY] * len(shapes),
        scratch_shapes=here
        + [
            pltpu.VMEM(mel.shape, BF16),
            pltpu.VMEM((2, 2, TILE, 2 * LANES), BF16),
            pltpu.VMEM((2, 2, TILE, 2 * LANES), BF16),
            pltpu.VMEM((states + TILE, width), F32),
            pltpu.VMEM((max(rows, states + TILE), 256), F32),
            pltpu.VMEM((rows, width), F32),
            pltpu.VMEM((2, rows, every), BF16),
            pltpu.VMEM(wout_own.shape, BF16),
            pltpu.VMEM(wfc1_own.shape, BF16),
            pltpu.VMEM(wfc2_own.shape, BF16),
            pltpu.SemaphoreType.DMA((slots,)),
            pltpu.SemaphoreType.DMA((slots,)),
            pltpu.SemaphoreType.DMA((8,)),
            pltpu.SemaphoreType.DMA((8,)),
            pltpu.SemaphoreType.DMA((6,)),
            pltpu.SemaphoreType.DMA((6,)),
            pltpu.SemaphoreType.DMA((12,)),
            pltpu.SemaphoreType.DMA((len(both) + 4,)),
            pltpu.SemaphoreType.DMA((2,)),
        ],
        compiler_params=pltpu.CompilerParams(
            collective_id=1, has_side_effects=True, vmem_limit_bytes=62 << 20
        ),
        name="fore",
    )(mel, *owns, pos, bias)


class Reducer:
    def __init__(self, at, rows, ahead, held, result, landings, sends, receives):
        self.at, self.rows, self.ahead = at, rows, ahead
        self.source, self.result, self.landings = held, result, landings
        self.sends, self.receives = sends, receives
        self.chunks = result.shape[0] // rows
        self.y_bits = list(reversed(bits_of(at.y_size)))
        plane = [(at.x, b, b) for b in bits_of(at.x_size)]
        plane += [(at.z, b, b * at.x_size) for b in bits_of(at.z_size)]
        self.mine = [(place // b) % 2 for place, b, _ in plane]
        self.partner = [at.clip_partner(mask) for _, _, mask in plane]
        self.y_partner = [at.tm_partner(2 * b) for b in self.y_bits]
        self.tops, self.depth = len(self.y_bits), len(plane)
        self.stages = 1 + self.tops + 2 * self.depth
        self.delays = [0] + [ahead + s for s in range(self.stages - 1)]
        self.times = self.chunks + self.delays[-1]

    @staticmethod
    def scratch(y_size, plane, chunks, rows, width):
        shapes = [pltpu.VMEM((chunks, b, rows, width), BF16) for b in reversed(bits_of(y_size))]
        shapes += [pltpu.VMEM((chunks, rows >> (k + 1), width), BF16) for k in range(plane)]
        slots = len(bits_of(y_size)) + 2 * plane
        return shapes + [pltpu.SemaphoreType.DMA((chunks, slots))] * 2

    def remote(self, src, dst, c, slot, device):
        return pltpu.make_async_remote_copy(
            src_ref=src,
            dst_ref=dst,
            send_sem=self.sends.at[c, slot],
            recv_sem=self.receives.at[c, slot],
            device_id=device,
            device_id_type=MESH,
        )

    def chunk(self, c):
        return pl.ds(pl.multiple_of(c * self.rows, self.rows), self.rows)

    def y_copy(self, c, k):
        b = self.y_bits[k]
        away = b * (1 - (self.at.y // b) % 2)
        if k == 0:
            src = self.source.at[pl.ds(away, b), self.chunk(c)]
        else:
            src = self.landings[k - 1].at[c, pl.ds(away, b)]
        return self.remote(src, self.landings[k].at[c], c, k, self.y_partner[k])

    def half(self, k, bit):
        count = self.rows >> (k + 1)
        return pl.ds(aligned(bit, count), count)

    def current(self, k, c, region):
        if k == 0:
            return self.landings[self.tops - 1].at[c, 0, region]
        return self.landings[self.tops + k - 1].at[c, region]

    def spread(self, c, k):
        src = self.current(k, c, self.half(k, 1 - self.mine[k]))
        dst = self.landings[self.tops + k].at[c]
        return self.remote(src, dst, c, self.tops + k, self.partner[k])

    def kept(self, c, k):
        first = c * self.rows
        for i in range(k + 1):
            first = first + self.mine[i] * (self.rows >> (i + 1))
        count = self.rows >> (k + 1)
        return pl.ds(pl.multiple_of(first, count), count)

    def collect(self, c, k):
        region = self.result.at[self.kept(c, k)]
        src = self.landings[self.tops + k].at[c] if k == self.depth - 1 else region
        return self.remote(src, region, c, self.tops + self.depth + k, self.partner[k])

    def keep(self, c):
        k = self.depth - 1
        return pltpu.make_async_copy(
            self.landings[self.tops + k].at[c], self.result.at[self.kept(c, k)], self.local.at[c]
        )

    def run(self, stage, c):
        if stage == 0:
            self.y_copy(c, 0).start()
        elif stage <= self.tops:
            k = stage - 1
            b = self.y_bits[k]
            own = pl.ds(b * ((self.at.y // b) % 2), b)
            self.y_copy(c, k).wait_recv()
            mine = self.source[own, self.chunk(c)] if k == 0 else self.landings[k - 1][c, own]
            total = mine.astype(F32) + self.landings[k][c].astype(F32)
            self.landings[k][c] = total.astype(BF16)
            if k + 1 < self.tops:
                self.y_copy(c, k + 1).start()
            else:
                self.spread(c, 0).start()
        elif stage <= self.tops + self.depth:
            k = stage - self.tops - 1
            self.spread(c, k).wait_recv()
            mine = self.current(k, c, self.half(k, self.mine[k]))[...]
            total = mine.astype(F32) + self.landings[self.tops + k][c].astype(F32)
            self.landings[self.tops + k][c] = total.astype(BF16)
            if k + 1 < self.depth:
                self.spread(c, k + 1).start()
            else:
                self.collect(c, k).start()
                self.keep(c).start()
        else:
            k = self.depth - 1 - (stage - self.tops - self.depth - 1)
            self.collect(c, k).wait_recv()
            if k == self.depth - 1:
                self.keep(c).wait()
            if k > 0:
                self.collect(c, k - 1).start()

    def step(self, time):
        for stage in range(self.stages):
            c = time - self.delays[stage]

            @pl.when((c >= 0) & (c < self.chunks))
            def _(stage=stage, c=c):
                self.run(stage, c)

    def steps(self, first, last):
        def body(time, carry):
            self.step(time)
            return carry

        lax.fori_loop(first, last, body, 0)

    def close(self):
        def body(c, carry):
            for k in range(self.tops):
                self.y_copy(c, k).wait_send()
            for k in range(self.depth):
                self.spread(c, k).wait_send()
                self.collect(c, k).wait_send()
            return carry

        lax.fori_loop(0, self.chunks, body, 0)


def tile_of(count):
    return max(t for t in range(TILE, 257, TILE) if count % t == 0)


def back_plan(parts, clips, width, hidden):
    share = width // parts
    plane = len(bits_of(parts // 2)) + len(bits_of(clips // (parts // 2)))
    rows = TILE << plane
    plan, first = {}, 0
    early = [("fc2", hidden // parts), ("fc1", hidden // parts), ("out", share)]
    late = [("qkv", 3 * share), ("conv2", 3 * share), ("conv1", share // 2), ("vec", TILE)]
    for group in (early, late):
        for name, count in group:
            plan[name] = (first, count)
            first += count
        plan["gap%d" % len(plan)] = (first, -first % rows)
        first += -first % rows
    plan["last"] = plan["end"] = (first, 0)
    return plan, plane, rows, first


def back_kernel(plan, rows, *refs):
    (
        cot_in, attended_in, wout_in, wfc1_in, wfc2_in, q_in, k_in, v_in, inv_in, expo, wqkv_in,
        w2_in, w1_in, normed1_in, block_input_in, slope_state_in, slope_even_in, slope_odd_in,
        taps_in, x_even_in, x_odd_in, vecs_in,
        result, mel_out, states_out,
        held, stage, arena, weights, w1, g_t, cot_t, branch_t, normed2, attended, att_grad, q, kv,
        inv, normed1, block_input, middle, slope_odd, x_even, x_odd, vec, vec_got, vecs,
        ebuf, score_grad, q_t, k_t, v_t, kv_land, q_grad, state_grad, prev, tmp, even_grad, odd_grad,
        conv1_t, mel_v,
        core_send, core_recv, kv_send, kv_recv, load_sem, expo_sem, local,
    ) = refs[: 25 + 44]
    *landings, sends, receives = refs[25 + 44 :]
    at = Place()
    width = q.shape[1]
    count = q.shape[0]
    states = count // 2
    size = states + TILE
    every = k_in.shape[0]
    hidden = wfc1_in.shape[0]
    share = width // at.parts
    core, mine = at.core, at.y % 2
    core_partner = at.tm_partner(1)

    loads = {}

    def load(name, src, dst):
        copy = pltpu.make_async_copy(src, dst, load_sem.at[len(loads)])
        copy.start()
        loads[name] = copy

    def need(*names):
        for name in names:
            loads[name].wait()

    blocks = hidden // width

    def load_block(i):
        low = pl.ds(i * width, width)
        load("fc1_%d" % i, wfc1_in.at[low], weights.at[i % 2])
        load("fc2_%d" % i, wfc2_in.at[:, low], weights.at[2 + i % 2])

    load("attended", attended_in, attended)
    load("wout", wout_in, arena.at[pl.ds(0, width)])
    load("block_input", block_input_in, block_input)
    load("vecs", vecs_in, vecs)
    load_block(0)
    load_block(1)
    load("q", q_in, q)
    load("inv", inv_in, inv)
    load("k", k_in, kv.at[pl.ds(0, every)])
    load("v", v_in, kv.at[pl.ds(every, every)])
    load("w1", w1_in, w1)
    load("slope_odd", slope_odd_in, slope_odd)
    load("x_even", x_even_in, x_even)
    load("x_odd", x_odd_in, x_odd)

    def fetch(n, slot):
        return pltpu.make_async_copy(expo.at[n], ebuf.at[slot], expo_sem.at[slot])

    fetch(0, 0).start()
    reducer = Reducer(at, rows, 3, held, result, landings, sends, receives)
    reducer.local = local
    greet([core_partner] + reducer.y_partner + reducer.partner)
    place = pl.ds(pl.multiple_of(mine * states, states), states)
    cot_swap = pltpu.make_async_remote_copy(
        src_ref=cot_in.at[1 - mine],
        dst_ref=q_grad.at[place],
        send_sem=kv_send.at[len(bits_of(at.parts)) - 1, 1],
        recv_sem=kv_recv.at[len(bits_of(at.parts)) - 1, 1],
        device_id=at.tm_partner(2),
        device_id_type=MESH,
    )
    cot_swap.start()
    load("cot", cot_in.at[mine], q_grad.at[place])
    done = [0]

    def advance(steps, ready):
        ready = ready if isinstance(ready, int) else plan[ready][0]
        last = max(done[0], min(done[0] + steps, ready // rows))
        if steps == 0:
            last = reducer.times
        reducer.steps(done[0], last)
        done[0] = last
    for name, (first, n) in plan.items():
        if name.startswith("gap") and n:
            for y in range(at.y_size):
                held[y, pl.ds(first, n)] = jnp.zeros((n, width), BF16)

    copies = {}
    slots = {}
    ring = [None] * stage.shape[0]
    turn = [0]

    def give(name, first, parts, places=None):
        for y in places or range(at.y_size):
            slot = turn[0] % len(ring)
            turn[0] += 1
            if ring[slot] is not None:
                ring[slot].wait_send()
            offset = 0
            for n, rows_of, acts in parts:
                tile = tile_of(n)
                for i in range(n // tile):
                    g = rows_of(2 * y + 1 - core, i * tile, tile)
                    stage[slot, pl.ds(offset + i * tile, tile)] = mat(g, acts()).astype(BF16)
                offset += n
            number = len(copies)
            copy = pltpu.make_async_remote_copy(
                src_ref=stage.at[slot, pl.ds(0, offset)],
                dst_ref=held.at[y, pl.ds(first, offset)],
                send_sem=core_send.at[number],
                recv_sem=core_recv.at[number],
                device_id=core_partner,
                device_id_type=MESH,
            )
            copy.start()
            ring[slot] = copy
            copies[name, y] = copy

    def take(name, first, parts, places=None):
        for y in places or range(at.y_size):
            copies[name, y].wait_recv()
            offset = first
            for n, rows_of, acts in parts:
                tile = tile_of(n)
                for i in range(n // tile):
                    g = rows_of(2 * y + core, i * tile, tile)
                    place = pl.ds(offset + i * tile, tile)
                    total = mat(g, acts()) + held[y, place].astype(F32)
                    held[y, place] = total.astype(BF16)
                offset += n

    def rows_from(ref, base, n):
        def rows_of(part, offset, tile):
            return ref[pl.ds(pl.multiple_of(base + part * n + offset, TILE), tile)]

        return rows_of

    def whole(ref):
        return lambda: ref[...]

    def block_of(ref, i, n):
        return lambda: ref[pl.ds(i * n, n)]

    def vec_row(i):
        return vecs[pl.ds(i, 1)]

    tile = 64

    def over_rows(body):
        def run(i, carry):
            body(pl.ds(aligned(i, tile), tile))
            return carry

        lax.fori_loop(0, count // tile, run, 0)

    need("attended", "wout", "block_input", "vecs")
    prev[...] = mat_t(attended[...], arena[pl.ds(0, width)])

    def middle_rows(r):
        total = block_input[r] + prev[r] + vec_row(6)
        middle[r] = total
        unit, _ = norm_parts(total)
        normed2[r] = (unit * vec_row(7) + vec_row(8)).astype(BF16)

    over_rows(middle_rows)
    vec[...] = jnp.zeros(vec.shape, F32)
    acts = (state_grad, even_grad)
    slope_hid = odd_grad.at[pl.ds(0, count)]
    per_y = 2 * (hidden // at.parts)
    group_blocks = per_y // width
    fc2, fc1 = [], []
    for i in range(blocks):
        fc2.append([(share, rows_from(cot_t, 0, share), whole(acts[i % 2]))])
    for y in range(at.y_size):
        fc1.append([(hidden // at.parts, rows_from(g_t, 0, hidden // at.parts), whole(normed2))])
    ready = 0
    for i in range(blocks):
        need("fc1_%d" % i, "fc2_%d" % i)
        up, down, act = weights.at[i % 2], weights.at[2 + i % 2], acts[i % 2]
        tmp[...] = mat_t(normed2[...], up[...])

        def hidden_rows(r, i=i, act=act):
            value, slope = gelu_pair(tmp[r] + vec_row(10 + i))
            act[r] = value.astype(BF16)
            slope_hid[r] = slope.astype(BF16)

        over_rows(hidden_rows)
        part = mat_t(act[...], down[...])
        prev[...] = part if i == 0 else prev[...] + part
        if i == 0:
            need("cot")
            cot_swap.wait()
            wide_cot = q_grad[...].astype(F32)
            vec[pl.ds(9, 1)] = jnp.sum(wide_cot, axis=0, keepdims=True)
            cot_t[...] = jnp.transpose(wide_cot).astype(BF16)
        tmp[...] = mat(q_grad[...], down[...])

        def hidden_back(r):
            slope_hid[r] = (tmp[r] * slope_hid[r].astype(F32)).astype(BF16)

        over_rows(hidden_back)
        part = mat(slope_hid[...], up[...])
        block_input[...] = part if i == 0 else block_input[...] + part
        wide = slope_hid[...].astype(F32)
        vec[pl.ds(10 + i, 1)] = jnp.sum(wide, axis=0, keepdims=True)
        g_t[pl.ds(i * width, width)] = jnp.transpose(wide).astype(BF16)
        if i + 2 < blocks:
            load_block(i + 2)
        give("fc2_%d" % i, plan["fc2"][0] + i * share, fc2[i])
        if i > 0:
            take("fc2_%d" % (i - 1), plan["fc2"][0] + (i - 1) * share, fc2[i - 1])
            ready = i * share
        if (i + 1) % group_blocks == 0:
            y = i // group_blocks
            give("fc1_%d" % y, plan["fc1"][0], fc1[y], [y])
        if i == blocks - 1:
            take("fc2_%d" % i, plan["fc2"][0] + i * share, fc2[i])
            ready = blocks * share
        advance(2, ready)

    def out_rows(r):
        total = middle[r] + prev[r] + vec_row(9)
        normed1[r] = total.astype(BF16)

    over_rows(out_rows)
    state_rows = [pl.ds(pl.multiple_of(m * states, states), states) for m in (mine, 1 - mine)]
    out_swap = pltpu.make_async_remote_copy(
        src_ref=normed1.at[state_rows[1]],
        dst_ref=states_out.at[mine],
        send_sem=kv_send.at[len(bits_of(at.parts)), 0],
        recv_sem=kv_recv.at[len(bits_of(at.parts)), 0],
        device_id=at.tm_partner(2),
        device_id_type=MESH,
    )
    out_swap.start()
    load("out_own", normed1.at[state_rows[0]], states_out.at[mine])
    branch = odd_grad.at[pl.ds(0, count)]

    def middle_back(r):
        grad = block_input[r]
        unit, scale = norm_parts(middle[r])
        vec[pl.ds(7, 1)] += jnp.sum(grad * unit, axis=0, keepdims=True)
        vec[pl.ds(8, 1)] += jnp.sum(grad, axis=0, keepdims=True)
        total = q_grad[r].astype(F32) + norm_back(grad, unit, scale, vec_row(7))
        middle[r] = total
        low = total.astype(BF16)
        branch[r] = low

    over_rows(middle_back)
    load("block_input_again", block_input_in, block_input)
    wide = branch[...].astype(F32)
    vec[pl.ds(6, 1)] = jnp.sum(wide, axis=0, keepdims=True)
    branch_t[...] = jnp.transpose(wide).astype(BF16)
    att_grad[...] = mat(branch[...], arena[pl.ds(0, width)]).astype(BF16)
    load("wqkv", wqkv_in, arena.at[pl.ds(0, wqkv_in.shape[0])])
    for i in range(3):
        load("w2_%d" % i, w2_in.at[:, pl.ds(i * width, width)], weights.at[i])
    out = [(share, rows_from(branch_t, 0, share), whole(attended))]
    give("out", plan["out"][0], out)
    for y in range(at.y_size):
        take("fc1_%d" % y, plan["fc1"][0], fc1[y], [y])
    advance(1, "out")
    take("out", plan["out"][0], out)
    load("slope_even", slope_even_in, normed2)
    need("q", "inv", "k", "v")

    pairs = width // LANES
    lane = lax.broadcasted_iota(jnp.int32, (count, LANES), 1)

    def pair_body(p, carry):
        cols = pl.ds(aligned(p, LANES), LANES)
        q_t[...] = jnp.transpose(q[:, cols].astype(F32)).astype(BF16)
        grads = []
        for h in range(2):
            n = 2 * p + h
            if h == 0:
                fetch(n + 1, 1).start()
            else:

                @pl.when(p < pairs - 1)
                def _(n=n):
                    fetch(n + 1, 0).start()

            fetch(n, h).wait()
            scale = jnp.sum(jnp.where(lane == n, inv[...], 0.0), axis=-1, keepdims=True)
            keep = (lane < HEAD_DIM) if h == 0 else (lane >= HEAD_DIM)
            grad = jnp.where(keep, att_grad[:, cols].astype(F32) * scale, 0.0).astype(BF16)
            wide = grad.astype(F32)
            dot = jnp.sum(wide * attended[:, cols].astype(F32), axis=-1, keepdims=True)
            grad_t = jnp.transpose(wide).astype(BF16)[HEAD_DIM * h : HEAD_DIM * (h + 1)]
            head = pl.ds(pl.multiple_of(p * LANES + h * HEAD_DIM, HEAD_DIM), HEAD_DIM)
            v_t[head, :] = mat(grad_t, ebuf[h]).astype(BF16)
            diff = mat_t(grad, kv[pl.ds(every, every), cols]) - dot
            score_grad[...] = (ebuf[h].astype(F32) * diff).astype(BF16)
            grads.append(mat(score_grad[...], kv[pl.ds(0, every), cols]) * SCALE)
            part = q_t[pl.ds(HEAD_DIM * h, HEAD_DIM)]
            k_t[head, :] = (mat(part, score_grad[...]) * SCALE).astype(BF16)
        q_grad[:, cols] = jnp.where(lane < HEAD_DIM, grads[0], grads[1]).astype(BF16)

        @pl.when(p < most)
        def _():
            reducer.step(done[0] + p)

        return carry

    most = min(pairs, plan["qkv"][0] // rows - done[0])
    lax.fori_loop(0, pairs, pair_body, 0)
    done[0] += most

    for i in range(3):
        load("taps%d" % i, taps_in.at[:, pl.ds(i * width, width)], kv.at[pl.ds(i * count, count)])
    load("slope_state", slope_state_in, kv.at[pl.ds(3 * count, count)])
    group = [m for m in bits_of(at.parts) if m != 2]
    held_cols = every
    first = 0
    for number, mask in enumerate(reversed(group)):
        held_cols = held_cols // 2
        sent = []
        for i, ref in enumerate((k_t, v_t)):
            copy = pltpu.make_async_remote_copy(
                src_ref=ref.at[:, pl.ds(held_cols, held_cols)],
                dst_ref=kv_land.at[i, :, pl.ds(first, held_cols)],
                send_sem=kv_send.at[number, i],
                recv_sem=kv_recv.at[number, i],
                device_id=at.tm_partner(mask),
                device_id_type=MESH,
            )
            copy.start()
            sent.append(copy)
        if number == 0:
            g_t[pl.ds(0, width)] = jnp.transpose(q_grad[...].astype(F32)).astype(BF16)
            advance(1, "qkv")
        for i, (ref, copy) in enumerate(zip((k_t, v_t), sent)):
            copy.wait()
            low = pl.ds(0, held_cols)
            total = ref[:, low].astype(F32) + kv_land[i, :, pl.ds(first, held_cols)].astype(F32)
            ref[:, low] = total.astype(BF16)
        first += held_cols
    own = pl.ds(0, count)
    for i, (ref, target) in enumerate(((k_t, q), (v_t, att_grad))):
        part = ref[:, own]
        g_t[pl.ds((i + 1) * width, width)] = part
        target[...] = jnp.transpose(part.astype(F32)).astype(BF16)
    need("out_own")
    out_swap.wait()
    load("normed1", normed1_in, normed1)
    vec[pl.ds(4, 1)] = jnp.sum(q_grad[...].astype(F32), axis=0, keepdims=True)
    vec[pl.ds(5, 1)] = jnp.sum(att_grad[...].astype(F32), axis=0, keepdims=True)
    need("normed1")
    qkv = [(3 * share, rows_from(g_t, 0, 3 * share), whole(normed1))]
    give("qkv", plan["qkv"][0], qkv)
    advance(1, "qkv")
    need("wqkv", "block_input_again", "slope_state")
    tile = 128

    def norm_rows(i, carry):
        r = pl.ds(aligned(i, tile), tile)
        grad = mat(q_grad[r], arena[pl.ds(0, width)])
        grad = grad + mat(q[r], arena[pl.ds(width, width)])
        grad = grad + mat(att_grad[r], arena[pl.ds(2 * width, width)])
        unit, scale = norm_parts(block_input[r])
        vec[pl.ds(2, 1)] += jnp.sum(grad * unit, axis=0, keepdims=True)
        vec[pl.ds(3, 1)] += jnp.sum(grad, axis=0, keepdims=True)
        total = middle[r] + norm_back(grad, unit, scale, vecs[pl.ds(2, 1)])
        slope = kv[pl.ds(aligned(i, tile) + 3 * count, tile)].astype(F32)
        state_grad[r] = (total * slope).astype(BF16)
        return carry

    lax.fori_loop(0, count // tile, norm_rows, 0)
    vec[pl.ds(1, 1)] = jnp.sum(state_grad[...].astype(F32), axis=0, keepdims=True)
    take("qkv", plan["qkv"][0], qkv)
    advance(1, "conv2")
    cot_t[...] = jnp.transpose(state_grad[...].astype(F32)).astype(BF16)
    need("taps0", "taps1", "taps2")
    conv2 = [(share, rows_from(cot_t, 0, share), block_of(kv, i, count)) for i in range(3)]
    give("conv2", plan["conv2"][0], conv2)
    advance(1, "conv2")
    need("w2_0", "w2_1", "w2_2", "w1", "slope_even", "slope_odd")
    prev[...] = mat(state_grad[...], weights[0])
    for s in range(2):
        r = pl.ds(s * states, states)
        even = mat(state_grad[r], weights[1])
        even_grad[r] = (even * normed2[r].astype(F32)).astype(BF16)
        odd = mat(state_grad[r], weights[2])
        place = lax.broadcasted_iota(jnp.int32, (states, width), 0)
        moved = pltpu.roll(prev[r], states - 1, 0)
        odd = odd + jnp.where(place < states - 1, moved, 0.0)
        r_odd = pl.ds(s * size, states)
        odd_grad[r_odd] = (odd * slope_odd[r_odd].astype(F32)).astype(BF16)
        r_edge = pl.ds(s * size + states, TILE)
        edge = jnp.broadcast_to(prev[pl.ds(s * states, 1)], (TILE, width))
        odd_grad[r_edge] = (edge * slope_odd[r_edge].astype(F32)).astype(BF16)
    take("conv2", plan["conv2"][0], conv2)
    advance(1, "conv1")
    need("x_even", "x_odd")
    vec[pl.ds(0, 1)] = jnp.sum(even_grad[...].astype(F32), axis=0, keepdims=True) + jnp.sum(
        odd_grad[...].astype(F32), axis=0, keepdims=True
    )
    vec_copy = pltpu.make_async_remote_copy(
        src_ref=vec,
        dst_ref=vec_got,
        send_sem=core_send.at[len(copies)],
        recv_sem=core_recv.at[len(copies)],
        device_id=core_partner,
        device_id_type=MESH,
    )
    vec_copy.start()
    conv1 = mat_l(even_grad[...], x_even[...]) + mat_l(odd_grad[...], x_odd[...])
    conv1_t[...] = conv1.astype(BF16)
    cols = conv1.shape[1]
    half = share // 2
    ring_slot = turn[0] % len(ring)
    if ring[ring_slot] is not None:
        ring[ring_slot].wait_send()
    conv1_copies = []
    first = plan["conv1"][0]

    def conv1_rows(part):
        low = conv1_t[pl.ds(pl.multiple_of(part * share, TILE), half)]
        high = conv1_t[pl.ds(pl.multiple_of(part * share + half, TILE), half)]
        return jnp.concatenate([low, high], axis=1)

    for y in range(at.y_size):
        stage[ring_slot, pl.ds(y * half, half)] = conv1_rows(2 * y + 1 - core)
        number = len(copies) + 1 + y
        copy = pltpu.make_async_remote_copy(
            src_ref=stage.at[ring_slot, pl.ds(y * half, half)],
            dst_ref=held.at[y, pl.ds(first, half)],
            send_sem=core_send.at[number],
            recv_sem=core_recv.at[number],
            device_id=core_partner,
            device_id_type=MESH,
        )
        copy.start()
        conv1_copies.append(copy)
    for y, copy in enumerate(conv1_copies):
        copy.wait_recv()
        place = pl.ds(first, half)
        total = conv1_rows(2 * y + core).astype(F32) + held[y, place].astype(F32)
        held[y, place] = total.astype(BF16)
    vec_copy.wait()
    total = (vec[...] + vec_got[...]).astype(BF16)
    for y in range(at.y_size):
        held[y, pl.ds(plan["vec"][0], TILE)] = total
    advance(1, "last")
    for s in range(2):
        even = mat(even_grad[pl.ds(s * states, states)], w1[...])
        even = jnp.concatenate([even, jnp.zeros((TILE, cols), F32)], axis=0)
        odd = mat(odd_grad[pl.ds(s * size, size)], w1[...])
        one, two, three = [slice(i * LANES, (i + 1) * LANES) for i in range(3)]
        mel_v[s, :, one] = even[:, two] + odd[:, one] + pltpu.roll(odd[:, three], 1, 0)
        mel_v[s, :, two] = pltpu.roll(even[:, one], size - 1, 0) + even[:, three] + odd[:, two]
    swap = pltpu.make_async_remote_copy(
        src_ref=mel_v.at[1 - mine],
        dst_ref=mel_out.at[mine],
        send_sem=kv_send.at[len(group), 0],
        recv_sem=kv_recv.at[len(group), 0],
        device_id=at.tm_partner(2),
        device_id_type=MESH,
    )
    swap.start()
    keep_mel = pltpu.make_async_copy(mel_v.at[mine], mel_out.at[mine], load_sem.at[len(loads)])
    keep_mel.start()
    advance(0, "end")
    for copy in ring:
        if copy is not None and copy is not ring[ring_slot]:
            copy.wait_send()
    for copy in conv1_copies:
        copy.wait_send()
    swap.wait()
    keep_mel.wait()
    reducer.close()


def back(operands, parts, clips):
    q, k, wfc1, w1, inv, slope_odd, x_even, x_odd = [operands[i] for i in (5, 6, 3, 12, 8, 17, 19, 20)]
    count, width = q.shape
    every = k.shape[0]
    hidden = wfc1.shape[0]
    states = count // 2
    size = states + TILE
    y_size = parts // 2
    plan, plane, rows, total = back_plan(parts, clips, width, hidden)
    big = max(hidden // parts, 3 * (width // parts))
    scratch = [
        ((y_size, total, width), BF16),
        ((3, big, width), BF16),
        ((3 * width, width), BF16),
        ((4, width, width), BF16),
        (w1.shape, BF16),
        ((max(hidden, 3 * width), count), BF16),
        ((width, count), BF16),
        ((width, count), BF16),
        ((count, width), BF16),
        ((count, width), BF16),
        ((count, width), BF16),
        ((count, width), BF16),
        ((max(2 * every, 4 * count), width), BF16),
        (inv.shape, F32),
        ((count, width), BF16),
        ((count, width), F32),
        ((count, width), F32),
        (slope_odd.shape, BF16),
        (x_even.shape, BF16),
        (x_odd.shape, BF16),
        ((TILE, width), F32),
        ((TILE, width), F32),
        ((TILE, width), F32),
        ((2, count, every), BF16),
        ((count, every), BF16),
        ((LANES, count), BF16),
        ((width, every), BF16),
        ((width, every), BF16),
        ((2, width, every - count), BF16),
        ((count, width), BF16),
        ((count, width), BF16),
        ((count, width), F32),
        ((count, width), F32),
        ((count, width), BF16),
        ((2 * size, width), BF16),
        ((width, x_even.shape[1]), BF16),
        ((2, size, 2 * LANES), F32),
    ]
    scratch = [pltpu.VMEM(s, d) for s, d in scratch]
    groups = len(bits_of(parts)) - 1
    scratch += [
        pltpu.SemaphoreType.DMA(((6 + hidden // width) * y_size + 1,)),
        pltpu.SemaphoreType.DMA(((6 + hidden // width) * y_size + 1,)),
        pltpu.SemaphoreType.DMA((groups + 2, 2)),
        pltpu.SemaphoreType.DMA((groups + 2, 2)),
        pltpu.SemaphoreType.DMA((32 + 2 * (hidden // width),)),
        pltpu.SemaphoreType.DMA((2,)),
        pltpu.SemaphoreType.DMA((total // rows,)),
    ]
    scratch += Reducer.scratch(y_size, plane, total // rows, rows, width)
    return pl.pallas_call(
        functools.partial(back_kernel, plan, rows),
        out_shape=[
            jax.ShapeDtypeStruct((total, width), BF16),
            jax.ShapeDtypeStruct((2, size, 2 * LANES), F32),
            jax.ShapeDtypeStruct((2, states, width), BF16),
        ],
        in_specs=[ANY] * len(operands),
        out_specs=[ANY] * 3,
        scratch_shapes=scratch,
        compiler_params=pltpu.CompilerParams(
            collective_id=3, has_side_effects=True, vmem_limit_bytes=64 << 20
        ),
        name="back",
    )(*operands)


def per_device(
    mel_frames,
    lengths,
    conv1_weight,
    conv1_bias,
    conv2_weight,
    conv2_bias,
    ln1_gain,
    ln1_bias,
    qkv_weight,
    q_bias,
    v_bias,
    out_weight,
    out_bias,
    ln2_gain,
    ln2_bias,
    fc1_weight,
    fc1_bias,
    fc2_weight,
    fc2_bias,
    cotangent,
):
    parts = lax.axis_size("tm")
    place = lax.axis_index("tm")
    clips = lax.axis_size("clip")
    y_size = parts // 2
    core, y_place = place % 2, place // 2
    mine = y_place % 2
    frames, mels = mel_frames.shape[1:]
    states, width = cotangent.shape[1:]
    hidden = fc1_weight.shape[1] * parts
    rows = 2 * states
    share = conv1_bias.shape[0]
    size = states + TILE

    w1_own = jnp.pad(conv1_weight, ((0, 0), (0, LANES - mels), (0, 0))).reshape(3 * LANES, share).T
    w2_own = conv2_weight.reshape(3 * width, share).T
    vec_list = [
        conv1_bias, conv2_bias, ln1_gain, ln1_bias, q_bias, v_bias, out_bias, ln2_gain, ln2_bias,
        fc2_bias,
    ]
    vec_list = vec_list + [fc1_bias[i : i + share] for i in range(0, fc1_bias.shape[0], share)]
    vec_count = len(vec_list)
    vec_row = jnp.arange(TILE)[:, None]
    vec_own = jnp.zeros((TILE, share), BF16)
    for i, member in enumerate(vec_list):
        vec_own = jnp.where(vec_row == i, member[None], vec_own)
    vec_own = jnp.pad(vec_own, ((0, 0), (0, -share % LANES)))

    frame_ids = place * frames + jnp.arange(frames)
    frame_valid = (frame_ids[None, :] < lengths[:, None])[..., None]
    masked = jnp.where(frame_valid, mel_frames, jnp.zeros_like(mel_frames))
    masked = jnp.pad(masked.reshape(2, states, 2, mels), ((0, 0), (0, 0), (0, 0), (0, LANES - mels)))
    masked = masked.reshape(2, states, 2 * LANES)

    length = jnp.where(mine == 0, lengths[0], lengths[1])
    group = [m for m in bits_of(parts) if m != 2]
    segs = [4 * ((place ^ m) // 4) + 2 * jnp.arange(2) + (place ^ m) % 2 for m in combos(group)]
    segs = jnp.concatenate(segs)
    key_ids = (segs[:, None] * states + jnp.arange(states)[None, :]).reshape(1, -1)
    bias = jnp.where(2 * key_ids < length, 0.0, -1e30).astype(F32)
    owns = (
        w1_own, vec_own, w2_own, qkv_weight.T, out_weight.T, fc1_weight.T, fc2_weight.T,
    )
    table = jnp.asarray(positions(states * parts, width))
    (
        w1, w2, wqkv, vecs, state_taps, x_even, x_odd, slope_even, slope_odd, state_slope,
        block_input, normed1, queries, keys, values, attended, inverse, wout, wfc1, wfc2, exponents,
    ) = fore(masked, owns, table, bias, parts, y_size)
    summed, mel_back, out_states = back(
        (
            cotangent, attended, wout, wfc1, wfc2, queries, keys, values, inverse, exponents, wqkv, w2, w1,
            normed1, block_input, state_slope, slope_even, slope_odd, state_taps, x_even, x_odd, vecs,
        ),
        parts,
        clips,
    )
    plan = back_plan(parts, clips, width, hidden)[0]

    def rows_of(name):
        first, count = plan[name]
        return summed[first : first + count].astype(F32)

    fc2_sum = rows_of("fc2").reshape(hidden // width, share, width)
    fc2_sum = jnp.swapaxes(fc2_sum, 1, 2).reshape(hidden, share)
    conv2_sum = jnp.swapaxes(rows_of("conv2").reshape(3, share, width), 1, 2)
    conv1_sum = rows_of("conv1")
    conv1_sum = jnp.concatenate([conv1_sum[:, : 3 * LANES], conv1_sum[:, 3 * LANES :]], axis=0)
    conv1_sum = conv1_sum.T.reshape(3, LANES, share)[:, :mels]
    all_vec = rows_of("vec")
    vec_sum = lax.dynamic_slice_in_dim(all_vec, place * share, share, axis=1)
    bfc1_sum = lax.dynamic_slice_in_dim(
        all_vec[10:vec_count].reshape(-1), place * (hidden // parts), hidden // parts
    )

    up = [(i, i + 1) for i in range(parts - 1)]
    down = [(j, i) for i, j in up]
    from_before = lax.ppermute(mel_back[:, states], "tm", up)
    from_after = lax.ppermute(mel_back[:, size - 1], "tm", down)
    mel_back = mel_back[:, :states].at[:, 0].add(from_before).at[:, -1].add(from_after)
    mel_back = mel_back.reshape(2, states, 2, LANES)[..., :mels].reshape(2, frames, mels)
    mel_grad = jnp.where(frame_valid, mel_back, 0.0).astype(BF16)

    return (
        out_states,
        mel_grad,
        conv1_sum,
        vec_sum[0],
        conv2_sum,
        vec_sum[1],
        vec_sum[2],
        vec_sum[3],
        rows_of("qkv").T,
        vec_sum[4],
        vec_sum[5],
        rows_of("out").T,
        vec_sum[6],
        vec_sum[7],
        vec_sum[8],
        rows_of("fc1").T,
        bfc1_sum,
        fc2_sum,
        vec_sum[9],
    )


def solution(mesh):
    return jax.shard_map(
        per_device,
        mesh=mesh,
        in_specs=(
            P("clip", "tm", None),
            P("clip"),
            P(None, None, "tm"),
            P("tm"),
            P(None, None, "tm"),
            P("tm"),
            P("tm"),
            P("tm"),
            P(None, "tm"),
            P("tm"),
            P("tm"),
            P(None, "tm"),
            P("tm"),
            P("tm"),
            P("tm"),
            P(None, "tm"),
            P("tm"),
            P(None, "tm"),
            P("tm"),
            P("clip", "tm", None),
        ),
        out_specs=(
            P("clip", "tm", None),
            P("clip", "tm", None),
            P(None, None, "tm"),
            P("tm"),
            P(None, None, "tm"),
            P("tm"),
            P("tm"),
            P("tm"),
            P(None, "tm"),
            P("tm"),
            P("tm"),
            P(None, "tm"),
            P("tm"),
            P("tm"),
            P("tm"),
            P(None, "tm"),
            P("tm"),
            P(None, "tm"),
            P("tm"),
        ),
        check_vma=False,
    )
```

```python
import functools
import math

import jax
import jax.numpy as jnp
import numpy as np
from jax import lax
from jax.experimental import pallas as pl
from jax.experimental.pallas import tpu as pltpu
from jax.sharding import PartitionSpec as P

HEADS = 12
HEAD_DIM = 64
F32 = jnp.float32
BF16 = jnp.bfloat16
SCALE = 1.0 / math.sqrt(HEAD_DIM)
TILE = 16
LANES = 128
MESH = pl.DeviceIdType.MESH
ANY = pl.BlockSpec(memory_space=pl.ANY)
VMEM = pl.BlockSpec(memory_space=pltpu.VMEM)


def xor_swap(array, axis, mask):
    size = lax.axis_size(axis)
    return lax.ppermute(array, axis, [(i, i ^ mask) for i in range(size)])


def pick(array, index, axis=0):
    return lax.dynamic_index_in_dim(array, index, axis=axis, keepdims=False)


def bits_of(size):
    return [1 << b for b in range(size.bit_length() - 1)]


def combos(masks):
    found = [0]
    for mask in masks:
        found = found + [m ^ mask for m in found]
    return found


def flip(index, mask):
    return index + mask * (1 - 2 * ((index // mask) % 2))


def flip_all(index, mask):
    for bit in bits_of(2 * mask) if mask else []:
        if mask & bit:
            index = flip(index, bit)
    return index


def gelu_pair(v):
    a = jnp.abs(v) * (1.0 / math.sqrt(2.0))
    t = 1.0 / (1.0 + 0.3275911 * a)
    poly = t * (
        0.254829592
        + t * (-0.284496736 + t * (1.421413741 + t * (-1.453152027 + t * 1.061405429)))
    )
    bell = jnp.exp(-0.5 * v * v)
    tail = 0.5 * poly * bell
    cdf = jnp.where(v >= 0, 1.0 - tail, tail)
    return v * cdf, cdf + v * bell * (1.0 / math.sqrt(2.0 * math.pi))


def norm_parts(v):
    center = v - jnp.mean(v, axis=-1, keepdims=True)
    spread = jnp.mean(center * center, axis=-1, keepdims=True)
    scale = lax.rsqrt(spread + 1e-05)
    return center * scale, scale


def norm_back(grad, unit, scale, gain):
    a = grad * gain
    mean_a = jnp.mean(a, axis=-1, keepdims=True)
    mean_an = jnp.mean(a * unit, axis=-1, keepdims=True)
    return (a - mean_a - unit * mean_an) * scale


def positions(count, width):
    half = width // 2
    rates = np.exp(-(math.log(10000.0) / (half - 1)) * np.arange(half))
    angles = np.arange(count)[:, None] * rates[None, :]
    return np.concatenate([np.sin(angles), np.cos(angles)], axis=1).astype(np.float32)


def mat(a, b):
    return jnp.dot(a, b, preferred_element_type=F32)


def mat_t(a, b):
    return lax.dot_general(a, b, (((1,), (1,)), ((), ())), preferred_element_type=F32)


def mat_l(a, b):
    return lax.dot_general(a, b, (((0,), (0,)), ((), ())), preferred_element_type=F32)


def aligned(index, step):
    return pl.multiple_of(index * step, step)


class Place:
    def __init__(self):
        self.parts = lax.axis_size("tm")
        self.clips = lax.axis_size("clip")
        self.tm = lax.axis_index("tm")
        self.cl = lax.axis_index("clip")
        self.y_size = self.parts // 2
        self.x_size = self.y_size
        self.z_size = self.clips // self.x_size
        self.core = self.tm % 2
        self.y = self.tm // 2
        self.x = self.cl % self.x_size
        self.z = self.cl // self.x_size

    def tm_partner(self, mask):
        return {"tm": flip(self.tm, mask)}

    def clip_partner(self, mask):
        return {"clip": flip(self.cl, mask)}


def greet(partners):
    barrier = pltpu.get_barrier_semaphore()
    for partner in partners:
        pl.semaphore_signal(barrier, inc=1, device_id=partner, device_id_type=MESH)
    pl.semaphore_wait(barrier, len(partners))


class Gather:
    def __init__(self, at, own, full, first, count, sends, receives, base):
        self.at, self.own, self.full = at, own, full
        self.first, self.count = first, count
        self.shard = own.shape[0]
        self.split = 4 if count % (4 * TILE) == 0 and at.x_size > 1 and at.z_size > 1 else 1
        self.sends, self.receives, self.base = sends, receives, base
        self.used = 0
        self.y_masks = [2 * b for b in bits_of(at.y_size)]
        self.own_y, self.late_y, self.sides = [], [], []
        self.core_copies, self.started = [], []

    @staticmethod
    def slots(parts):
        return 8 * (parts // 2 - 1) + 1

    def region(self, mask, part):
        rows = self.count // self.split
        index = flip_all(self.at.tm, mask) * self.shard + self.first
        if part is not None:
            index = index + part * rows
        else:
            rows = self.count
        return pl.ds(pl.multiple_of(index, TILE), rows)

    def send(self, source, region, partner):
        slot = self.base + self.used
        self.used += 1
        copy = pltpu.make_async_remote_copy(
            src_ref=source,
            dst_ref=self.full.at[region],
            send_sem=self.sends.at[slot],
            recv_sem=self.receives.at[slot],
            device_id=partner,
            device_id_type=MESH,
        )
        copy.start()
        self.started.append(copy)
        return copy

    def part(self, q):
        if self.split == 1:
            return 0
        x, z = self.at.x % 2, self.at.z % 2
        x = 1 - x if q & 1 else x
        z = 1 - z if q & 2 else z
        return x + 2 * z

    def own_part(self, q):
        rows = self.count // self.split
        return self.own.at[pl.ds(pl.multiple_of(self.first + self.part(q) * rows, TILE), rows)]

    def start(self):
        at = self.at
        mask = self.y_masks[0]
        for q, pending in ((0, self.own_y), (3, self.late_y))[: 1 if self.split == 1 else 2]:
            copy = self.send(self.own_part(q), self.region(0, self.part(q)), at.tm_partner(mask))
            pending.append((copy, mask))
        whole = self.own.at[pl.ds(self.first, self.count)]
        self.core_copies.append(self.send(whole, self.region(0, None), at.tm_partner(1)))

    def relay(self, mask, part):
        region = self.region(mask, part)
        self.core_copies.append(self.send(self.full.at[region], region, self.at.tm_partner(1)))

    def over_y(self, pending, q):
        have = []
        for i, mask in enumerate(self.y_masks):
            for copy, m in pending:
                copy.wait_recv()
                have.append(m)
            pending = []
            if i + 1 < len(self.y_masks):
                after = self.y_masks[i + 1]
                for m in [0] + have:
                    region = self.region(m, self.part(q))
                    source = self.full.at[region] if m else self.own_part(q)
                    copy = self.send(source, region, self.at.tm_partner(after))
                    pending.append((copy, m ^ after))
        return have

    def on_y(self):
        at = self.at
        have = self.over_y(self.own_y, 0)
        for m in have:
            region = self.region(m, self.part(0))
            if self.split > 1:
                for q, mask in ((1, 1), (2, at.x_size)):
                    copy = self.send(self.full.at[region], region, at.clip_partner(mask))
                    self.sides.append((copy, m, q))
        for m in have:
            self.relay(m, self.part(0))

    def on_x(self):
        if self.split > 1:
            for m in self.over_y(self.late_y, 3):
                self.relay(m, self.part(3))
        for copy, m, q in self.sides:
            copy.wait_recv()
            self.relay(m, self.part(q))

    def finish(self):
        for copy in self.core_copies:
            copy.wait_recv()

    def close(self):
        for copy in self.started:
            copy.wait_send()


def fore_kernel(states, *refs):
    (
        mel_in, w1_own, vec_own, w2_own, wqkv_own, wout_own, wfc1_own, wfc2_own, pos_in,
        bias,
        w1_out, w2_out, wqkv_out, vecs_out, taps_out, x_even_out, x_odd_out, slope_even_out,
        slope_odd_out, slope_state_out, block_input_out, normed_out, queries_out, keys_out,
        values_out, attended_out, inverse_out, wout, wfc1, wfc2, expo,
        w1, vec_raw, vecs, w2, wqkv, taps, x_even, x_odd, slope_even, slope_odd, slope_state,
        block_input, normed, queries, keys, values, attended, inverse,
        mel, beside, edges, odd_act, tmp, pos, buffer, own_out, own_fc1, own_fc2,
        sends, receives, kv_send, kv_recv, mel_send, mel_recv, local, out_sem, expo_sem,
    ) = refs
    at = Place()
    width = block_input.shape[1]
    rows = 2 * states
    size = states + TILE
    block = 256
    mine = at.y % 2
    seg = [4 * (at.tm // 4) + 2 * s + at.core for s in range(2)]
    right = {"tm": (at.tm + 1) % at.parts}
    left = {"tm": (at.tm + at.parts - 1) % at.parts}
    partners = [at.tm_partner(m) for m in bits_of(at.parts)] + [right, left]
    partners += [at.clip_partner(m) for m in bits_of(2 * at.x_size)]

    loads = {}

    def load(name, src, dst):
        loads[name] = pltpu.make_async_copy(src, dst, local.at[len(loads)])
        loads[name].start()

    def place_of(own):
        return pl.ds(aligned(at.tm, own.shape[0]), own.shape[0])

    kept = []

    def keep(src, dst):
        kept.append(pltpu.make_async_copy(src, dst, out_sem.at[len(kept)]))
        kept[-1].start()

    load("mel", mel_in.at[mine], mel.at[mine])
    for name, own, full in (
        ("w1", w1_own, w1), ("vec", vec_own, vec_raw), ("w2", w2_own, w2), ("wqkv", wqkv_own, wqkv),
    ):
        load(name, own, full.at[place_of(own)])
    through = (("wout", wout_own, own_out), ("wfc1", wfc1_own, own_fc1), ("wfc2", wfc2_own, own_fc2))
    for name, own, stop in through:
        load(name, own, stop)
    for s in range(2):
        from_table = pos_in.at[pl.ds(aligned(seg[s], states), states)]
        load("pos%d" % s, from_table, pos.at[pl.ds(s * states, states)])
    greet(partners)

    def send(src, dst, slot, partner):
        copy = pltpu.make_async_remote_copy(
            src_ref=src,
            dst_ref=dst,
            send_sem=mel_send.at[slot],
            recv_sem=mel_recv.at[slot],
            device_id=partner,
            device_id_type=MESH,
        )
        copy.start()
        return copy

    to_right = send(mel_in.at[:, pl.ds(states - TILE, TILE)], beside.at[0], 0, right)
    to_left = send(mel_in.at[:, pl.ds(0, TILE)], beside.at[1], 1, left)
    swap = send(mel_in.at[1 - mine], mel.at[mine], 2, at.tm_partner(2))
    base = 0
    groups = {}
    for name, own, full, pieces in (
        ("w1", w1_own, w1, 1), ("vec", vec_own, vec_raw, 1), ("w2", w2_own, w2, 1),
        ("qkv", wqkv_own, wqkv, 3), ("out", wout_own, wout, 1), ("fc1", wfc1_own, wfc1, 2),
        ("fc2", wfc2_own, wfc2, 1),
    ):
        whole = own.shape[0]
        count = whole // pieces if whole % (pieces * TILE * 4) == 0 else whole
        groups[name] = []
        for first in range(0, whole, count):
            g = Gather(at, own, full, first, count, sends, receives, base)
            base += Gather.slots(at.parts)
            groups[name].append(g)

    def part(name, i):
        return groups[name][i : i + 1]

    def run(what, *pieces):
        for piece in pieces:
            for g in piece:
                getattr(g, what)()

    def finish(*names):
        for name in names:
            run("finish", groups[name])

    run("start", groups["w1"], groups["vec"], groups["w2"])
    to_right.wait_recv()
    to_left.wait_recv()
    forward = [
        send(beside.at[i, 1 - mine], edges.at[mine, i], 3 + i, at.tm_partner(2)) for i in range(2)
    ]
    for i in range(2):
        edges[mine, i] = beside[i, mine]
    swap.wait_recv()
    loads["mel"].wait()
    for copy in forward:
        copy.wait_recv()
    for s in range(2):
        row = lax.broadcasted_iota(jnp.int32, (TILE, 2 * LANES), 0)
        has_before = jnp.minimum(seg[s], 1).astype(F32)
        has_after = jnp.minimum(at.parts - 1 - seg[s], 1).astype(F32)
        tail = jnp.where(row == 0, edges[s, 1].astype(F32) * has_after, 0.0)
        tail = jnp.where(row == TILE - 1, edges[s, 0].astype(F32) * has_before, tail)
        m = jnp.concatenate([mel[s].astype(F32), tail], axis=0)
        before = pltpu.roll(m, 1, 0)
        after = pltpu.roll(m, size - 1, 0)
        low = pl.ds(0, LANES)
        even_rows = pl.ds(s * states, states)
        odd_rows = pl.ds(s * size, size)
        x_even[even_rows, low] = before[:states, LANES:].astype(BF16)
        x_even[even_rows, pl.ds(LANES, 2 * LANES)] = m[:states].astype(BF16)
        x_odd[odd_rows, pl.ds(0, 2 * LANES)] = m.astype(BF16)
        x_odd[odd_rows, pl.ds(2 * LANES, LANES)] = after[:, :LANES].astype(BF16)
    keep(x_even, x_even_out)
    keep(x_odd, x_odd_out)
    for (name, own, stop), full in zip(through, (wout, wfc1, wfc2)):
        loads[name].wait()
        keep(stop, full.at[place_of(own)])
    run("on_y", groups["w1"], groups["vec"])
    run("on_x", groups["w1"], groups["vec"])
    run("on_y", groups["w2"])
    run("start", part("qkv", 0))
    finish("w1", "vec")
    loads["w1"].wait()
    loads["vec"].wait()
    keep(w1, w1_out)
    total = jnp.zeros(vecs.shape, F32)
    share = width // at.parts
    for j in range(at.parts):
        piece = vec_raw[pl.ds(j * TILE, TILE)].astype(F32)
        low = (j * share) // LANES * LANES
        cells = [piece]
        if low > 0:
            cells = [jnp.zeros((TILE, low), F32)] + cells
        if width - low - piece.shape[1] > 0:
            cells = cells + [jnp.zeros((TILE, width - low - piece.shape[1]), F32)]
        placed = jnp.concatenate(cells, axis=1)
        shift = j * share - low
        total = total + (pltpu.roll(placed, shift, 1) if shift else placed)
    row = lax.broadcasted_iota(jnp.int32, vecs.shape, 0)
    total = jnp.where(row < 10, total, 0.0)
    pieces = wfc1_own.shape[0] // share
    for j in range(at.parts):
        for i in range(pieces):
            first = (j * pieces + i) * share
            piece = vec_raw[pl.ds(j * TILE, TILE)].astype(F32)[10 + i : 11 + i]
            column = first % width
            low = column // LANES * LANES
            cells = [piece]
            if low > 0:
                cells = [jnp.zeros((1, low), F32)] + cells
            if width - low - piece.shape[1] > 0:
                cells = cells + [jnp.zeros((1, width - low - piece.shape[1]), F32)]
            placed = jnp.broadcast_to(jnp.concatenate(cells, axis=1), vecs.shape)
            if column - low:
                placed = pltpu.roll(placed, column - low, 1)
            total = total + jnp.where(row == 10 + first // width, placed, 0.0)
    vecs[...] = total

    def vec(i, cols):
        return vecs[pl.ds(i, 1), cols]

    keep(vecs, vecs_out)
    between = [
        lambda: run("start", part("qkv", 1)),
        lambda: None,
        lambda: (run("on_x", groups["w2"]), run("on_y", part("qkv", 0)), run("start", part("qkv", 2))),
        lambda: (run("on_y", part("qkv", 1)), run("start", groups["out"], part("fc1", 0))),
    ]
    for s in range(2):

        def odd_columns(j, carry, s=s):
            cols = pl.ds(aligned(j, block), block)
            tmp[pl.ds(0, size)] = mat_t(x_odd[pl.ds(s * size, size)], w1[cols])

            def odd_rows(i, carry):
                r = pl.ds(aligned(i, 64), 64)
                act, slope = gelu_pair(tmp[r] + vec(0, cols))
                odd_act[r, cols] = act
                taps[pl.ds(aligned(i, 64) + s * states, 64), pl.ds(2 * width + aligned(j, block), block)] = act.astype(BF16)
                slope_odd[pl.ds(aligned(i, 64) + s * size, 64), cols] = slope.astype(BF16)
                return carry

            lax.fori_loop(0, states // 64, odd_rows, 0)
            r = pl.ds(states, TILE)
            act, slope = gelu_pair(tmp[r] + vec(0, cols))
            last = lax.broadcasted_iota(jnp.int32, act.shape, 0) == TILE - 1
            first = jnp.minimum(seg[s], 1).astype(F32)
            act = jnp.where(last, act * first, 0.0)
            slope = jnp.where(last, slope * first, 0.0)
            odd_act[r, cols] = act
            slope_odd[pl.ds(s * size + states, TILE), cols] = slope.astype(BF16)
            moved = pltpu.roll(odd_act[:, cols], 1, 0)
            taps[pl.ds(s * states, states), cols] = moved[:states].astype(BF16)
            return carry

        lax.fori_loop(0, width // block, odd_columns, 0)
        between[2 * s]()

        def even_columns(j, carry, s=s):
            cols = pl.ds(aligned(j, block), block)
            tmp[pl.ds(0, states)] = mat_t(x_even[pl.ds(s * states, states)], w1[cols])

            def even_rows(i, carry):
                r = pl.ds(aligned(i, 64), 64)
                act, slope = gelu_pair(tmp[r] + vec(0, cols))
                out = pl.ds(aligned(i, 64) + s * states, 64)
                taps[out, pl.ds(width + aligned(j, block), block)] = act.astype(BF16)
                slope_even[out, cols] = slope.astype(BF16)
                return carry

            lax.fori_loop(0, states // 64, even_rows, 0)
            return carry

        lax.fori_loop(0, width // block, even_columns, 0)
        between[2 * s + 1]()

    finish("w2")
    loads["w2"].wait()
    loads["pos0"].wait()
    loads["pos1"].wait()
    keep(w2, w2_out)
    keep(taps, taps_out)
    keep(slope_even, slope_even_out)
    keep(slope_odd, slope_odd_out)

    def state_columns(j, carry):
        cols = pl.ds(aligned(j, block), block)
        tmp[pl.ds(0, rows)] = mat_t(taps[...], w2[cols])

        def state_rows(i, carry):
            r = pl.ds(aligned(i, 64), 64)
            act, slope = gelu_pair(tmp[r] + vec(1, cols))
            block_input[r, cols] = act + pos[r, cols]
            slope_state[r, cols] = slope.astype(BF16)
            return carry

        lax.fori_loop(0, rows // 64, state_rows, 0)
        return carry

    third = width // block // 3
    lax.fori_loop(0, third, state_columns, 0)
    run("on_y", part("qkv", 2))
    run("start", part("fc1", 1))
    lax.fori_loop(third, 2 * third, state_columns, 0)
    run("on_x", part("qkv", 0))
    lax.fori_loop(2 * third, width // block, state_columns, 0)
    keep(block_input, block_input_out)
    keep(slope_state, slope_state_out)
    full = pl.ds(0, width)

    def norm_rows(i, carry):
        r = pl.ds(aligned(i, 32), 32)
        unit, _ = norm_parts(block_input[r])
        normed[r] = (unit * vec(2, full) + vec(3, full)).astype(BF16)
        return carry

    lax.fori_loop(0, rows // 32, norm_rows, 0)
    run("on_x", part("qkv", 1), part("qkv", 2))
    keep(normed, normed_out)
    finish("qkv")
    loads["wqkv"].wait()
    keep(wqkv, wqkv_out)
    group = [m for m in bits_of(at.parts) if m != 2]

    def exchange(array, base):
        held = rows
        for n, mask in enumerate(group):
            copy = pltpu.make_async_remote_copy(
                src_ref=array.at[pl.ds(0, held)],
                dst_ref=array.at[pl.ds(held, held)],
                send_sem=kv_send.at[base + n],
                recv_sem=kv_recv.at[base + n],
                device_id=at.tm_partner(mask),
                device_id_type=MESH,
            )
            copy.start()
            if n + 1 < len(group):
                copy.wait()
                held = 2 * held
            else:
                return copy

    def project(target, first, bias):
        def columns(j, carry):
            cols = pl.ds(aligned(j, block), block)
            part = mat_t(normed[...], wqkv[pl.ds(first + aligned(j, block), block)])
            if bias is not None:
                part = part + vec(bias, cols)
            target[pl.ds(0, rows), cols] = part.astype(BF16)
            return carry

        lax.fori_loop(0, width // block, columns, 0)

    project(keys, width, None)
    key_copy = exchange(keys, 1)
    run("on_y", groups["out"], part("fc1", 0))
    run("start", groups["fc2"])
    project(values, 2 * width, 5)
    value_copy = exchange(values, 1 + len(group))
    project(queries, 0, 4)
    keep(queries, queries_out)
    run("on_y", part("fc1", 1))
    run("on_x", groups["out"])
    key_copy.wait()
    value_copy.wait()
    keep(keys, keys_out)
    keep(values, values_out)
    q, k, v = queries, keys, values
    pairs = width // LANES
    inverse[...] = jnp.zeros(inverse.shape, F32)
    lane = lax.broadcasted_iota(jnp.int32, (rows, LANES), 1)

    def out_copy(p, h):
        return pltpu.make_async_copy(buffer.at[h], expo.at[2 * p + h], expo_sem.at[h])

    def pair_body(p, carry):
        cols = pl.ds(aligned(p, LANES), LANES)
        for h in range(2):

            @pl.when(p > 0)
            def _(h=h):
                out_copy(p - 1, h).wait()

        scaled = q[:, cols].astype(F32) * SCALE
        inv = inverse[...]
        outs = []
        scores = []
        for h in range(2):
            own = (lane < HEAD_DIM) if h == 0 else (lane >= HEAD_DIM)
            head = jnp.where(own, scaled, 0.0).astype(BF16)
            scores.append(mat_t(head, k[:, cols]) + bias[pl.ds(0, 1)])
        for h in range(2):
            largest = jnp.max(scores[h], axis=-1, keepdims=True)
            exponent = jnp.exp(scores[h] - largest)
            one = 1.0 / jnp.sum(exponent, axis=-1, keepdims=True)
            low = exponent.astype(BF16)
            buffer[h] = low
            outs.append(mat(low, v[:, cols]) * one)
            inv = jnp.where(lane == 2 * p + h, one, inv)
        attended[:, cols] = jnp.where(lane < HEAD_DIM, outs[0], outs[1]).astype(BF16)
        inverse[...] = inv
        for h in range(2):
            out_copy(p, h).start()
        return carry

    events = [
        ("on_x", part("fc1", 0)),
        ("on_y", groups["fc2"]),
        ("on_x", part("fc1", 1)),
        ("on_x", groups["fc2"]),
    ]
    for i, event in enumerate(events):
        lax.fori_loop(i * pairs // len(events), (i + 1) * pairs // len(events), pair_body, 0)
        run(*event)
    keep(attended, attended_out)
    keep(inverse, inverse_out)
    for h in range(2):
        out_copy(pairs - 1, h).wait()
    finish("out", "fc1", "fc2")
    for copy in [to_right, to_left, swap] + forward:
        copy.wait_send()
    for pieces in groups.values():
        run("close", pieces)
    for copy in kept:
        copy.wait()


def fore(mel, owns, pos, bias, parts):
    w1_own, vec_own, w2_own, wqkv_own, wout_own, wfc1_own, wfc2_own = owns
    states = mel.shape[1]
    rows, width = 2 * states, pos.shape[1]
    every = bias.shape[1]
    full = lambda own: ((parts * own.shape[0], own.shape[1]), BF16)
    both = [
        full(w1_own),
        full(w2_own),
        full(wqkv_own),
        ((TILE, width), F32),
        ((rows, 3 * width), BF16),
        ((rows, 3 * LANES), BF16),
        ((rows + 2 * TILE, 3 * LANES), BF16),
        ((rows, width), BF16),
        ((rows + 2 * TILE, width), BF16),
        ((rows, width), BF16),
        ((rows, width), F32),
        ((rows, width), BF16),
        ((rows, width), BF16),
        ((every, width), BF16),
        ((every, width), BF16),
        ((rows, width), BF16),
        ((rows, LANES), F32),
    ]
    shapes = both + [
        full(wout_own),
        full(wfc1_own),
        full(wfc2_own),
        ((width // HEAD_DIM, rows, every), BF16),
    ]
    here = [pltpu.VMEM(s, d) for s, d in both]
    vec_raw = pltpu.VMEM((parts * TILE, vec_own.shape[1]), BF16)
    here = [here[0], vec_raw, here[3], here[1], here[2]] + here[4:]
    slots = 12 * Gather.slots(parts)
    return pl.pallas_call(
        functools.partial(fore_kernel, states),
        out_shape=[jax.ShapeDtypeStruct(s, d) for s, d in shapes],
        in_specs=[ANY] * 9 + [VMEM],
        out_specs=[ANY] * len(shapes),
        scratch_shapes=here
        + [
            pltpu.VMEM(mel.shape, BF16),
            pltpu.VMEM((2, 2, TILE, 2 * LANES), BF16),
            pltpu.VMEM((2, 2, TILE, 2 * LANES), BF16),
            pltpu.VMEM((states + TILE, width), F32),
            pltpu.VMEM((max(rows, states + TILE), 256), F32),
            pltpu.VMEM((rows, width), F32),
            pltpu.VMEM((2, rows, every), BF16),
            pltpu.VMEM(wout_own.shape, BF16),
            pltpu.VMEM(wfc1_own.shape, BF16),
            pltpu.VMEM(wfc2_own.shape, BF16),
            pltpu.SemaphoreType.DMA((slots,)),
            pltpu.SemaphoreType.DMA((slots,)),
            pltpu.SemaphoreType.DMA((8,)),
            pltpu.SemaphoreType.DMA((8,)),
            pltpu.SemaphoreType.DMA((6,)),
            pltpu.SemaphoreType.DMA((6,)),
            pltpu.SemaphoreType.DMA((12,)),
            pltpu.SemaphoreType.DMA((len(both) + 4,)),
            pltpu.SemaphoreType.DMA((2,)),
        ],
        compiler_params=pltpu.CompilerParams(
            collective_id=1, has_side_effects=True, vmem_limit_bytes=62 << 20
        ),
        name="fore",
    )(mel, *owns, pos, bias)


class Reducer:
    def __init__(self, at, rows, ahead, held, result, landings, sends, receives, local):
        self.at, self.rows, self.ahead = at, rows, ahead
        self.source, self.result, self.landings = held, result, landings
        self.sends, self.receives, self.local = sends, receives, local
        self.chunks = result.shape[0] // rows
        self.y_bits = list(reversed(bits_of(at.y_size)))
        self.x_bits = bits_of(at.x_size)
        self.mine = [(at.x // b) % 2 for b in self.x_bits]
        self.x_partner = [at.clip_partner(b) for b in self.x_bits]
        self.others = range(1, at.z_size)
        self.y_partner = [at.tm_partner(2 * b) for b in self.y_bits]
        self.tops, self.depth = len(self.y_bits), len(self.x_bits)
        self.stages = self.tops + 2 * self.depth + 3
        self.delays = [0] + [ahead + s for s in range(self.stages - 1)]
        self.times = self.chunks + self.delays[-1]
        self.piece = (rows >> self.depth) // at.z_size

    @staticmethod
    def scratch(y_size, x_size, z_size, chunks, rows, width):
        shapes = [pltpu.VMEM((chunks, b, rows, width), BF16) for b in reversed(bits_of(y_size))]
        depth = len(bits_of(x_size))
        shapes += [pltpu.VMEM((chunks, rows >> (k + 1), width), BF16) for k in range(depth)]
        piece = (rows >> depth) // z_size
        shapes += [pltpu.VMEM((chunks, z_size - 1, piece, width), BF16)]
        slots = len(bits_of(y_size)) + 2 * depth + 2 * (z_size - 1)
        return shapes + [pltpu.SemaphoreType.DMA((chunks, slots))] * 2

    def z_place(self, d):
        return (self.at.z + d) % self.at.z_size

    def z_partner(self, d):
        return {"clip": self.at.x + self.at.x_size * self.z_place(d)}

    def partners(self):
        return self.y_partner + self.x_partner + [self.z_partner(d) for d in self.others]

    def remote(self, src, dst, c, slot, device):
        return pltpu.make_async_remote_copy(
            src_ref=src,
            dst_ref=dst,
            send_sem=self.sends.at[c, slot],
            recv_sem=self.receives.at[c, slot],
            device_id=device,
            device_id_type=MESH,
        )

    def chunk(self, c):
        return pl.ds(pl.multiple_of(c * self.rows, self.rows), self.rows)

    def y_copy(self, c, k):
        b = self.y_bits[k]
        away = b * (1 - (self.at.y // b) % 2)
        if k == 0:
            src = self.source.at[pl.ds(away, b), self.chunk(c)]
        else:
            src = self.landings[k - 1].at[c, pl.ds(away, b)]
        return self.remote(src, self.landings[k].at[c], c, k, self.y_partner[k])

    def half(self, k, bit):
        count = self.rows >> (k + 1)
        return pl.ds(aligned(bit, count), count)

    def current(self, k, c, region):
        if k == 0:
            return self.landings[self.tops - 1].at[c, 0, region]
        return self.landings[self.tops + k - 1].at[c, region]

    def spread(self, c, k):
        src = self.current(k, c, self.half(k, 1 - self.mine[k]))
        dst = self.landings[self.tops + k].at[c]
        return self.remote(src, dst, c, self.tops + k, self.x_partner[k])

    def z_rows(self, place):
        return pl.ds(aligned(place, self.piece), self.piece)

    def z_copy(self, c, d):
        src = self.current(self.depth, c, self.z_rows(self.z_place(d)))
        dst = self.landings[-1].at[c, d - 1]
        return self.remote(src, dst, c, self.tops + self.depth + d - 1, self.z_partner(d))

    def kept(self, c, k):
        first = c * self.rows
        for i in range(k + 1):
            first = first + self.mine[i] * (self.rows >> (i + 1))
        count = self.rows >> (k + 1)
        return pl.ds(pl.multiple_of(first, count), count)

    def finished(self, c):
        first = c * self.rows + self.at.z * self.piece
        for i in range(self.depth):
            first = first + self.mine[i] * (self.rows >> (i + 1))
        return pl.ds(pl.multiple_of(first, self.piece), self.piece)

    def own_rows(self, c):
        return self.current(self.depth, c, self.z_rows(self.at.z))

    def z_collect(self, c, d):
        slot = self.tops + self.depth + len(self.others) + d - 1
        region = self.result.at[self.finished(c)]
        return self.remote(self.own_rows(c), region, c, slot, self.z_partner(d))

    def keep(self, c):
        return pltpu.make_async_copy(
            self.own_rows(c), self.result.at[self.finished(c)], self.local.at[c]
        )

    def collect(self, c, k):
        region = self.result.at[self.kept(c, k)]
        slot = self.tops + self.depth + 2 * len(self.others) + k
        return self.remote(region, region, c, slot, self.x_partner[k])

    def run(self, stage, c):
        if stage == 0:
            self.y_copy(c, 0).start()
        elif stage <= self.tops:
            k = stage - 1
            b = self.y_bits[k]
            own = pl.ds(b * ((self.at.y // b) % 2), b)
            self.y_copy(c, k).wait_recv()
            mine = self.source[own, self.chunk(c)] if k == 0 else self.landings[k - 1][c, own]
            total = mine.astype(F32) + self.landings[k][c].astype(F32)
            self.landings[k][c] = total.astype(BF16)
            if k + 1 < self.tops:
                self.y_copy(c, k + 1).start()
            else:
                self.spread(c, 0).start()
        elif stage <= self.tops + self.depth:
            k = stage - self.tops - 1
            self.spread(c, k).wait_recv()
            mine = self.current(k, c, self.half(k, self.mine[k]))[...]
            total = mine.astype(F32) + self.landings[self.tops + k][c].astype(F32)
            self.landings[self.tops + k][c] = total.astype(BF16)
            if k + 1 < self.depth:
                self.spread(c, k + 1).start()
            else:
                for d in self.others:
                    self.z_copy(c, d).start()
        elif stage == self.tops + self.depth + 1:
            total = self.own_rows(c)[...].astype(F32)
            for d in self.others:
                self.z_copy(c, d).wait_recv()
                total = total + self.landings[-1][c, d - 1].astype(F32)
            self.own_rows(c)[...] = total.astype(BF16)
            self.keep(c).start()
            for d in self.others:
                self.z_collect(c, d).start()
        elif stage == self.tops + self.depth + 2:
            for d in self.others:
                self.z_collect(c, d).wait_recv()
            self.keep(c).wait()
            self.collect(c, self.depth - 1).start()
        else:
            k = self.depth - 1 - (stage - self.tops - self.depth - 3)
            self.collect(c, k).wait_recv()
            if k > 0:
                self.collect(c, k - 1).start()

    def step(self, time):
        for stage in range(self.stages):
            c = time - self.delays[stage]

            @pl.when((c >= 0) & (c < self.chunks))
            def _(stage=stage, c=c):
                self.run(stage, c)

    def steps(self, first, last):
        def body(time, carry):
            self.step(time)
            return carry

        lax.fori_loop(first, last, body, 0)

    def close(self):
        def body(c, carry):
            for k in range(self.tops):
                self.y_copy(c, k).wait_send()
            for k in range(self.depth):
                self.spread(c, k).wait_send()
                self.collect(c, k).wait_send()
            for d in self.others:
                self.z_copy(c, d).wait_send()
                self.z_collect(c, d).wait_send()
            return carry

        lax.fori_loop(0, self.chunks, body, 0)


AHEAD = 2


def tile_of(count):
    return max(t for t in range(TILE, 257, TILE) if count % t == 0)


def back_plan(parts, clips, width, hidden):
    share = width // parts
    plane = len(bits_of(parts // 2)) + len(bits_of(clips // (parts // 2)))
    rows = TILE << plane
    plan, first = {}, 0
    early = [("fc2", hidden // parts), ("fc1", hidden // parts), ("out", share)]
    late = [("qkv", 3 * share), ("conv2", 3 * share), ("conv1", share // 2), ("vec", TILE)]
    for group in (early, late):
        for name, count in group:
            plan[name] = (first, count)
            first += count
        plan["gap%d" % len(plan)] = (first, -first % rows)
        first += -first % rows
    plan["last"] = plan["more"] = plan["end"] = (first, 0)
    return plan, plane, rows, first


def back_kernel(plan, rows, *refs):
    (
        cot_in, attended_in, wout_in, wfc1_in, wfc2_in, q_in, k_in, v_in, inv_in, expo, wqkv_in,
        w2_in, w1_in, normed1_in, block_input_in, slope_state_in, slope_even_in, slope_odd_in,
        taps_in, x_even_in, x_odd_in, vecs_in,
        result, mel_out, states_out, fc1_out, fc2_out, out_out,
        held, stage, arena, weights, w1, g_t, cot_t, branch_t, normed2, attended, att_grad, q, kv,
        inv, normed1, block_input, middle, slope_odd, x_even, x_odd, vec, vec_got, vecs,
        ebuf, score_grad, q_t, k_t, v_t, kv_land, q_grad, state_grad, prev, tmp, even_grad, odd_grad,
        conv1_t, mel_v, mel_all, mel_side, mel_low, turned,
        core_send, core_recv, kv_send, kv_recv, load_sem, expo_sem, local, side_sem,
    ) = refs[: 28 + 49]
    *landings, sends, receives = refs[28 + 49 :]
    at = Place()
    width = q.shape[1]
    count = q.shape[0]
    states = count // 2
    size = states + TILE
    every = k_in.shape[0]
    hidden = wfc1_in.shape[0]
    share = width // at.parts
    core, mine = at.core, at.y % 2
    core_partner = at.tm_partner(1)

    loads = {}

    def load(name, src, dst):
        copy = pltpu.make_async_copy(src, dst, load_sem.at[len(loads)])
        copy.start()
        loads[name] = copy

    def need(*names):
        for name in names:
            loads[name].wait()

    blocks = hidden // width

    def load_block(i):
        low = pl.ds(i * width, width)
        load("fc1_%d" % i, wfc1_in.at[low], weights.at[i % 2])
        load("fc2_%d" % i, wfc2_in.at[:, low], weights.at[2 + i % 2])

    load("att", attended_in, attended)
    load("wout", wout_in, arena.at[pl.ds(0, width)])
    load("block_input", block_input_in, block_input)
    load("vecs", vecs_in, vecs)
    load_block(0)
    load_block(1)
    load("q", q_in, q)
    load("inv", inv_in, inv)
    load("k", k_in, kv.at[pl.ds(0, every)])
    load("v", v_in, kv.at[pl.ds(every, every)])
    load("w1", w1_in, w1)
    load("so", slope_odd_in, slope_odd)
    load("x_even", x_even_in, x_even)
    load("x_odd", x_odd_in, x_odd)

    def fetch(n, slot):
        return pltpu.make_async_copy(expo.at[n], ebuf.at[slot], expo_sem.at[slot])

    fetch(0, 0).start()
    reducer = Reducer(at, rows, AHEAD, held, result, landings, sends, receives, local)
    right = {"tm": (at.tm + 1) % at.parts}
    left = {"tm": (at.tm + at.parts - 1) % at.parts}
    greet([core_partner, right, left] + reducer.partners())
    place = pl.ds(pl.multiple_of(mine * states, states), states)
    cot_swap = pltpu.make_async_remote_copy(
        src_ref=cot_in.at[1 - mine],
        dst_ref=q_grad.at[place],
        send_sem=kv_send.at[len(bits_of(at.parts)) - 1, 1],
        recv_sem=kv_recv.at[len(bits_of(at.parts)) - 1, 1],
        device_id=at.tm_partner(2),
        device_id_type=MESH,
    )
    cot_swap.start()
    load("cot", cot_in.at[mine], q_grad.at[place])
    def send(src, dst, slot, device):
        copy = pltpu.make_async_remote_copy(
            src_ref=src,
            dst_ref=dst,
            send_sem=side_sem.at[0, slot],
            recv_sem=side_sem.at[1, slot],
            device_id=device,
            device_id_type=MESH,
        )
        copy.start()
        return copy

    done = [0]

    def advance(steps, ready):
        ready = ready if isinstance(ready, int) else plan[ready][0]
        limit = reducer.times if ready == reducer.chunks * rows else ready // rows
        last = max(done[0], min(done[0] + steps, limit))
        if steps == 0:
            last = reducer.times
        reducer.steps(done[0], last)
        done[0] = last
    for name, (first, n) in plan.items():
        if name.startswith("gap") and n:
            for y in range(at.y_size):
                held[y, pl.ds(first, n)] = jnp.zeros((n, width), BF16)

    copies = {}
    slots = {}
    ring = [None] * stage.shape[0]
    turn = [0]

    def give(name, first, parts, places=None):
        for y in places or range(at.y_size):
            slot = turn[0] % len(ring)
            turn[0] += 1
            if ring[slot] is not None:
                ring[slot].wait_send()
            offset = 0
            for n, rows_of, acts in parts:
                tile = tile_of(n)
                for i in range(n // tile):
                    g = rows_of(2 * y + 1 - core, i * tile, tile)
                    stage[slot, pl.ds(offset + i * tile, tile)] = mat(g, acts()).astype(BF16)
                offset += n
            number = len(copies)
            copy = pltpu.make_async_remote_copy(
                src_ref=stage.at[slot, pl.ds(0, offset)],
                dst_ref=held.at[y, pl.ds(first, offset)],
                send_sem=core_send.at[number],
                recv_sem=core_recv.at[number],
                device_id=core_partner,
                device_id_type=MESH,
            )
            copy.start()
            ring[slot] = copy
            copies[name, y] = copy

    def take(name, first, parts, places=None):
        for y in places or range(at.y_size):
            copies[name, y].wait_recv()
            offset = first
            for n, rows_of, acts in parts:
                tile = tile_of(n)
                for i in range(n // tile):
                    g = rows_of(2 * y + core, i * tile, tile)
                    place = pl.ds(offset + i * tile, tile)
                    total = mat(g, acts()) + held[y, place].astype(F32)
                    held[y, place] = total.astype(BF16)
                offset += n

    def rows_from(ref, base, n):
        def rows_of(part, offset, tile):
            return ref[pl.ds(pl.multiple_of(base + part * n + offset, TILE), tile)]

        return rows_of

    def whole(ref):
        return lambda: ref[...]

    def block_of(ref, i, n):
        return lambda: ref[pl.ds(i * n, n)]

    def vec_row(i):
        return vecs[pl.ds(i, 1)]

    tile = 64

    def over_rows(body):
        def run(i, carry):
            body(pl.ds(aligned(i, tile), tile))
            return carry

        lax.fori_loop(0, count // tile, run, 0)

    need("att", "wout", "block_input", "vecs")
    prev[...] = mat_t(attended[...], arena[pl.ds(0, width)])

    def middle_rows(r):
        total = block_input[r] + prev[r] + vec_row(6)
        middle[r] = total
        unit, _ = norm_parts(total)
        normed2[r] = (unit * vec_row(7) + vec_row(8)).astype(BF16)

    over_rows(middle_rows)
    vec[...] = jnp.zeros(vec.shape, F32)
    acts = (state_grad, even_grad)
    slope_hid = odd_grad.at[pl.ds(0, count)]
    per_y = 2 * (hidden // at.parts)
    group_blocks = per_y // width
    fc2, fc1 = [], []
    for i in range(blocks):
        fc2.append([(share, rows_from(cot_t, 0, share), whole(acts[i % 2]))])
    for y in range(at.y_size):
        fc1.append([(hidden // at.parts, rows_from(g_t, 0, hidden // at.parts), whole(normed2))])
    ready = 0
    for i in range(blocks):
        need("fc1_%d" % i, "fc2_%d" % i)
        up, down, act = weights.at[i % 2], weights.at[2 + i % 2], acts[i % 2]
        tmp[...] = mat_t(normed2[...], up[...])

        def hidden_rows(r, i=i, act=act):
            value, slope = gelu_pair(tmp[r] + vec_row(10 + i))
            act[r] = value.astype(BF16)
            slope_hid[r] = slope.astype(BF16)

        over_rows(hidden_rows)
        part = mat_t(act[...], down[...])
        prev[...] = part if i == 0 else prev[...] + part
        if i == 0:
            need("cot")
            cot_swap.wait()
            wide_cot = q_grad[...].astype(F32)
            vec[pl.ds(9, 1)] = jnp.sum(wide_cot, axis=0, keepdims=True)
            cot_t[...] = jnp.transpose(wide_cot).astype(BF16)
        tmp[...] = mat(q_grad[...], down[...])

        def hidden_back(r):
            slope_hid[r] = (tmp[r] * slope_hid[r].astype(F32)).astype(BF16)

        over_rows(hidden_back)
        part = mat(slope_hid[...], up[...])
        block_input[...] = part if i == 0 else block_input[...] + part
        wide = slope_hid[...].astype(F32)
        vec[pl.ds(10 + i, 1)] = jnp.sum(wide, axis=0, keepdims=True)
        g_t[pl.ds(i * width, width)] = jnp.transpose(wide).astype(BF16)
        if i + 2 < blocks:
            load_block(i + 2)
        give("fc2_%d" % i, plan["fc2"][0] + i * share, fc2[i])
        if i > 0:
            take("fc2_%d" % (i - 1), plan["fc2"][0] + (i - 1) * share, fc2[i - 1])
            ready = i * share
        if (i + 1) % group_blocks == 0:
            y = i // group_blocks
            give("fc1_%d" % y, plan["fc1"][0], fc1[y], [y])
        if i == blocks - 1:
            take("fc2_%d" % i, plan["fc2"][0] + i * share, fc2[i])
            ready = blocks * share
        advance(2, ready)

    def out_rows(r):
        total = middle[r] + prev[r] + vec_row(9)
        normed1[r] = total.astype(BF16)

    over_rows(out_rows)
    state_rows = [pl.ds(pl.multiple_of(m * states, states), states) for m in (mine, 1 - mine)]
    out_swap = send(normed1.at[state_rows[1]], states_out.at[mine], 1, at.tm_partner(2))
    load("out_own", normed1.at[state_rows[0]], states_out.at[mine])
    branch = odd_grad.at[pl.ds(0, count)]

    def middle_back(r):
        grad = block_input[r]
        unit, scale = norm_parts(middle[r])
        vec[pl.ds(7, 1)] += jnp.sum(grad * unit, axis=0, keepdims=True)
        vec[pl.ds(8, 1)] += jnp.sum(grad, axis=0, keepdims=True)
        total = q_grad[r].astype(F32) + norm_back(grad, unit, scale, vec_row(7))
        middle[r] = total
        low = total.astype(BF16)
        branch[r] = low

    over_rows(middle_back)
    load("again", block_input_in, block_input)
    wide = branch[...].astype(F32)
    vec[pl.ds(6, 1)] = jnp.sum(wide, axis=0, keepdims=True)
    branch_t[...] = jnp.transpose(wide).astype(BF16)
    att_grad[...] = mat(branch[...], arena[pl.ds(0, width)]).astype(BF16)
    load("wqkv", wqkv_in, arena.at[pl.ds(0, wqkv_in.shape[0])])
    for i in range(3):
        load("w2_%d" % i, w2_in.at[:, pl.ds(i * width, width)], weights.at[i])
    out = [(share, rows_from(branch_t, 0, share), whole(attended))]
    give("out", plan["out"][0], out)
    for y in range(at.y_size):
        take("fc1_%d" % y, plan["fc1"][0], fc1[y], [y])
    advance(1, "out")
    take("out", plan["out"][0], out)
    load("se", slope_even_in, normed2)
    need("q", "inv", "k", "v")

    pairs = width // LANES
    lane = lax.broadcasted_iota(jnp.int32, (count, LANES), 1)

    def pair_body(p, carry):
        cols = pl.ds(aligned(p, LANES), LANES)
        q_t[...] = jnp.transpose(q[:, cols].astype(F32)).astype(BF16)
        grads = []
        for h in range(2):
            n = 2 * p + h
            if h == 0:
                fetch(n + 1, 1).start()
            else:

                @pl.when(p < pairs - 1)
                def _(n=n):
                    fetch(n + 1, 0).start()

            fetch(n, h).wait()
            scale = jnp.sum(jnp.where(lane == n, inv[...], 0.0), axis=-1, keepdims=True)
            keep = (lane < HEAD_DIM) if h == 0 else (lane >= HEAD_DIM)
            grad = jnp.where(keep, att_grad[:, cols].astype(F32) * scale, 0.0).astype(BF16)
            wide = grad.astype(F32)
            dot = jnp.sum(wide * attended[:, cols].astype(F32), axis=-1, keepdims=True)
            grad_t = jnp.transpose(wide).astype(BF16)[HEAD_DIM * h : HEAD_DIM * (h + 1)]
            head = pl.ds(pl.multiple_of(p * LANES + h * HEAD_DIM, HEAD_DIM), HEAD_DIM)
            v_t[head, :] = mat(grad_t, ebuf[h]).astype(BF16)
            diff = mat_t(grad, kv[pl.ds(every, every), cols]) - dot
            score_grad[...] = (ebuf[h].astype(F32) * diff).astype(BF16)
            grads.append(mat(score_grad[...], kv[pl.ds(0, every), cols]) * SCALE)
            part = q_t[pl.ds(HEAD_DIM * h, HEAD_DIM)]
            k_t[head, :] = (mat(part, score_grad[...]) * SCALE).astype(BF16)
        q_grad[:, cols] = jnp.where(lane < HEAD_DIM, grads[0], grads[1]).astype(BF16)

        @pl.when(p < most)
        def _():
            reducer.step(done[0] + p)

        return carry

    most = min(pairs, plan["qkv"][0] // rows - done[0])
    lax.fori_loop(0, pairs, pair_body, 0)
    done[0] += most

    for i in range(3):
        load("taps%d" % i, taps_in.at[:, pl.ds(i * width, width)], kv.at[pl.ds(i * count, count)])
    load("ss", slope_state_in, kv.at[pl.ds(3 * count, count)])
    group = [m for m in bits_of(at.parts) if m != 2]
    held_cols = every
    first = 0
    for number, mask in enumerate(reversed(group)):
        held_cols = held_cols // 2
        sent = []
        for i, ref in enumerate((k_t, v_t)):
            copy = pltpu.make_async_remote_copy(
                src_ref=ref.at[:, pl.ds(held_cols, held_cols)],
                dst_ref=kv_land.at[i, :, pl.ds(first, held_cols)],
                send_sem=kv_send.at[number, i],
                recv_sem=kv_recv.at[number, i],
                device_id=at.tm_partner(mask),
                device_id_type=MESH,
            )
            copy.start()
            sent.append(copy)
        if number == 0:
            g_t[pl.ds(0, width)] = jnp.transpose(q_grad[...].astype(F32)).astype(BF16)
            advance(1, "qkv")
        for i, (ref, copy) in enumerate(zip((k_t, v_t), sent)):
            copy.wait()
            low = pl.ds(0, held_cols)
            total = ref[:, low].astype(F32) + kv_land[i, :, pl.ds(first, held_cols)].astype(F32)
            ref[:, low] = total.astype(BF16)
        first += held_cols
    own = pl.ds(0, count)
    for i, (ref, target) in enumerate(((k_t, q), (v_t, att_grad))):
        part = ref[:, own]
        g_t[pl.ds((i + 1) * width, width)] = part
        target[...] = jnp.transpose(part.astype(F32)).astype(BF16)
    need("out_own")
    out_swap.wait()
    load("normed1", normed1_in, normed1)
    vec[pl.ds(4, 1)] = jnp.sum(q_grad[...].astype(F32), axis=0, keepdims=True)
    vec[pl.ds(5, 1)] = jnp.sum(att_grad[...].astype(F32), axis=0, keepdims=True)
    need("normed1")
    qkv = [(3 * share, rows_from(g_t, 0, 3 * share), whole(normed1))]
    give("qkv", plan["qkv"][0], qkv)
    advance(1, "qkv")
    need("wqkv", "again", "ss")
    tile = 128

    def norm_rows(i, carry):
        r = pl.ds(aligned(i, tile), tile)
        grad = mat(q_grad[r], arena[pl.ds(0, width)])
        grad = grad + mat(q[r], arena[pl.ds(width, width)])
        grad = grad + mat(att_grad[r], arena[pl.ds(2 * width, width)])
        unit, scale = norm_parts(block_input[r])
        vec[pl.ds(2, 1)] += jnp.sum(grad * unit, axis=0, keepdims=True)
        vec[pl.ds(3, 1)] += jnp.sum(grad, axis=0, keepdims=True)
        total = middle[r] + norm_back(grad, unit, scale, vecs[pl.ds(2, 1)])
        slope = kv[pl.ds(aligned(i, tile) + 3 * count, tile)].astype(F32)
        state_grad[r] = (total * slope).astype(BF16)
        return carry

    lax.fori_loop(0, count // tile, norm_rows, 0)
    vec[pl.ds(1, 1)] = jnp.sum(state_grad[...].astype(F32), axis=0, keepdims=True)
    take("qkv", plan["qkv"][0], qkv)
    advance(1, "conv2")
    cot_t[...] = jnp.transpose(state_grad[...].astype(F32)).astype(BF16)
    need("taps0", "taps1", "taps2")
    conv2 = [(share, rows_from(cot_t, 0, share), block_of(kv, i, count)) for i in range(3)]
    give("conv2", plan["conv2"][0], conv2)
    advance(1, "conv2")
    need("w2_0", "w2_1", "w2_2", "w1", "se", "so")
    prev[...] = mat(state_grad[...], weights[0])
    for s in range(2):
        r = pl.ds(s * states, states)
        even = mat(state_grad[r], weights[1])
        even_grad[r] = (even * normed2[r].astype(F32)).astype(BF16)
        odd = mat(state_grad[r], weights[2])
        place = lax.broadcasted_iota(jnp.int32, (states, width), 0)
        moved = pltpu.roll(prev[r], states - 1, 0)
        odd = odd + jnp.where(place < states - 1, moved, 0.0)
        r_odd = pl.ds(s * size, states)
        odd_grad[r_odd] = (odd * slope_odd[r_odd].astype(F32)).astype(BF16)
        r_edge = pl.ds(s * size + states, TILE)
        edge = jnp.broadcast_to(prev[pl.ds(s * states, 1)], (TILE, width))
        odd_grad[r_edge] = (edge * slope_odd[r_edge].astype(F32)).astype(BF16)
    take("conv2", plan["conv2"][0], conv2)
    advance(1, "conv1")
    need("x_even", "x_odd")
    vec[pl.ds(0, 1)] = jnp.sum(even_grad[...].astype(F32), axis=0, keepdims=True) + jnp.sum(
        odd_grad[...].astype(F32), axis=0, keepdims=True
    )
    vec_copy = pltpu.make_async_remote_copy(
        src_ref=vec,
        dst_ref=vec_got,
        send_sem=core_send.at[len(copies)],
        recv_sem=core_recv.at[len(copies)],
        device_id=core_partner,
        device_id_type=MESH,
    )
    vec_copy.start()
    conv1 = mat_l(even_grad[...], x_even[...]) + mat_l(odd_grad[...], x_odd[...])
    conv1_t[...] = conv1.astype(BF16)
    cols = conv1.shape[1]
    half = share // 2
    ring_slot = turn[0] % len(ring)
    if ring[ring_slot] is not None:
        ring[ring_slot].wait_send()
    conv1_copies = []
    first = plan["conv1"][0]

    def conv1_rows(part):
        low = conv1_t[pl.ds(pl.multiple_of(part * share, TILE), half)]
        high = conv1_t[pl.ds(pl.multiple_of(part * share + half, TILE), half)]
        return jnp.concatenate([low, high], axis=1)

    for y in range(at.y_size):
        stage[ring_slot, pl.ds(y * half, half)] = conv1_rows(2 * y + 1 - core)
        number = len(copies) + 1 + y
        copy = pltpu.make_async_remote_copy(
            src_ref=stage.at[ring_slot, pl.ds(y * half, half)],
            dst_ref=held.at[y, pl.ds(first, half)],
            send_sem=core_send.at[number],
            recv_sem=core_recv.at[number],
            device_id=core_partner,
            device_id_type=MESH,
        )
        copy.start()
        conv1_copies.append(copy)
    for y, copy in enumerate(conv1_copies):
        copy.wait_recv()
        place = pl.ds(first, half)
        total = conv1_rows(2 * y + core).astype(F32) + held[y, place].astype(F32)
        held[y, place] = total.astype(BF16)
    vec_copy.wait()
    total = (vec[...] + vec_got[...]).astype(BF16)
    for y in range(at.y_size):
        held[y, pl.ds(plan["vec"][0], TILE)] = total
    advance(1, "last")
    for s in range(2):
        even = mat(even_grad[pl.ds(s * states, states)], w1[...])
        even = jnp.concatenate([even, jnp.zeros((TILE, cols), F32)], axis=0)
        odd = mat(odd_grad[pl.ds(s * size, size)], w1[...])
        one, two, three = [slice(i * LANES, (i + 1) * LANES) for i in range(3)]
        mel_v[s, :, one] = even[:, two] + odd[:, one] + pltpu.roll(odd[:, three], 1, 0)
        mel_v[s, :, two] = pltpu.roll(even[:, one], size - 1, 0) + even[:, three] + odd[:, two]
    swap = send(mel_v.at[1 - mine], mel_all.at[mine], 0, at.tm_partner(2))
    mel_all[mine] = mel_v[mine]
    advance(1, "last")
    swap.wait()
    sides = [
        send(mel_all.at[:, pl.ds(states, 8)], mel_side.at[0], 2, right),
        send(mel_all.at[:, pl.ds(states + 8, 8)], mel_side.at[1], 3, left),
    ]
    advance(1, "last")
    for copy in sides:
        copy.wait()
    row = lax.broadcasted_iota(jnp.int32, (8, 2 * LANES), 0)
    has_before = jnp.minimum(at.tm, 1).astype(F32)
    has_after = jnp.minimum(at.parts - 1 - at.tm, 1).astype(F32)
    for clip in range(2):
        first, last = pl.ds(0, 8), pl.ds(states - 8, 8)
        mel_all[clip, first] += jnp.where(row == 0, mel_side[0, clip] * has_before, 0.0)
        mel_all[clip, last] += jnp.where(row == 7, mel_side[1, clip] * has_after, 0.0)
        mel_low[clip] = mel_all[clip, pl.ds(0, states)].astype(BF16)
    load("mel_low", mel_low, mel_out)
    for copy in ring:
        if copy is not None and copy is not ring[ring_slot]:
            copy.wait_send()
    for copy in conv1_copies:
        copy.wait_send()
    past = min(reducer.times, plan["qkv"][0] // rows + reducer.delays[-1])
    reducer.steps(done[0], max(done[0], past))
    done[0] = max(done[0], past)
    n = hidden // at.parts
    load("fc1_sum", result.at[pl.ds(plan["fc1"][0], n)], stage.at[0, pl.ds(0, n)])
    load("fc2_sum", result.at[pl.ds(plan["fc2"][0], blocks * share)], stage.at[1, pl.ds(0, blocks * share)])
    load("out_sum", result.at[pl.ds(plan["out"][0], share)], stage.at[2, pl.ds(0, share)])
    advance(1, "more")
    need("fc1_sum", "fc2_sum", "out_sum")
    cut = min(count, 512)
    lanes = pl.ds(0, n)
    pending = []
    buffers = [prev, tmp, middle]
    for i, low in enumerate(range(0, width, cut)):
        high = min(width, low + cut)
        part = stage[0, pl.ds(0, n), pl.ds(low, high - low)].astype(F32)
        buffers[i][pl.ds(0, high - low), lanes] = jnp.transpose(part)
        load("g%d" % i, buffers[i].at[pl.ds(0, high - low), lanes], fc1_out.at[pl.ds(low, high - low)])
        pending.append("g%d" % i)
        advance(1, "more")
    for i in range(blocks):
        if i > 0:
            need("f%d" % (i - 1))
        turned[...] = stage[1, pl.ds(i * share, share)].astype(F32)
        load("f%d" % i, turned, fc2_out.at[:, pl.ds(i * width, width)])
        if i % 2:
            advance(1, "more")
    need("f%d" % (blocks - 1))
    turned[...] = stage[2, pl.ds(0, share)].astype(F32)
    load("out_out", turned, out_out)
    advance(0, "end")
    need("out_out", "mel_low", *pending)
    reducer.close()


def back(operands, parts, clips):
    q, k, wfc1, w1, inv, slope_odd, x_even, x_odd = [operands[i] for i in (5, 6, 3, 12, 8, 17, 19, 20)]
    count, width = q.shape
    every = k.shape[0]
    hidden = wfc1.shape[0]
    states = count // 2
    size = states + TILE
    y_size = parts // 2
    plan, plane, rows, total = back_plan(parts, clips, width, hidden)
    big = max(hidden // parts, 3 * (width // parts))
    scratch = [
        ((y_size, total, width), BF16),
        ((3, big, width), BF16),
        ((3 * width, width), BF16),
        ((4, width, width), BF16),
        (w1.shape, BF16),
        ((max(hidden, 3 * width), count), BF16),
        ((width, count), BF16),
        ((width, count), BF16),
        ((count, width), BF16),
        ((count, width), BF16),
        ((count, width), BF16),
        ((count, width), BF16),
        ((max(2 * every, 4 * count), width), BF16),
        (inv.shape, F32),
        ((count, width), BF16),
        ((count, width), F32),
        ((count, width), F32),
        (slope_odd.shape, BF16),
        (x_even.shape, BF16),
        (x_odd.shape, BF16),
        ((TILE, width), F32),
        ((TILE, width), F32),
        ((TILE, width), F32),
        ((2, count, every), BF16),
        ((count, every), BF16),
        ((LANES, count), BF16),
        ((width, every), BF16),
        ((width, every), BF16),
        ((2, width, every - count), BF16),
        ((count, width), BF16),
        ((count, width), BF16),
        ((count, width), F32),
        ((count, width), F32),
        ((count, width), BF16),
        ((2 * size, width), BF16),
        ((width, x_even.shape[1]), BF16),
        ((2, size, 2 * LANES), F32),
        ((2, size, 2 * LANES), F32),
        ((2, 2, 8, 2 * LANES), F32),
        ((2, states, 2 * LANES), BF16),
        ((width // parts, width), F32),
    ]
    scratch = [pltpu.VMEM(s, d) for s, d in scratch]
    groups = len(bits_of(parts)) - 1
    scratch += [
        pltpu.SemaphoreType.DMA(((6 + hidden // width) * y_size + 1,)),
        pltpu.SemaphoreType.DMA(((6 + hidden // width) * y_size + 1,)),
        pltpu.SemaphoreType.DMA((groups + 2, 2)),
        pltpu.SemaphoreType.DMA((groups + 2, 2)),
        pltpu.SemaphoreType.DMA((48 + 4 * (hidden // width),)),
        pltpu.SemaphoreType.DMA((2,)),
        pltpu.SemaphoreType.DMA((total // rows,)),
        pltpu.SemaphoreType.DMA((2, 4)),
    ]
    scratch += Reducer.scratch(y_size, y_size, clips // y_size, total // rows, rows, width)
    return pl.pallas_call(
        functools.partial(back_kernel, plan, rows),
        out_shape=[
            jax.ShapeDtypeStruct((total, width), BF16),
            jax.ShapeDtypeStruct((2, states, 2 * LANES), BF16),
            jax.ShapeDtypeStruct((2, states, width), BF16),
            jax.ShapeDtypeStruct((width, hidden // parts), F32),
            jax.ShapeDtypeStruct((width // parts, hidden), F32),
            jax.ShapeDtypeStruct((width // parts, width), F32),
        ],
        in_specs=[ANY] * len(operands),
        out_specs=[ANY] * 6,
        scratch_shapes=scratch,
        compiler_params=pltpu.CompilerParams(
            collective_id=3, has_side_effects=True, vmem_limit_bytes=64 << 20
        ),
        name="back",
    )(*operands)


def per_device(
    mel_frames,
    lengths,
    conv1_weight,
    conv1_bias,
    conv2_weight,
    conv2_bias,
    ln1_gain,
    ln1_bias,
    qkv_weight,
    q_bias,
    v_bias,
    out_weight,
    out_bias,
    ln2_gain,
    ln2_bias,
    fc1_weight,
    fc1_bias,
    fc2_weight,
    fc2_bias,
    cotangent,
):
    parts = lax.axis_size("tm")
    place = lax.axis_index("tm")
    clips = lax.axis_size("clip")
    y_size = parts // 2
    core, y_place = place % 2, place // 2
    mine = y_place % 2
    frames, mels = mel_frames.shape[1:]
    states, width = cotangent.shape[1:]
    hidden = fc1_weight.shape[1] * parts
    rows = 2 * states
    share = conv1_bias.shape[0]
    size = states + TILE

    w1_own = jnp.pad(conv1_weight, ((0, 0), (0, LANES - mels), (0, 0))).reshape(3 * LANES, share).T
    w2_own = conv2_weight.reshape(3 * width, share).T
    vec_list = [
        conv1_bias, conv2_bias, ln1_gain, ln1_bias, q_bias, v_bias, out_bias, ln2_gain, ln2_bias,
        fc2_bias,
    ]
    vec_list = vec_list + [fc1_bias[i : i + share] for i in range(0, fc1_bias.shape[0], share)]
    vec_count = len(vec_list)
    vec_row = jnp.arange(TILE)[:, None]
    vec_own = jnp.zeros((TILE, share), BF16)
    for i, member in enumerate(vec_list):
        vec_own = jnp.where(vec_row == i, member[None], vec_own)
    vec_own = jnp.pad(vec_own, ((0, 0), (0, -share % LANES)))

    frame_ids = place * frames + jnp.arange(frames)
    frame_valid = (frame_ids[None, :] < lengths[:, None])[..., None]
    masked = jnp.where(frame_valid, mel_frames, jnp.zeros_like(mel_frames))
    masked = jnp.pad(masked.reshape(2, states, 2, mels), ((0, 0), (0, 0), (0, 0), (0, LANES - mels)))
    masked = masked.reshape(2, states, 2 * LANES)

    length = jnp.where(mine == 0, lengths[0], lengths[1])
    group = [m for m in bits_of(parts) if m != 2]
    segs = [4 * ((place ^ m) // 4) + 2 * jnp.arange(2) + (place ^ m) % 2 for m in combos(group)]
    segs = jnp.concatenate(segs)
    key_ids = (segs[:, None] * states + jnp.arange(states)[None, :]).reshape(1, -1)
    bias = jnp.where(2 * key_ids < length, 0.0, -1e30).astype(F32)
    owns = (
        w1_own, vec_own, w2_own, qkv_weight.T, out_weight.T, fc1_weight.T, fc2_weight.T,
    )
    table = jnp.asarray(positions(states * parts, width))
    (
        w1, w2, wqkv, vecs, state_taps, x_even, x_odd, slope_even, slope_odd, state_slope,
        block_input, normed1, queries, keys, values, attended, inverse, wout, wfc1, wfc2, exponents,
    ) = fore(masked, owns, table, bias, parts)
    summed, mel_back, out_states, fc1_sum, fc2_sum, out_sum = back(
        (
            cotangent, attended, wout, wfc1, wfc2, queries, keys, values, inverse, exponents, wqkv, w2, w1,
            normed1, block_input, state_slope, slope_even, slope_odd, state_taps, x_even, x_odd, vecs,
        ),
        parts,
        clips,
    )
    plan = back_plan(parts, clips, width, hidden)[0]

    def rows_of(name):
        first, count = plan[name]
        return summed[first : first + count].astype(F32)

    conv2_sum = jnp.swapaxes(rows_of("conv2").reshape(3, share, width), 1, 2)
    conv1_sum = rows_of("conv1")
    conv1_sum = jnp.concatenate([conv1_sum[:, : 3 * LANES], conv1_sum[:, 3 * LANES :]], axis=0)
    conv1_sum = conv1_sum.T.reshape(3, LANES, share)[:, :mels]
    all_vec = rows_of("vec")
    vec_sum = lax.dynamic_slice_in_dim(all_vec, place * share, share, axis=1)
    bfc1_sum = lax.dynamic_slice_in_dim(
        all_vec[10:vec_count].reshape(-1), place * (hidden // parts), hidden // parts
    )

    mel_back = mel_back.reshape(2, states, 2, LANES)[..., :mels].reshape(2, frames, mels)
    mel_grad = jnp.where(frame_valid, mel_back, jnp.zeros_like(mel_back))

    return (
        out_states,
        mel_grad,
        conv1_sum,
        vec_sum[0],
        conv2_sum,
        vec_sum[1],
        vec_sum[2],
        vec_sum[3],
        rows_of("qkv").T,
        vec_sum[4],
        vec_sum[5],
        out_sum.T,
        vec_sum[6],
        vec_sum[7],
        vec_sum[8],
        fc1_sum,
        bfc1_sum,
        fc2_sum.T,
        vec_sum[9],
    )


def solution(mesh):
    return jax.shard_map(
        per_device,
        mesh=mesh,
        in_specs=(
            P("clip", "tm", None),
            P("clip"),
            P(None, None, "tm"),
            P("tm"),
            P(None, None, "tm"),
            P("tm"),
            P("tm"),
            P("tm"),
            P(None, "tm"),
            P("tm"),
            P("tm"),
            P(None, "tm"),
            P("tm"),
            P("tm"),
            P("tm"),
            P(None, "tm"),
            P("tm"),
            P(None, "tm"),
            P("tm"),
            P("clip", "tm", None),
        ),
        out_specs=(
            P("clip", "tm", None),
            P("clip", "tm", None),
            P(None, None, "tm"),
            P("tm"),
            P(None, None, "tm"),
            P("tm"),
            P("tm"),
            P("tm"),
            P(None, "tm"),
            P("tm"),
            P("tm"),
            P(None, "tm"),
            P("tm"),
            P("tm"),
            P("tm"),
            P(None, "tm"),
            P("tm"),
            P(None, "tm"),
            P("tm"),
        ),
        check_vma=False,
    )
```

```python
import functools
import math

import jax
import jax.numpy as jnp
import numpy as np
from jax import lax
from jax.experimental import pallas as pl
from jax.experimental.pallas import tpu as pltpu
from jax.sharding import PartitionSpec as P

HEADS = 12
HEAD_DIM = 64
F32 = jnp.float32
BF16 = jnp.bfloat16
SCALE = 1.0 / math.sqrt(HEAD_DIM)
TILE = 16
LANES = 128
MESH = pl.DeviceIdType.MESH
ANY = pl.BlockSpec(memory_space=pl.ANY)
VMEM = pl.BlockSpec(memory_space=pltpu.VMEM)


def xor_swap(array, axis, mask):
    size = lax.axis_size(axis)
    return lax.ppermute(array, axis, [(i, i ^ mask) for i in range(size)])


def pick(array, index, axis=0):
    return lax.dynamic_index_in_dim(array, index, axis=axis, keepdims=False)


def bits_of(size):
    return [1 << b for b in range(size.bit_length() - 1)]


def combos(masks):
    found = [0]
    for mask in masks:
        found = found + [m ^ mask for m in found]
    return found


def flip(index, mask):
    return index + mask * (1 - 2 * ((index // mask) % 2))


def flip_all(index, mask):
    for bit in bits_of(2 * mask) if mask else []:
        if mask & bit:
            index = flip(index, bit)
    return index


def gelu_pair(v):
    a = jnp.abs(v) * (1.0 / math.sqrt(2.0))
    t = 1.0 / (1.0 + 0.3275911 * a)
    poly = t * (
        0.254829592
        + t * (-0.284496736 + t * (1.421413741 + t * (-1.453152027 + t * 1.061405429)))
    )
    bell = jnp.exp(-0.5 * v * v)
    tail = 0.5 * poly * bell
    cdf = jnp.where(v >= 0, 1.0 - tail, tail)
    return v * cdf, cdf + v * bell * (1.0 / math.sqrt(2.0 * math.pi))


def norm_parts(v):
    center = v - jnp.mean(v, axis=-1, keepdims=True)
    spread = jnp.mean(center * center, axis=-1, keepdims=True)
    scale = lax.rsqrt(spread + 1e-05)
    return center * scale, scale


def norm_back(grad, unit, scale, gain):
    a = grad * gain
    mean_a = jnp.mean(a, axis=-1, keepdims=True)
    mean_an = jnp.mean(a * unit, axis=-1, keepdims=True)
    return (a - mean_a - unit * mean_an) * scale


def positions(count, width):
    half = width // 2
    rates = np.exp(-(math.log(10000.0) / (half - 1)) * np.arange(half))
    angles = np.arange(count)[:, None] * rates[None, :]
    return np.concatenate([np.sin(angles), np.cos(angles)], axis=1).astype(np.float32)


def mat(a, b):
    return jnp.dot(a, b, preferred_element_type=F32)


def mat_t(a, b):
    return lax.dot_general(a, b, (((1,), (1,)), ((), ())), preferred_element_type=F32)


def mat_l(a, b):
    return lax.dot_general(a, b, (((0,), (0,)), ((), ())), preferred_element_type=F32)


def aligned(index, step):
    return pl.multiple_of(index * step, step)


class Place:
    def __init__(self):
        self.parts = lax.axis_size("tm")
        self.clips = lax.axis_size("clip")
        self.tm = lax.axis_index("tm")
        self.cl = lax.axis_index("clip")
        self.y_size = self.parts // 2
        self.x_size = self.y_size
        self.z_size = self.clips // self.x_size
        self.core = self.tm % 2
        self.y = self.tm // 2
        self.x = self.cl % self.x_size
        self.z = self.cl // self.x_size

    def tm_partner(self, mask):
        return {"tm": flip(self.tm, mask)}

    def clip_partner(self, mask):
        return {"clip": flip(self.cl, mask)}


def greet(partners):
    barrier = pltpu.get_barrier_semaphore()
    for partner in partners:
        pl.semaphore_signal(barrier, inc=1, device_id=partner, device_id_type=MESH)
    pl.semaphore_wait(barrier, len(partners))


class Gather:
    def __init__(self, at, own, full, first, count, sends, receives, base):
        self.at, self.own, self.full = at, own, full
        self.first, self.count = first, count
        self.shard = own.shape[0]
        self.split = 4 if count % (4 * TILE) == 0 and at.x_size > 1 and at.z_size > 1 else 1
        self.sends, self.receives, self.base = sends, receives, base
        self.used = 0
        self.y_masks = [2 * b for b in bits_of(at.y_size)]
        self.own_y, self.late_y, self.sides = [], [], []
        self.core_copies, self.started = [], []

    @staticmethod
    def slots(parts):
        return 8 * (parts // 2 - 1) + 1

    def region(self, mask, part):
        rows = self.count // self.split
        index = flip_all(self.at.tm, mask) * self.shard + self.first
        if part is not None:
            index = index + part * rows
        else:
            rows = self.count
        return pl.ds(pl.multiple_of(index, TILE), rows)

    def send(self, source, region, partner):
        slot = self.base + self.used
        self.used += 1
        copy = pltpu.make_async_remote_copy(
            src_ref=source,
            dst_ref=self.full.at[region],
            send_sem=self.sends.at[slot],
            recv_sem=self.receives.at[slot],
            device_id=partner,
            device_id_type=MESH,
        )
        copy.start()
        self.started.append(copy)
        return copy

    def part(self, q):
        if self.split == 1:
            return 0
        x, z = self.at.x % 2, self.at.z % 2
        x = 1 - x if q & 1 else x
        z = 1 - z if q & 2 else z
        return x + 2 * z

    def own_part(self, q):
        rows = self.count // self.split
        return self.own.at[pl.ds(pl.multiple_of(self.first + self.part(q) * rows, TILE), rows)]

    def start(self):
        at = self.at
        mask = self.y_masks[0]
        for q, pending in ((0, self.own_y), (3, self.late_y))[: 1 if self.split == 1 else 2]:
            copy = self.send(self.own_part(q), self.region(0, self.part(q)), at.tm_partner(mask))
            pending.append((copy, mask))
        whole = self.own.at[pl.ds(self.first, self.count)]
        self.core_copies.append(self.send(whole, self.region(0, None), at.tm_partner(1)))

    def relay(self, mask, part):
        region = self.region(mask, part)
        self.core_copies.append(self.send(self.full.at[region], region, self.at.tm_partner(1)))

    def over_y(self, pending, q):
        have = []
        for i, mask in enumerate(self.y_masks):
            for copy, m in pending:
                copy.wait_recv()
                have.append(m)
            pending = []
            if i + 1 < len(self.y_masks):
                after = self.y_masks[i + 1]
                for m in [0] + have:
                    region = self.region(m, self.part(q))
                    source = self.full.at[region] if m else self.own_part(q)
                    copy = self.send(source, region, self.at.tm_partner(after))
                    pending.append((copy, m ^ after))
        return have

    def on_y(self):
        at = self.at
        have = self.over_y(self.own_y, 0)
        for m in have:
            region = self.region(m, self.part(0))
            if self.split > 1:
                for q, mask in ((1, 1), (2, at.x_size)):
                    copy = self.send(self.full.at[region], region, at.clip_partner(mask))
                    self.sides.append((copy, m, q))
        for m in have:
            self.relay(m, self.part(0))

    def on_x(self):
        if self.split > 1:
            for m in self.over_y(self.late_y, 3):
                self.relay(m, self.part(3))
        for copy, m, q in self.sides:
            copy.wait_recv()
            self.relay(m, self.part(q))

    def finish(self):
        for copy in self.core_copies:
            copy.wait_recv()

    def close(self):
        for copy in self.started:
            copy.wait_send()


def fore_kernel(states, *refs):
    (
        mel_in, w1_own, vec_own, w2_own, wqkv_own, wout_own, wfc1_own, wfc2_own, pos_in,
        bias,
        w1_out, w2_out, wqkv_out, vecs_out, taps_out, x_even_out, x_odd_out, slope_even_out,
        slope_odd_out, slope_state_out, block_input_out, normed_out, queries_out, keys_out,
        values_out, attended_out, inverse_out, wout, wfc1, wfc2, expo,
        w1, vec_raw, vecs, w2, wqkv, taps, x_even, x_odd, slope_even, slope_odd, slope_state,
        block_input, normed, queries, keys, values, attended, inverse,
        mel, beside, edges, odd_act, tmp, pos, buffer, own_out, own_fc1, own_fc2,
        sends, receives, kv_send, kv_recv, mel_send, mel_recv, local, out_sem, expo_sem,
    ) = refs
    at = Place()
    width = block_input.shape[1]
    rows = 2 * states
    size = states + TILE
    block = 256
    mine = at.y % 2
    seg = [4 * (at.tm // 4) + 2 * s + at.core for s in range(2)]
    right = {"tm": (at.tm + 1) % at.parts}
    left = {"tm": (at.tm + at.parts - 1) % at.parts}
    partners = [at.tm_partner(m) for m in bits_of(at.parts)] + [right, left]
    partners += [at.clip_partner(m) for m in bits_of(2 * at.x_size)]

    loads = {}

    def load(name, src, dst):
        loads[name] = pltpu.make_async_copy(src, dst, local.at[len(loads)])
        loads[name].start()

    def place_of(own):
        return pl.ds(aligned(at.tm, own.shape[0]), own.shape[0])

    kept = []

    def keep(src, dst):
        kept.append(pltpu.make_async_copy(src, dst, out_sem.at[len(kept)]))
        kept[-1].start()

    load("mel", mel_in.at[mine], mel.at[mine])
    for name, own, full in (
        ("w1", w1_own, w1), ("vec", vec_own, vec_raw), ("w2", w2_own, w2), ("wqkv", wqkv_own, wqkv),
    ):
        load(name, own, full.at[place_of(own)])
    through = (("wout", wout_own, own_out), ("wfc1", wfc1_own, own_fc1), ("wfc2", wfc2_own, own_fc2))
    for name, own, stop in through:
        load(name, own, stop)
    for s in range(2):
        from_table = pos_in.at[pl.ds(aligned(seg[s], states), states)]
        load("pos%d" % s, from_table, pos.at[pl.ds(s * states, states)])
    greet(partners)

    def send(src, dst, slot, partner):
        copy = pltpu.make_async_remote_copy(
            src_ref=src,
            dst_ref=dst,
            send_sem=mel_send.at[slot],
            recv_sem=mel_recv.at[slot],
            device_id=partner,
            device_id_type=MESH,
        )
        copy.start()
        return copy

    to_right = send(mel_in.at[:, pl.ds(states - TILE, TILE)], beside.at[0], 0, right)
    to_left = send(mel_in.at[:, pl.ds(0, TILE)], beside.at[1], 1, left)
    swap = send(mel_in.at[1 - mine], mel.at[mine], 2, at.tm_partner(2))
    base = 0
    groups = {}
    for name, own, full, pieces in (
        ("w1", w1_own, w1, 1), ("vec", vec_own, vec_raw, 1), ("w2", w2_own, w2, 1),
        ("qkv", wqkv_own, wqkv, 3), ("out", wout_own, wout, 1), ("fc1", wfc1_own, wfc1, 2),
        ("fc2", wfc2_own, wfc2, 1),
    ):
        whole = own.shape[0]
        count = whole // pieces if whole % (pieces * TILE * 4) == 0 else whole
        groups[name] = []
        for first in range(0, whole, count):
            g = Gather(at, own, full, first, count, sends, receives, base)
            base += Gather.slots(at.parts)
            groups[name].append(g)

    def part(name, i):
        return groups[name][i : i + 1]

    def run(what, *pieces):
        for piece in pieces:
            for g in piece:
                getattr(g, what)()

    def finish(*names):
        for name in names:
            run("finish", groups[name])

    run("start", groups["w1"], groups["vec"], groups["w2"])
    to_right.wait_recv()
    to_left.wait_recv()
    forward = [
        send(beside.at[i, 1 - mine], edges.at[mine, i], 3 + i, at.tm_partner(2)) for i in range(2)
    ]
    for i in range(2):
        edges[mine, i] = beside[i, mine]
    swap.wait_recv()
    loads["mel"].wait()
    for copy in forward:
        copy.wait_recv()
    for s in range(2):
        row = lax.broadcasted_iota(jnp.int32, (TILE, 2 * LANES), 0)
        has_before = jnp.minimum(seg[s], 1).astype(F32)
        has_after = jnp.minimum(at.parts - 1 - seg[s], 1).astype(F32)
        tail = jnp.where(row == 0, edges[s, 1].astype(F32) * has_after, 0.0)
        tail = jnp.where(row == TILE - 1, edges[s, 0].astype(F32) * has_before, tail)
        m = jnp.concatenate([mel[s].astype(F32), tail], axis=0)
        before = pltpu.roll(m, 1, 0)
        after = pltpu.roll(m, size - 1, 0)
        low = pl.ds(0, LANES)
        even_rows = pl.ds(s * states, states)
        odd_rows = pl.ds(s * size, size)
        x_even[even_rows, low] = before[:states, LANES:].astype(BF16)
        x_even[even_rows, pl.ds(LANES, 2 * LANES)] = m[:states].astype(BF16)
        x_odd[odd_rows, pl.ds(0, 2 * LANES)] = m.astype(BF16)
        x_odd[odd_rows, pl.ds(2 * LANES, LANES)] = after[:, :LANES].astype(BF16)
    keep(x_even, x_even_out)
    keep(x_odd, x_odd_out)
    for (name, own, stop), full in zip(through, (wout, wfc1, wfc2)):
        loads[name].wait()
        keep(stop, full.at[place_of(own)])
    run("on_y", groups["w1"], groups["vec"])
    run("on_x", groups["w1"], groups["vec"])
    run("on_y", groups["w2"])
    run("start", part("qkv", 0))
    finish("w1", "vec")
    loads["w1"].wait()
    loads["vec"].wait()
    keep(w1, w1_out)
    total = jnp.zeros(vecs.shape, F32)
    share = width // at.parts
    for j in range(at.parts):
        piece = vec_raw[pl.ds(j * TILE, TILE)].astype(F32)
        low = (j * share) // LANES * LANES
        cells = [piece]
        if low > 0:
            cells = [jnp.zeros((TILE, low), F32)] + cells
        if width - low - piece.shape[1] > 0:
            cells = cells + [jnp.zeros((TILE, width - low - piece.shape[1]), F32)]
        placed = jnp.concatenate(cells, axis=1)
        shift = j * share - low
        total = total + (pltpu.roll(placed, shift, 1) if shift else placed)
    row = lax.broadcasted_iota(jnp.int32, vecs.shape, 0)
    total = jnp.where(row < 10, total, 0.0)
    pieces = wfc1_own.shape[0] // share
    for j in range(at.parts):
        for i in range(pieces):
            first = (j * pieces + i) * share
            piece = vec_raw[pl.ds(j * TILE, TILE)].astype(F32)[10 + i : 11 + i]
            column = first % width
            low = column // LANES * LANES
            cells = [piece]
            if low > 0:
                cells = [jnp.zeros((1, low), F32)] + cells
            if width - low - piece.shape[1] > 0:
                cells = cells + [jnp.zeros((1, width - low - piece.shape[1]), F32)]
            placed = jnp.broadcast_to(jnp.concatenate(cells, axis=1), vecs.shape)
            if column - low:
                placed = pltpu.roll(placed, column - low, 1)
            total = total + jnp.where(row == 10 + first // width, placed, 0.0)
    vecs[...] = total

    def vec(i, cols):
        return vecs[pl.ds(i, 1), cols]

    keep(vecs, vecs_out)
    between = [
        lambda: run("start", part("qkv", 1)),
        lambda: None,
        lambda: (run("on_x", groups["w2"]), run("on_y", part("qkv", 0)), run("start", part("qkv", 2))),
        lambda: (run("on_y", part("qkv", 1)), run("start", groups["out"], part("fc1", 0))),
    ]
    for s in range(2):

        def odd_columns(j, carry, s=s):
            cols = pl.ds(aligned(j, block), block)
            tmp[pl.ds(0, size)] = mat_t(x_odd[pl.ds(s * size, size)], w1[cols])

            def odd_rows(i, carry):
                r = pl.ds(aligned(i, 64), 64)
                act, slope = gelu_pair(tmp[r] + vec(0, cols))
                odd_act[r, cols] = act
                taps[pl.ds(aligned(i, 64) + s * states, 64), pl.ds(2 * width + aligned(j, block), block)] = act.astype(BF16)
                slope_odd[pl.ds(aligned(i, 64) + s * size, 64), cols] = slope.astype(BF16)
                return carry

            lax.fori_loop(0, states // 64, odd_rows, 0)
            r = pl.ds(states, TILE)
            act, slope = gelu_pair(tmp[r] + vec(0, cols))
            last = lax.broadcasted_iota(jnp.int32, act.shape, 0) == TILE - 1
            first = jnp.minimum(seg[s], 1).astype(F32)
            act = jnp.where(last, act * first, 0.0)
            slope = jnp.where(last, slope * first, 0.0)
            odd_act[r, cols] = act
            slope_odd[pl.ds(s * size + states, TILE), cols] = slope.astype(BF16)
            moved = pltpu.roll(odd_act[:, cols], 1, 0)
            taps[pl.ds(s * states, states), cols] = moved[:states].astype(BF16)
            return carry

        lax.fori_loop(0, width // block, odd_columns, 0)
        between[2 * s]()

        def even_columns(j, carry, s=s):
            cols = pl.ds(aligned(j, block), block)
            tmp[pl.ds(0, states)] = mat_t(x_even[pl.ds(s * states, states)], w1[cols])

            def even_rows(i, carry):
                r = pl.ds(aligned(i, 64), 64)
                act, slope = gelu_pair(tmp[r] + vec(0, cols))
                out = pl.ds(aligned(i, 64) + s * states, 64)
                taps[out, pl.ds(width + aligned(j, block), block)] = act.astype(BF16)
                slope_even[out, cols] = slope.astype(BF16)
                return carry

            lax.fori_loop(0, states // 64, even_rows, 0)
            return carry

        lax.fori_loop(0, width // block, even_columns, 0)
        between[2 * s + 1]()

    finish("w2")
    loads["w2"].wait()
    loads["pos0"].wait()
    loads["pos1"].wait()
    keep(w2, w2_out)
    keep(taps, taps_out)
    keep(slope_even, slope_even_out)
    keep(slope_odd, slope_odd_out)

    def state_columns(j, carry):
        cols = pl.ds(aligned(j, block), block)
        tmp[pl.ds(0, rows)] = mat_t(taps[...], w2[cols])

        def state_rows(i, carry):
            r = pl.ds(aligned(i, 64), 64)
            act, slope = gelu_pair(tmp[r] + vec(1, cols))
            block_input[r, cols] = act + pos[r, cols]
            slope_state[r, cols] = slope.astype(BF16)
            return carry

        lax.fori_loop(0, rows // 64, state_rows, 0)
        return carry

    third = width // block // 3
    lax.fori_loop(0, third, state_columns, 0)
    run("on_y", part("qkv", 2))
    run("start", part("fc1", 1))
    lax.fori_loop(third, 2 * third, state_columns, 0)
    run("on_x", part("qkv", 0))
    lax.fori_loop(2 * third, width // block, state_columns, 0)
    keep(block_input, block_input_out)
    keep(slope_state, slope_state_out)
    full = pl.ds(0, width)

    def norm_rows(i, carry):
        r = pl.ds(aligned(i, 32), 32)
        unit, _ = norm_parts(block_input[r])
        normed[r] = (unit * vec(2, full) + vec(3, full)).astype(BF16)
        return carry

    lax.fori_loop(0, rows // 32, norm_rows, 0)
    run("on_x", part("qkv", 1), part("qkv", 2))
    keep(normed, normed_out)
    finish("qkv")
    loads["wqkv"].wait()
    keep(wqkv, wqkv_out)
    group = [m for m in bits_of(at.parts) if m != 2]

    def exchange(array, base):
        held = rows
        for n, mask in enumerate(group):
            copy = pltpu.make_async_remote_copy(
                src_ref=array.at[pl.ds(0, held)],
                dst_ref=array.at[pl.ds(held, held)],
                send_sem=kv_send.at[base + n],
                recv_sem=kv_recv.at[base + n],
                device_id=at.tm_partner(mask),
                device_id_type=MESH,
            )
            copy.start()
            if n + 1 < len(group):
                copy.wait()
                held = 2 * held
            else:
                return copy

    def project(target, first, bias):
        def columns(j, carry):
            cols = pl.ds(aligned(j, block), block)
            part = mat_t(normed[...], wqkv[pl.ds(first + aligned(j, block), block)])
            if bias is not None:
                part = part + vec(bias, cols)
            target[pl.ds(0, rows), cols] = part.astype(BF16)
            return carry

        lax.fori_loop(0, width // block, columns, 0)

    project(keys, width, None)
    key_copy = exchange(keys, 1)
    run("on_y", groups["out"], part("fc1", 0))
    run("start", groups["fc2"])
    project(values, 2 * width, 5)
    value_copy = exchange(values, 1 + len(group))
    project(queries, 0, 4)
    keep(queries, queries_out)
    run("on_y", part("fc1", 1))
    run("on_x", groups["out"])
    key_copy.wait()
    value_copy.wait()
    keep(keys, keys_out)
    keep(values, values_out)
    q, k, v = queries, keys, values
    pairs = width // LANES
    inverse[...] = jnp.zeros(inverse.shape, F32)
    lane = lax.broadcasted_iota(jnp.int32, (rows, LANES), 1)

    def out_copy(p, h):
        return pltpu.make_async_copy(buffer.at[h], expo.at[2 * p + h], expo_sem.at[h])

    def pair_body(p, carry):
        cols = pl.ds(aligned(p, LANES), LANES)
        for h in range(2):

            @pl.when(p > 0)
            def _(h=h):
                out_copy(p - 1, h).wait()

        scaled = q[:, cols].astype(F32) * SCALE
        inv = inverse[...]
        outs = []
        scores = []
        for h in range(2):
            own = (lane < HEAD_DIM) if h == 0 else (lane >= HEAD_DIM)
            head = jnp.where(own, scaled, 0.0).astype(BF16)
            scores.append(mat_t(head, k[:, cols]) + bias[pl.ds(0, 1)])
        for h in range(2):
            largest = jnp.max(scores[h], axis=-1, keepdims=True)
            exponent = jnp.exp(scores[h] - largest)
            one = 1.0 / jnp.sum(exponent, axis=-1, keepdims=True)
            low = exponent.astype(BF16)
            buffer[h] = low
            outs.append(mat(low, v[:, cols]) * one)
            inv = jnp.where(lane == 2 * p + h, one, inv)
        attended[:, cols] = jnp.where(lane < HEAD_DIM, outs[0], outs[1]).astype(BF16)
        inverse[...] = inv
        for h in range(2):
            out_copy(p, h).start()
        return carry

    events = [
        ("on_x", part("fc1", 0)),
        ("on_y", groups["fc2"]),
        ("on_x", part("fc1", 1)),
        ("on_x", groups["fc2"]),
    ]
    for i, event in enumerate(events):
        lax.fori_loop(i * pairs // len(events), (i + 1) * pairs // len(events), pair_body, 0)
        run(*event)
    keep(attended, attended_out)
    keep(inverse, inverse_out)
    for h in range(2):
        out_copy(pairs - 1, h).wait()
    finish("out", "fc1", "fc2")
    for copy in [to_right, to_left, swap] + forward:
        copy.wait_send()
    for pieces in groups.values():
        run("close", pieces)
    for copy in kept:
        copy.wait()


def fore(mel, owns, pos, bias, parts):
    w1_own, vec_own, w2_own, wqkv_own, wout_own, wfc1_own, wfc2_own = owns
    states = mel.shape[1]
    rows, width = 2 * states, pos.shape[1]
    every = bias.shape[1]
    full = lambda own: ((parts * own.shape[0], own.shape[1]), BF16)
    both = [
        full(w1_own),
        full(w2_own),
        full(wqkv_own),
        ((TILE, width), F32),
        ((rows, 3 * width), BF16),
        ((rows, 3 * LANES), BF16),
        ((rows + 2 * TILE, 3 * LANES), BF16),
        ((rows, width), BF16),
        ((rows + 2 * TILE, width), BF16),
        ((rows, width), BF16),
        ((rows, width), F32),
        ((rows, width), BF16),
        ((rows, width), BF16),
        ((every, width), BF16),
        ((every, width), BF16),
        ((rows, width), BF16),
        ((rows, LANES), F32),
    ]
    shapes = both + [
        full(wout_own),
        full(wfc1_own),
        full(wfc2_own),
        ((width // HEAD_DIM, rows, every), BF16),
    ]
    here = [pltpu.VMEM(s, d) for s, d in both]
    vec_raw = pltpu.VMEM((parts * TILE, vec_own.shape[1]), BF16)
    here = [here[0], vec_raw, here[3], here[1], here[2]] + here[4:]
    slots = 12 * Gather.slots(parts)
    return pl.pallas_call(
        functools.partial(fore_kernel, states),
        out_shape=[jax.ShapeDtypeStruct(s, d) for s, d in shapes],
        in_specs=[ANY] * 9 + [VMEM],
        out_specs=[ANY] * len(shapes),
        scratch_shapes=here
        + [
            pltpu.VMEM(mel.shape, BF16),
            pltpu.VMEM((2, 2, TILE, 2 * LANES), BF16),
            pltpu.VMEM((2, 2, TILE, 2 * LANES), BF16),
            pltpu.VMEM((states + TILE, width), F32),
            pltpu.VMEM((max(rows, states + TILE), 256), F32),
            pltpu.VMEM((rows, width), F32),
            pltpu.VMEM((2, rows, every), BF16),
            pltpu.VMEM(wout_own.shape, BF16),
            pltpu.VMEM(wfc1_own.shape, BF16),
            pltpu.VMEM(wfc2_own.shape, BF16),
            pltpu.SemaphoreType.DMA((slots,)),
            pltpu.SemaphoreType.DMA((slots,)),
            pltpu.SemaphoreType.DMA((8,)),
            pltpu.SemaphoreType.DMA((8,)),
            pltpu.SemaphoreType.DMA((6,)),
            pltpu.SemaphoreType.DMA((6,)),
            pltpu.SemaphoreType.DMA((12,)),
            pltpu.SemaphoreType.DMA((len(both) + 4,)),
            pltpu.SemaphoreType.DMA((2,)),
        ],
        compiler_params=pltpu.CompilerParams(
            collective_id=1, has_side_effects=True, vmem_limit_bytes=62 << 20
        ),
        name="fore",
    )(mel, *owns, pos, bias)


class Reducer:
    def __init__(self, at, rows, ahead, held, result, landings, sends, receives, local):
        self.at, self.rows, self.ahead = at, rows, ahead
        self.source, self.result, self.landings = held, result, landings
        self.sends, self.receives, self.local = sends, receives, local
        self.chunks = result.shape[0] // rows
        self.y_bits = list(reversed(bits_of(at.y_size)))
        self.x_bits = bits_of(at.x_size)
        self.mine = [(at.x // b) % 2 for b in self.x_bits]
        self.x_partner = [at.clip_partner(b) for b in self.x_bits]
        self.others = range(1, at.z_size)
        self.y_partner = [at.tm_partner(2 * b) for b in self.y_bits]
        self.tops, self.depth = len(self.y_bits), len(self.x_bits)
        self.stages = self.tops + 2 * self.depth + 3
        self.delays = [0] + [ahead + s for s in range(self.stages - 1)]
        self.times = self.chunks + self.delays[-1]
        self.piece = (rows >> self.depth) // at.z_size

    @staticmethod
    def scratch(y_size, x_size, z_size, chunks, rows, width):
        shapes = [pltpu.VMEM((chunks, b, rows, width), BF16) for b in reversed(bits_of(y_size))]
        depth = len(bits_of(x_size))
        shapes += [pltpu.VMEM((chunks, rows >> (k + 1), width), BF16) for k in range(depth)]
        piece = (rows >> depth) // z_size
        shapes += [pltpu.VMEM((chunks, z_size - 1, piece, width), BF16)]
        slots = len(bits_of(y_size)) + 2 * depth + 2 * (z_size - 1)
        return shapes + [pltpu.SemaphoreType.DMA((chunks, slots))] * 2

    def z_place(self, d):
        return (self.at.z + d) % self.at.z_size

    def z_partner(self, d):
        return {"clip": self.at.x + self.at.x_size * self.z_place(d)}

    def partners(self):
        return self.y_partner + self.x_partner + [self.z_partner(d) for d in self.others]

    def remote(self, src, dst, c, slot, device):
        return pltpu.make_async_remote_copy(
            src_ref=src,
            dst_ref=dst,
            send_sem=self.sends.at[c, slot],
            recv_sem=self.receives.at[c, slot],
            device_id=device,
            device_id_type=MESH,
        )

    def chunk(self, c):
        return pl.ds(pl.multiple_of(c * self.rows, self.rows), self.rows)

    def y_copy(self, c, k):
        b = self.y_bits[k]
        away = b * (1 - (self.at.y // b) % 2)
        if k == 0:
            src = self.source.at[pl.ds(away, b), self.chunk(c)]
        else:
            src = self.landings[k - 1].at[c, pl.ds(away, b)]
        return self.remote(src, self.landings[k].at[c], c, k, self.y_partner[k])

    def half(self, k, bit):
        count = self.rows >> (k + 1)
        return pl.ds(aligned(bit, count), count)

    def current(self, k, c, region):
        if k == 0:
            return self.landings[self.tops - 1].at[c, 0, region]
        return self.landings[self.tops + k - 1].at[c, region]

    def spread(self, c, k):
        src = self.current(k, c, self.half(k, 1 - self.mine[k]))
        dst = self.landings[self.tops + k].at[c]
        return self.remote(src, dst, c, self.tops + k, self.x_partner[k])

    def z_rows(self, place):
        return pl.ds(aligned(place, self.piece), self.piece)

    def z_copy(self, c, d):
        src = self.current(self.depth, c, self.z_rows(self.z_place(d)))
        dst = self.landings[-1].at[c, d - 1]
        return self.remote(src, dst, c, self.tops + self.depth + d - 1, self.z_partner(d))

    def kept(self, c, k):
        first = c * self.rows
        for i in range(k + 1):
            first = first + self.mine[i] * (self.rows >> (i + 1))
        count = self.rows >> (k + 1)
        return pl.ds(pl.multiple_of(first, count), count)

    def finished(self, c):
        first = c * self.rows + self.at.z * self.piece
        for i in range(self.depth):
            first = first + self.mine[i] * (self.rows >> (i + 1))
        return pl.ds(pl.multiple_of(first, self.piece), self.piece)

    def own_rows(self, c):
        return self.current(self.depth, c, self.z_rows(self.at.z))

    def z_collect(self, c, d):
        slot = self.tops + self.depth + len(self.others) + d - 1
        region = self.result.at[self.finished(c)]
        return self.remote(self.own_rows(c), region, c, slot, self.z_partner(d))

    def keep(self, c):
        return pltpu.make_async_copy(
            self.own_rows(c), self.result.at[self.finished(c)], self.local.at[c]
        )

    def collect(self, c, k):
        region = self.result.at[self.kept(c, k)]
        slot = self.tops + self.depth + 2 * len(self.others) + k
        return self.remote(region, region, c, slot, self.x_partner[k])

    def run(self, stage, c):
        if stage == 0:
            self.y_copy(c, 0).start()
        elif stage <= self.tops:
            k = stage - 1
            b = self.y_bits[k]
            own = pl.ds(b * ((self.at.y // b) % 2), b)
            self.y_copy(c, k).wait_recv()
            mine = self.source[own, self.chunk(c)] if k == 0 else self.landings[k - 1][c, own]
            total = mine.astype(F32) + self.landings[k][c].astype(F32)
            self.landings[k][c] = total.astype(BF16)
            if k + 1 < self.tops:
                self.y_copy(c, k + 1).start()
            else:
                self.spread(c, 0).start()
        elif stage <= self.tops + self.depth:
            k = stage - self.tops - 1
            self.spread(c, k).wait_recv()
            mine = self.current(k, c, self.half(k, self.mine[k]))[...]
            total = mine.astype(F32) + self.landings[self.tops + k][c].astype(F32)
            self.landings[self.tops + k][c] = total.astype(BF16)
            if k + 1 < self.depth:
                self.spread(c, k + 1).start()
            else:
                for d in self.others:
                    self.z_copy(c, d).start()
        elif stage == self.tops + self.depth + 1:
            total = self.own_rows(c)[...].astype(F32)
            for d in self.others:
                self.z_copy(c, d).wait_recv()
                total = total + self.landings[-1][c, d - 1].astype(F32)
            self.own_rows(c)[...] = total.astype(BF16)
            self.keep(c).start()
            for d in self.others:
                self.z_collect(c, d).start()
        elif stage == self.tops + self.depth + 2:
            for d in self.others:
                self.z_collect(c, d).wait_recv()
            self.keep(c).wait()
            self.collect(c, self.depth - 1).start()
        else:
            k = self.depth - 1 - (stage - self.tops - self.depth - 3)
            self.collect(c, k).wait_recv()
            if k > 0:
                self.collect(c, k - 1).start()

    def step(self, time):
        for stage in range(self.stages):
            c = time - self.delays[stage]

            @pl.when((c >= 0) & (c < self.chunks))
            def _(stage=stage, c=c):
                self.run(stage, c)

    def steps(self, first, last):
        def body(time, carry):
            self.step(time)
            return carry

        lax.fori_loop(first, last, body, 0)

    def close(self):
        def body(c, carry):
            for k in range(self.tops):
                self.y_copy(c, k).wait_send()
            for k in range(self.depth):
                self.spread(c, k).wait_send()
                self.collect(c, k).wait_send()
            for d in self.others:
                self.z_copy(c, d).wait_send()
                self.z_collect(c, d).wait_send()
            return carry

        lax.fori_loop(0, self.chunks, body, 0)


AHEAD = 2


def tile_of(count):
    return max(t for t in range(TILE, 257, TILE) if count % t == 0)


def back_plan(parts, clips, width, hidden):
    share = width // parts
    plane = len(bits_of(parts // 2)) + len(bits_of(clips // (parts // 2)))
    rows = TILE << plane
    plan, first = {}, 0
    early = [("fc2", hidden // parts), ("fc1", hidden // parts), ("out", share)]
    late = [("qkv", 3 * share), ("conv2", 3 * share), ("conv1", share // 2), ("vec", TILE)]
    for group in (early, late):
        for name, count in group:
            plan[name] = (first, count)
            first += count
        plan["gap%d" % len(plan)] = (first, -first % rows)
        first += -first % rows
    plan["last"] = plan["more"] = plan["end"] = (first, 0)
    return plan, plane, rows, first


def back_kernel(plan, rows, *refs):
    (
        cot_in, attended_in, wout_in, wfc1_in, wfc2_in, q_in, k_in, v_in, inv_in, expo, wqkv_in,
        w2_in, w1_in, normed1_in, block_input_in, slope_state_in, slope_even_in, slope_odd_in,
        taps_in, x_even_in, x_odd_in, vecs_in,
        result, mel_out, states_out, fc1_out, fc2_out, out_out,
        held, stage, arena, weights, w1, g_t, cot_t, branch_t, normed2, attended, att_grad, q, kv,
        inv, normed1, block_input, middle, slope_odd, x_even, x_odd, vec, vec_got, vecs,
        ebuf, score_grad, q_t, k_t, v_t, kv_land, q_grad, state_grad, prev, tmp, even_grad, odd_grad,
        conv1_t, mel_v, mel_all, mel_side, mel_low, turned,
        core_send, core_recv, kv_send, kv_recv, load_sem, expo_sem, local, side_sem,
    ) = refs[: 28 + 49]
    *landings, sends, receives = refs[28 + 49 :]
    at = Place()
    width = q.shape[1]
    count = q.shape[0]
    states = count // 2
    size = states + TILE
    every = k_in.shape[0]
    hidden = wfc1_in.shape[0]
    share = width // at.parts
    core, mine = at.core, at.y % 2
    core_partner = at.tm_partner(1)

    loads = {}

    def load(name, src, dst):
        copy = pltpu.make_async_copy(src, dst, load_sem.at[len(loads)])
        copy.start()
        loads[name] = copy

    def need(*names):
        for name in names:
            loads[name].wait()

    blocks = hidden // width

    def load_block(i):
        low = pl.ds(i * width, width)
        load("fc1_%d" % i, wfc1_in.at[low], weights.at[i % 2])
        load("fc2_%d" % i, wfc2_in.at[:, low], weights.at[2 + i % 2])

    load("att", attended_in, attended)
    load("wout", wout_in, arena.at[pl.ds(0, width)])
    load("block_input", block_input_in, block_input)
    load("vecs", vecs_in, vecs)
    load_block(0)
    load_block(1)
    load("q", q_in, q)
    load("inv", inv_in, inv)
    load("k", k_in, kv.at[pl.ds(0, every)])
    load("v", v_in, kv.at[pl.ds(every, every)])
    load("w1", w1_in, w1)
    load("so", slope_odd_in, slope_odd)
    load("x_even", x_even_in, x_even)
    load("x_odd", x_odd_in, x_odd)

    def fetch(n, slot):
        return pltpu.make_async_copy(expo.at[n], ebuf.at[slot], expo_sem.at[slot])

    fetch(0, 0).start()
    reducer = Reducer(at, rows, AHEAD, held, result, landings, sends, receives, local)
    right = {"tm": (at.tm + 1) % at.parts}
    left = {"tm": (at.tm + at.parts - 1) % at.parts}
    greet([core_partner, right, left] + reducer.partners())
    place = pl.ds(pl.multiple_of(mine * states, states), states)
    cot_swap = pltpu.make_async_remote_copy(
        src_ref=cot_in.at[1 - mine],
        dst_ref=q_grad.at[place],
        send_sem=kv_send.at[len(bits_of(at.parts)) - 1, 1],
        recv_sem=kv_recv.at[len(bits_of(at.parts)) - 1, 1],
        device_id=at.tm_partner(2),
        device_id_type=MESH,
    )
    cot_swap.start()
    load("cot", cot_in.at[mine], q_grad.at[place])
    def send(src, dst, slot, device):
        copy = pltpu.make_async_remote_copy(
            src_ref=src,
            dst_ref=dst,
            send_sem=side_sem.at[0, slot],
            recv_sem=side_sem.at[1, slot],
            device_id=device,
            device_id_type=MESH,
        )
        copy.start()
        return copy

    done = [0]

    def advance(steps, ready):
        ready = ready if isinstance(ready, int) else plan[ready][0]
        limit = reducer.times if ready == reducer.chunks * rows else ready // rows
        last = max(done[0], min(done[0] + steps, limit))
        if steps == 0:
            last = reducer.times
        reducer.steps(done[0], last)
        done[0] = last
    for name, (first, n) in plan.items():
        if name.startswith("gap") and n:
            for y in range(at.y_size):
                held[y, pl.ds(first, n)] = jnp.zeros((n, width), BF16)

    copies = {}
    slots = {}
    ring = [None] * stage.shape[0]
    turn = [0]

    def give(name, first, parts, places=None):
        for y in places or range(at.y_size):
            slot = turn[0] % len(ring)
            turn[0] += 1
            if ring[slot] is not None:
                ring[slot].wait_send()
            offset = 0
            for n, rows_of, acts in parts:
                tile = tile_of(n)
                for i in range(n // tile):
                    g = rows_of(2 * y + 1 - core, i * tile, tile)
                    stage[slot, pl.ds(offset + i * tile, tile)] = mat(g, acts()).astype(BF16)
                offset += n
            number = len(copies)
            copy = pltpu.make_async_remote_copy(
                src_ref=stage.at[slot, pl.ds(0, offset)],
                dst_ref=held.at[y, pl.ds(first, offset)],
                send_sem=core_send.at[number],
                recv_sem=core_recv.at[number],
                device_id=core_partner,
                device_id_type=MESH,
            )
            copy.start()
            ring[slot] = copy
            copies[name, y] = copy

    def take(name, first, parts, places=None):
        for y in places or range(at.y_size):
            copies[name, y].wait_recv()
            offset = first
            for n, rows_of, acts in parts:
                tile = tile_of(n)
                for i in range(n // tile):
                    g = rows_of(2 * y + core, i * tile, tile)
                    place = pl.ds(offset + i * tile, tile)
                    total = mat(g, acts()) + held[y, place].astype(F32)
                    held[y, place] = total.astype(BF16)
                offset += n

    def rows_from(ref, base, n):
        def rows_of(part, offset, tile):
            return ref[pl.ds(pl.multiple_of(base + part * n + offset, TILE), tile)]

        return rows_of

    def whole(ref):
        return lambda: ref[...]

    def block_of(ref, i, n):
        return lambda: ref[pl.ds(i * n, n)]

    def vec_row(i):
        return vecs[pl.ds(i, 1)]

    tile = 64

    def over_rows(body):
        def run(i, carry):
            body(pl.ds(aligned(i, tile), tile))
            return carry

        lax.fori_loop(0, count // tile, run, 0)

    need("att", "wout", "block_input", "vecs")
    prev[...] = mat_t(attended[...], arena[pl.ds(0, width)])

    def middle_rows(r):
        total = block_input[r] + prev[r] + vec_row(6)
        middle[r] = total
        unit, _ = norm_parts(total)
        normed2[r] = (unit * vec_row(7) + vec_row(8)).astype(BF16)

    over_rows(middle_rows)
    vec[...] = jnp.zeros(vec.shape, F32)
    acts = (state_grad, even_grad)
    slope_hid = odd_grad.at[pl.ds(0, count)]
    per_y = 2 * (hidden // at.parts)
    group_blocks = per_y // width
    fc2, fc1 = [], []
    for i in range(blocks):
        fc2.append([(share, rows_from(cot_t, 0, share), whole(acts[i % 2]))])
    for y in range(at.y_size):
        fc1.append([(hidden // at.parts, rows_from(g_t, 0, hidden // at.parts), whole(normed2))])
    ready = 0
    for i in range(blocks):
        need("fc1_%d" % i, "fc2_%d" % i)
        up, down, act = weights.at[i % 2], weights.at[2 + i % 2], acts[i % 2]
        tmp[...] = mat_t(normed2[...], up[...])

        def hidden_rows(r, i=i, act=act):
            value, slope = gelu_pair(tmp[r] + vec_row(10 + i))
            act[r] = value.astype(BF16)
            slope_hid[r] = slope.astype(BF16)

        over_rows(hidden_rows)
        part = mat_t(act[...], down[...])
        prev[...] = part if i == 0 else prev[...] + part
        if i == 0:
            need("cot")
            cot_swap.wait()
            wide_cot = q_grad[...].astype(F32)
            vec[pl.ds(9, 1)] = jnp.sum(wide_cot, axis=0, keepdims=True)
            cot_t[...] = jnp.transpose(wide_cot).astype(BF16)
        tmp[...] = mat(q_grad[...], down[...])

        def hidden_back(r):
            slope_hid[r] = (tmp[r] * slope_hid[r].astype(F32)).astype(BF16)

        over_rows(hidden_back)
        part = mat(slope_hid[...], up[...])
        block_input[...] = part if i == 0 else block_input[...] + part
        wide = slope_hid[...].astype(F32)
        vec[pl.ds(10 + i, 1)] = jnp.sum(wide, axis=0, keepdims=True)
        g_t[pl.ds(i * width, width)] = jnp.transpose(wide).astype(BF16)
        if i + 2 < blocks:
            load_block(i + 2)
        give("fc2_%d" % i, plan["fc2"][0] + i * share, fc2[i])
        if i > 0:
            take("fc2_%d" % (i - 1), plan["fc2"][0] + (i - 1) * share, fc2[i - 1])
            ready = i * share
        if (i + 1) % group_blocks == 0:
            y = i // group_blocks
            give("fc1_%d" % y, plan["fc1"][0], fc1[y], [y])
        if i == blocks - 1:
            take("fc2_%d" % i, plan["fc2"][0] + i * share, fc2[i])
            ready = blocks * share
        advance(1, ready)

    def out_rows(r):
        total = middle[r] + prev[r] + vec_row(9)
        normed1[r] = total.astype(BF16)

    over_rows(out_rows)
    state_rows = [pl.ds(pl.multiple_of(m * states, states), states) for m in (mine, 1 - mine)]
    out_swap = send(normed1.at[state_rows[1]], states_out.at[mine], 1, at.tm_partner(2))
    load("out_own", normed1.at[state_rows[0]], states_out.at[mine])
    branch = odd_grad.at[pl.ds(0, count)]

    def middle_back(r):
        grad = block_input[r]
        unit, scale = norm_parts(middle[r])
        vec[pl.ds(7, 1)] += jnp.sum(grad * unit, axis=0, keepdims=True)
        vec[pl.ds(8, 1)] += jnp.sum(grad, axis=0, keepdims=True)
        total = q_grad[r].astype(F32) + norm_back(grad, unit, scale, vec_row(7))
        middle[r] = total
        low = total.astype(BF16)
        branch[r] = low

    over_rows(middle_back)
    load("again", block_input_in, block_input)
    wide = branch[...].astype(F32)
    vec[pl.ds(6, 1)] = jnp.sum(wide, axis=0, keepdims=True)
    branch_t[...] = jnp.transpose(wide).astype(BF16)
    att_grad[...] = mat(branch[...], arena[pl.ds(0, width)]).astype(BF16)
    load("wqkv", wqkv_in, arena.at[pl.ds(0, wqkv_in.shape[0])])
    for i in range(3):
        load("w2_%d" % i, w2_in.at[:, pl.ds(i * width, width)], weights.at[i])
    out = [(share, rows_from(branch_t, 0, share), whole(attended))]
    give("out", plan["out"][0], out)
    for y in range(at.y_size):
        take("fc1_%d" % y, plan["fc1"][0], fc1[y], [y])
    advance(1, "out")
    take("out", plan["out"][0], out)
    load("se", slope_even_in, normed2)
    need("q", "inv", "k", "v")

    pairs = width // LANES
    lane = lax.broadcasted_iota(jnp.int32, (count, LANES), 1)

    def pair_body(p, carry):
        cols = pl.ds(aligned(p, LANES), LANES)
        q_t[...] = jnp.transpose(q[:, cols].astype(F32)).astype(BF16)
        grads = []
        for h in range(2):
            n = 2 * p + h
            if h == 0:
                fetch(n + 1, 1).start()
            else:

                @pl.when(p < pairs - 1)
                def _(n=n):
                    fetch(n + 1, 0).start()

            fetch(n, h).wait()
            scale = jnp.sum(jnp.where(lane == n, inv[...], 0.0), axis=-1, keepdims=True)
            keep = (lane < HEAD_DIM) if h == 0 else (lane >= HEAD_DIM)
            grad = jnp.where(keep, att_grad[:, cols].astype(F32) * scale, 0.0).astype(BF16)
            wide = grad.astype(F32)
            dot = jnp.sum(wide * attended[:, cols].astype(F32), axis=-1, keepdims=True)
            grad_t = jnp.transpose(wide).astype(BF16)[HEAD_DIM * h : HEAD_DIM * (h + 1)]
            head = pl.ds(pl.multiple_of(p * LANES + h * HEAD_DIM, HEAD_DIM), HEAD_DIM)
            v_t[head, :] = mat(grad_t, ebuf[h]).astype(BF16)
            diff = mat_t(grad, kv[pl.ds(every, every), cols]) - dot
            score_grad[...] = (ebuf[h].astype(F32) * diff).astype(BF16)
            grads.append(mat(score_grad[...], kv[pl.ds(0, every), cols]) * SCALE)
            part = q_t[pl.ds(HEAD_DIM * h, HEAD_DIM)]
            k_t[head, :] = (mat(part, score_grad[...]) * SCALE).astype(BF16)
        q_grad[:, cols] = jnp.where(lane < HEAD_DIM, grads[0], grads[1]).astype(BF16)

        @pl.when(p < most)
        def _():
            reducer.step(done[0] + p)

        return carry

    most = min(pairs, plan["qkv"][0] // rows - done[0])
    lax.fori_loop(0, pairs, pair_body, 0)
    done[0] += most

    for i in range(3):
        load("taps%d" % i, taps_in.at[:, pl.ds(i * width, width)], kv.at[pl.ds(i * count, count)])
    load("ss", slope_state_in, kv.at[pl.ds(3 * count, count)])
    group = [m for m in bits_of(at.parts) if m != 2]
    held_cols = every
    first = 0
    for number, mask in enumerate(reversed(group)):
        held_cols = held_cols // 2
        sent = []
        for i, ref in enumerate((k_t, v_t)):
            copy = pltpu.make_async_remote_copy(
                src_ref=ref.at[:, pl.ds(held_cols, held_cols)],
                dst_ref=kv_land.at[i, :, pl.ds(first, held_cols)],
                send_sem=kv_send.at[number, i],
                recv_sem=kv_recv.at[number, i],
                device_id=at.tm_partner(mask),
                device_id_type=MESH,
            )
            copy.start()
            sent.append(copy)
        if number == 0:
            g_t[pl.ds(0, width)] = jnp.transpose(q_grad[...].astype(F32)).astype(BF16)
            advance(1, "qkv")
        for i, (ref, copy) in enumerate(zip((k_t, v_t), sent)):
            copy.wait()
            low = pl.ds(0, held_cols)
            total = ref[:, low].astype(F32) + kv_land[i, :, pl.ds(first, held_cols)].astype(F32)
            ref[:, low] = total.astype(BF16)
        first += held_cols
    own = pl.ds(0, count)
    for i, (ref, target) in enumerate(((k_t, q), (v_t, att_grad))):
        part = ref[:, own]
        g_t[pl.ds((i + 1) * width, width)] = part
        target[...] = jnp.transpose(part.astype(F32)).astype(BF16)
    need("out_own")
    out_swap.wait()
    load("normed1", normed1_in, normed1)
    vec[pl.ds(4, 1)] = jnp.sum(q_grad[...].astype(F32), axis=0, keepdims=True)
    vec[pl.ds(5, 1)] = jnp.sum(att_grad[...].astype(F32), axis=0, keepdims=True)
    need("normed1")
    qkv = [(3 * share, rows_from(g_t, 0, 3 * share), whole(normed1))]
    give("qkv", plan["qkv"][0], qkv)
    advance(1, "qkv")
    need("wqkv", "again", "ss")
    tile = 128

    def norm_rows(i, carry):
        r = pl.ds(aligned(i, tile), tile)
        grad = mat(q_grad[r], arena[pl.ds(0, width)])
        grad = grad + mat(q[r], arena[pl.ds(width, width)])
        grad = grad + mat(att_grad[r], arena[pl.ds(2 * width, width)])
        unit, scale = norm_parts(block_input[r])
        vec[pl.ds(2, 1)] += jnp.sum(grad * unit, axis=0, keepdims=True)
        vec[pl.ds(3, 1)] += jnp.sum(grad, axis=0, keepdims=True)
        total = middle[r] + norm_back(grad, unit, scale, vecs[pl.ds(2, 1)])
        slope = kv[pl.ds(aligned(i, tile) + 3 * count, tile)].astype(F32)
        state_grad[r] = (total * slope).astype(BF16)
        return carry

    lax.fori_loop(0, count // tile, norm_rows, 0)
    vec[pl.ds(1, 1)] = jnp.sum(state_grad[...].astype(F32), axis=0, keepdims=True)
    take("qkv", plan["qkv"][0], qkv)
    advance(1, "conv2")
    cot_t[...] = jnp.transpose(state_grad[...].astype(F32)).astype(BF16)
    need("taps0", "taps1", "taps2")
    conv2 = [(share, rows_from(cot_t, 0, share), block_of(kv, i, count)) for i in range(3)]
    give("conv2", plan["conv2"][0], conv2)
    advance(1, "conv2")
    need("w2_0", "w2_1", "w2_2", "w1", "se", "so")
    prev[...] = mat(state_grad[...], weights[0])
    for s in range(2):
        r = pl.ds(s * states, states)
        even = mat(state_grad[r], weights[1])
        even_grad[r] = (even * normed2[r].astype(F32)).astype(BF16)
        odd = mat(state_grad[r], weights[2])
        place = lax.broadcasted_iota(jnp.int32, (states, width), 0)
        moved = pltpu.roll(prev[r], states - 1, 0)
        odd = odd + jnp.where(place < states - 1, moved, 0.0)
        r_odd = pl.ds(s * size, states)
        odd_grad[r_odd] = (odd * slope_odd[r_odd].astype(F32)).astype(BF16)
        r_edge = pl.ds(s * size + states, TILE)
        edge = jnp.broadcast_to(prev[pl.ds(s * states, 1)], (TILE, width))
        odd_grad[r_edge] = (edge * slope_odd[r_edge].astype(F32)).astype(BF16)
    take("conv2", plan["conv2"][0], conv2)
    advance(1, "conv1")
    need("x_even", "x_odd")
    vec[pl.ds(0, 1)] = jnp.sum(even_grad[...].astype(F32), axis=0, keepdims=True) + jnp.sum(
        odd_grad[...].astype(F32), axis=0, keepdims=True
    )
    vec_copy = pltpu.make_async_remote_copy(
        src_ref=vec,
        dst_ref=vec_got,
        send_sem=core_send.at[len(copies)],
        recv_sem=core_recv.at[len(copies)],
        device_id=core_partner,
        device_id_type=MESH,
    )
    vec_copy.start()
    conv1 = mat_l(even_grad[...], x_even[...]) + mat_l(odd_grad[...], x_odd[...])
    conv1_t[...] = conv1.astype(BF16)
    cols = conv1.shape[1]
    half = share // 2
    ring_slot = turn[0] % len(ring)
    if ring[ring_slot] is not None:
        ring[ring_slot].wait_send()
    conv1_copies = []
    first = plan["conv1"][0]

    def conv1_rows(part):
        low = conv1_t[pl.ds(pl.multiple_of(part * share, TILE), half)]
        high = conv1_t[pl.ds(pl.multiple_of(part * share + half, TILE), half)]
        return jnp.concatenate([low, high], axis=1)

    for y in range(at.y_size):
        stage[ring_slot, pl.ds(y * half, half)] = conv1_rows(2 * y + 1 - core)
        number = len(copies) + 1 + y
        copy = pltpu.make_async_remote_copy(
            src_ref=stage.at[ring_slot, pl.ds(y * half, half)],
            dst_ref=held.at[y, pl.ds(first, half)],
            send_sem=core_send.at[number],
            recv_sem=core_recv.at[number],
            device_id=core_partner,
            device_id_type=MESH,
        )
        copy.start()
        conv1_copies.append(copy)
    for y, copy in enumerate(conv1_copies):
        copy.wait_recv()
        place = pl.ds(first, half)
        total = conv1_rows(2 * y + core).astype(F32) + held[y, place].astype(F32)
        held[y, place] = total.astype(BF16)
    vec_copy.wait()
    total = (vec[...] + vec_got[...]).astype(BF16)
    for y in range(at.y_size):
        held[y, pl.ds(plan["vec"][0], TILE)] = total
    advance(1, "last")
    for s in range(2):
        even = mat(even_grad[pl.ds(s * states, states)], w1[...])
        even = jnp.concatenate([even, jnp.zeros((TILE, cols), F32)], axis=0)
        odd = mat(odd_grad[pl.ds(s * size, size)], w1[...])
        one, two, three = [slice(i * LANES, (i + 1) * LANES) for i in range(3)]
        mel_v[s, :, one] = even[:, two] + odd[:, one] + pltpu.roll(odd[:, three], 1, 0)
        mel_v[s, :, two] = pltpu.roll(even[:, one], size - 1, 0) + even[:, three] + odd[:, two]
    swap = send(mel_v.at[1 - mine], mel_all.at[mine], 0, at.tm_partner(2))
    mel_all[mine] = mel_v[mine]
    advance(1, "last")
    swap.wait()
    sides = [
        send(mel_all.at[:, pl.ds(states, 8)], mel_side.at[0], 2, right),
        send(mel_all.at[:, pl.ds(states + 8, 8)], mel_side.at[1], 3, left),
    ]
    advance(1, "last")
    for copy in sides:
        copy.wait()
    row = lax.broadcasted_iota(jnp.int32, (8, 2 * LANES), 0)
    has_before = jnp.minimum(at.tm, 1).astype(F32)
    has_after = jnp.minimum(at.parts - 1 - at.tm, 1).astype(F32)
    for clip in range(2):
        first, last = pl.ds(0, 8), pl.ds(states - 8, 8)
        mel_all[clip, first] += jnp.where(row == 0, mel_side[0, clip] * has_before, 0.0)
        mel_all[clip, last] += jnp.where(row == 7, mel_side[1, clip] * has_after, 0.0)
        mel_low[clip] = mel_all[clip, pl.ds(0, states)].astype(BF16)
    load("mel_low", mel_low, mel_out)
    for copy in ring:
        if copy is not None and copy is not ring[ring_slot]:
            copy.wait_send()
    for copy in conv1_copies:
        copy.wait_send()
    past = min(reducer.times, plan["qkv"][0] // rows + reducer.delays[-1])
    reducer.steps(done[0], max(done[0], past))
    done[0] = max(done[0], past)
    n = hidden // at.parts
    load("fc1_sum", result.at[pl.ds(plan["fc1"][0], n)], stage.at[0, pl.ds(0, n)])
    load("fc2_sum", result.at[pl.ds(plan["fc2"][0], blocks * share)], stage.at[1, pl.ds(0, blocks * share)])
    load("out_sum", result.at[pl.ds(plan["out"][0], share)], stage.at[2, pl.ds(0, share)])
    advance(1, "more")
    need("fc1_sum", "fc2_sum", "out_sum")
    cut = min(count, 512)
    lanes = pl.ds(0, n)
    pending = []
    buffers = [prev, tmp, middle]
    for i, low in enumerate(range(0, width, cut)):
        high = min(width, low + cut)
        part = stage[0, pl.ds(0, n), pl.ds(low, high - low)].astype(F32)
        buffers[i][pl.ds(0, high - low), lanes] = jnp.transpose(part)
        load("g%d" % i, buffers[i].at[pl.ds(0, high - low), lanes], fc1_out.at[pl.ds(low, high - low)])
        pending.append("g%d" % i)
        advance(1, "more")
    for i in range(blocks):
        if i > 0:
            need("f%d" % (i - 1))
        turned[...] = stage[1, pl.ds(i * share, share)].astype(F32)
        load("f%d" % i, turned, fc2_out.at[:, pl.ds(i * width, width)])
        if i % 2:
            advance(1, "more")
    need("f%d" % (blocks - 1))
    turned[...] = stage[2, pl.ds(0, share)].astype(F32)
    load("out_out", turned, out_out)
    advance(0, "end")
    need("out_out", "mel_low", *pending)
    reducer.close()


def back(operands, parts, clips):
    q, k, wfc1, w1, inv, slope_odd, x_even, x_odd = [operands[i] for i in (5, 6, 3, 12, 8, 17, 19, 20)]
    count, width = q.shape
    every = k.shape[0]
    hidden = wfc1.shape[0]
    states = count // 2
    size = states + TILE
    y_size = parts // 2
    plan, plane, rows, total = back_plan(parts, clips, width, hidden)
    big = max(hidden // parts, 3 * (width // parts))
    scratch = [
        ((y_size, total, width), BF16),
        ((3, big, width), BF16),
        ((3 * width, width), BF16),
        ((4, width, width), BF16),
        (w1.shape, BF16),
        ((max(hidden, 3 * width), count), BF16),
        ((width, count), BF16),
        ((width, count), BF16),
        ((count, width), BF16),
        ((count, width), BF16),
        ((count, width), BF16),
        ((count, width), BF16),
        ((max(2 * every, 4 * count), width), BF16),
        (inv.shape, F32),
        ((count, width), BF16),
        ((count, width), F32),
        ((count, width), F32),
        (slope_odd.shape, BF16),
        (x_even.shape, BF16),
        (x_odd.shape, BF16),
        ((TILE, width), F32),
        ((TILE, width), F32),
        ((TILE, width), F32),
        ((2, count, every), BF16),
        ((count, every), BF16),
        ((LANES, count), BF16),
        ((width, every), BF16),
        ((width, every), BF16),
        ((2, width, every - count), BF16),
        ((count, width), BF16),
        ((count, width), BF16),
        ((count, width), F32),
        ((count, width), F32),
        ((count, width), BF16),
        ((2 * size, width), BF16),
        ((width, x_even.shape[1]), BF16),
        ((2, size, 2 * LANES), F32),
        ((2, size, 2 * LANES), F32),
        ((2, 2, 8, 2 * LANES), F32),
        ((2, states, 2 * LANES), BF16),
        ((width // parts, width), F32),
    ]
    scratch = [pltpu.VMEM(s, d) for s, d in scratch]
    groups = len(bits_of(parts)) - 1
    scratch += [
        pltpu.SemaphoreType.DMA(((6 + hidden // width) * y_size + 1,)),
        pltpu.SemaphoreType.DMA(((6 + hidden // width) * y_size + 1,)),
        pltpu.SemaphoreType.DMA((groups + 2, 2)),
        pltpu.SemaphoreType.DMA((groups + 2, 2)),
        pltpu.SemaphoreType.DMA((48 + 4 * (hidden // width),)),
        pltpu.SemaphoreType.DMA((2,)),
        pltpu.SemaphoreType.DMA((total // rows,)),
        pltpu.SemaphoreType.DMA((2, 4)),
    ]
    scratch += Reducer.scratch(y_size, y_size, clips // y_size, total // rows, rows, width)
    return pl.pallas_call(
        functools.partial(back_kernel, plan, rows),
        out_shape=[
            jax.ShapeDtypeStruct((total, width), BF16),
            jax.ShapeDtypeStruct((2, states, 2 * LANES), BF16),
            jax.ShapeDtypeStruct((2, states, width), BF16),
            jax.ShapeDtypeStruct((width, hidden // parts), F32),
            jax.ShapeDtypeStruct((width // parts, hidden), F32),
            jax.ShapeDtypeStruct((width // parts, width), F32),
        ],
        in_specs=[ANY] * len(operands),
        out_specs=[ANY] * 6,
        scratch_shapes=scratch,
        compiler_params=pltpu.CompilerParams(
            collective_id=3, has_side_effects=True, vmem_limit_bytes=64 << 20
        ),
        name="back",
    )(*operands)


def per_device(
    mel_frames,
    lengths,
    conv1_weight,
    conv1_bias,
    conv2_weight,
    conv2_bias,
    ln1_gain,
    ln1_bias,
    qkv_weight,
    q_bias,
    v_bias,
    out_weight,
    out_bias,
    ln2_gain,
    ln2_bias,
    fc1_weight,
    fc1_bias,
    fc2_weight,
    fc2_bias,
    cotangent,
):
    parts = lax.axis_size("tm")
    place = lax.axis_index("tm")
    clips = lax.axis_size("clip")
    y_size = parts // 2
    core, y_place = place % 2, place // 2
    mine = y_place % 2
    frames, mels = mel_frames.shape[1:]
    states, width = cotangent.shape[1:]
    hidden = fc1_weight.shape[1] * parts
    rows = 2 * states
    share = conv1_bias.shape[0]
    size = states + TILE

    w1_own = jnp.pad(conv1_weight, ((0, 0), (0, LANES - mels), (0, 0))).reshape(3 * LANES, share).T
    w2_own = conv2_weight.reshape(3 * width, share).T
    vec_list = [
        conv1_bias, conv2_bias, ln1_gain, ln1_bias, q_bias, v_bias, out_bias, ln2_gain, ln2_bias,
        fc2_bias,
    ]
    vec_list = vec_list + [fc1_bias[i : i + share] for i in range(0, fc1_bias.shape[0], share)]
    vec_count = len(vec_list)
    vec_row = jnp.arange(TILE)[:, None]
    vec_own = jnp.zeros((TILE, share), BF16)
    for i, member in enumerate(vec_list):
        vec_own = jnp.where(vec_row == i, member[None], vec_own)
    vec_own = jnp.pad(vec_own, ((0, 0), (0, -share % LANES)))

    frame_ids = place * frames + jnp.arange(frames)
    frame_valid = (frame_ids[None, :] < lengths[:, None])[..., None]
    masked = jnp.where(frame_valid, mel_frames, jnp.zeros_like(mel_frames))
    masked = jnp.pad(masked.reshape(2, states, 2, mels), ((0, 0), (0, 0), (0, 0), (0, LANES - mels)))
    masked = masked.reshape(2, states, 2 * LANES)

    length = jnp.where(mine == 0, lengths[0], lengths[1])
    group = [m for m in bits_of(parts) if m != 2]
    segs = [4 * ((place ^ m) // 4) + 2 * jnp.arange(2) + (place ^ m) % 2 for m in combos(group)]
    segs = jnp.concatenate(segs)
    key_ids = (segs[:, None] * states + jnp.arange(states)[None, :]).reshape(1, -1)
    bias = jnp.where(2 * key_ids < length, 0.0, -1e30).astype(F32)
    owns = (
        w1_own, vec_own, w2_own, qkv_weight.T, out_weight.T, fc1_weight.T, fc2_weight.T,
    )
    table = jnp.asarray(positions(states * parts, width))
    (
        w1, w2, wqkv, vecs, state_taps, x_even, x_odd, slope_even, slope_odd, state_slope,
        block_input, normed1, queries, keys, values, attended, inverse, wout, wfc1, wfc2, exponents,
    ) = fore(masked, owns, table, bias, parts)
    summed, mel_back, out_states, fc1_sum, fc2_sum, out_sum = back(
        (
            cotangent, attended, wout, wfc1, wfc2, queries, keys, values, inverse, exponents, wqkv, w2, w1,
            normed1, block_input, state_slope, slope_even, slope_odd, state_taps, x_even, x_odd, vecs,
        ),
        parts,
        clips,
    )
    plan = back_plan(parts, clips, width, hidden)[0]

    def rows_of(name):
        first, count = plan[name]
        return summed[first : first + count].astype(F32)

    conv2_sum = jnp.swapaxes(rows_of("conv2").reshape(3, share, width), 1, 2)
    conv1_sum = rows_of("conv1")
    conv1_sum = jnp.concatenate([conv1_sum[:, : 3 * LANES], conv1_sum[:, 3 * LANES :]], axis=0)
    conv1_sum = conv1_sum.T.reshape(3, LANES, share)[:, :mels]
    all_vec = rows_of("vec")
    vec_sum = lax.dynamic_slice_in_dim(all_vec, place * share, share, axis=1)
    bfc1_sum = lax.dynamic_slice_in_dim(
        all_vec[10:vec_count].reshape(-1), place * (hidden // parts), hidden // parts
    )

    mel_back = mel_back.reshape(2, states, 2, LANES)[..., :mels].reshape(2, frames, mels)
    mel_grad = jnp.where(frame_valid, mel_back, jnp.zeros_like(mel_back))

    return (
        out_states,
        mel_grad,
        conv1_sum,
        vec_sum[0],
        conv2_sum,
        vec_sum[1],
        vec_sum[2],
        vec_sum[3],
        rows_of("qkv").T,
        vec_sum[4],
        vec_sum[5],
        out_sum.T,
        vec_sum[6],
        vec_sum[7],
        vec_sum[8],
        fc1_sum,
        bfc1_sum,
        fc2_sum.T,
        vec_sum[9],
    )


def solution(mesh):
    return jax.shard_map(
        per_device,
        mesh=mesh,
        in_specs=(
            P("clip", "tm", None),
            P("clip"),
            P(None, None, "tm"),
            P("tm"),
            P(None, None, "tm"),
            P("tm"),
            P("tm"),
            P("tm"),
            P(None, "tm"),
            P("tm"),
            P("tm"),
            P(None, "tm"),
            P("tm"),
            P("tm"),
            P("tm"),
            P(None, "tm"),
            P("tm"),
            P(None, "tm"),
            P("tm"),
            P("clip", "tm", None),
        ),
        out_specs=(
            P("clip", "tm", None),
            P("clip", "tm", None),
            P(None, None, "tm"),
            P("tm"),
            P(None, None, "tm"),
            P("tm"),
            P("tm"),
            P("tm"),
            P(None, "tm"),
            P("tm"),
            P("tm"),
            P(None, "tm"),
            P("tm"),
            P("tm"),
            P("tm"),
            P(None, "tm"),
            P("tm"),
            P(None, "tm"),
            P("tm"),
        ),
        check_vma=False,
    )
```
